256 devices in a mesh: ctx: 16 (over x, z_hi), head: 16 (over y, z_lo, core).
Axes of the slice: x: 4, y: 4, z: 8 (z_hi: 4, z_lo: 2; z = z_hi * 2 + z_lo), core: 2. Of those that a mesh axis runs over, the one named last changes fastest.
Arguments:
- queries: bfloat16 [24576, 2048], P(('ctx', 'head')), may hold values from -8 to 8
- keys: bfloat16 [24576, 2048], P(('ctx', 'head')), may hold values from -8 to 8
- values: bfloat16 [24576, 2048], P(('ctx', 'head')), may hold values from -6 to 6
- kv_tiles: int32 [192, 96], replicated, may hold values from 0 to 191, as said below
- tile_count: int32 [192], replicated, may hold values from 24 to 96
- assign: int32 [192], replicated, may hold values from 0 to 191, as said below
Outputs:
- attended: bfloat16 [24576, 2048], P(('ctx', 'head'))
- slot_lse: float32 [16, 24576], P('head', 'ctx')
The draws below stay inside these ranges and needn't reach their ends.
Inputs may be any that keep to these rules, and one draw needn't show every extreme that they name: `kv_tiles`: row t lists 96 distinct key tiles and its first entry is t; entries at positions tile_count[t] and later are not used. `assign`: A permutation of the 192 tiles: entry d * 12 + s names the tile that index d of ctx takes in its slot s. Tile t belongs to index t // 12 of ctx; at most 2 of one index's slots hold tiles of one owner.
All inputs are finite; a program needn't handle non-finite values.
Results may differ from the reference program's by a relative error of at most 0.0095.
Values may be sent and summed in bfloat16 or wider, within the bound.
No kernel may reach another device: no remote copies, remote signals or barrier semaphores. Data moves between devices by JAX's collectives and lax.ppermute only.
A program may use at most 128 MiB of HBM per device.

```python
import jax
import jax.numpy as jnp
from jax import lax

HD = 128
HEADS = 16
BLK = 128
TOKENS = 24576
QTILES = 192
QT_DEV = 12
LIST = 96
N_CTX = 16


def draw_queries(key, part):
    key = jax.random.fold_in(key, 3)
    drawn = jnp.clip(jax.random.normal(key, (TOKENS, HEADS * HD), jnp.float32), -6.0, 6.0)
    return drawn.astype(jnp.bfloat16)


def draw_keys(key, part):
    key = jax.random.fold_in(key, 7)
    drawn = jnp.clip(jax.random.normal(key, (TOKENS, HEADS * HD), jnp.float32), -6.0, 6.0)
    return drawn.astype(jnp.bfloat16)


def draw_kv_tiles(key, part):
    key = jax.random.fold_in(key, 11)
    tile_ids = jnp.arange(QTILES, dtype=jnp.int32)[:, None]
    column_ids = jnp.arange(QTILES, dtype=jnp.int32)[None, :]
    distance = jnp.abs(tile_ids - column_ids)
    noise = jax.random.randint(key, (QTILES, QTILES), 0, QTILES)
    priority = (distance + noise) * QTILES + column_ids
    priority = jnp.where(column_ids == tile_ids, -1, priority)
    ordering = jnp.argsort(priority, axis=1)[:, :LIST]
    return ordering.astype(jnp.int32)


def draw_tile_count(key, part):
    key = jax.random.fold_in(key, 13)
    sub_keys = jax.random.split(key, 2)
    lowest = max(1, LIST // 4)
    drawn_counts = jax.random.randint(sub_keys[0], (QTILES,), lowest, LIST + 1)
    chosen_ids = jax.random.permutation(sub_keys[1], QTILES)
    drawn_counts = drawn_counts.at[chosen_ids[0]].set(LIST)
    drawn_counts = drawn_counts.at[chosen_ids[1]].set(lowest)
    return drawn_counts.astype(jnp.int32)


def draw_assign(key, part):
    key = jax.random.fold_in(key, 17)
    sub_keys = jax.random.split(key, 2)
    doubled = jax.random.permutation(sub_keys[0], 2 * N_CTX) // 2
    half_way = N_CTX // 2
    fixed_offsets = jnp.array([half_way, half_way, 1, N_CTX - 1], dtype=jnp.int32)
    excluded = (doubled == half_way) | (doubled == 1) | (doubled == N_CTX - 1)
    ordering = jnp.argsort(excluded.astype(jnp.int32), stable=True)
    remainder = doubled[ordering].astype(jnp.int32)
    offsets = jnp.concatenate([fixed_offsets, remainder[:QT_DEV - 4]])
    scores = jax.random.randint(sub_keys[1], (N_CTX, QT_DEV), 0, 1 << 20) * QT_DEV + jnp.arange(QT_DEV, dtype=jnp.int32)[None, :]
    shuffles = jnp.argsort(scores, axis=1)
    device_ids = jnp.arange(N_CTX, dtype=jnp.int32)[:, None]
    slot_ids = jnp.broadcast_to(jnp.arange(QT_DEV, dtype=jnp.int32)[None, :], (N_CTX, QT_DEV))
    owner_ids = (device_ids - offsets[None, :]) % N_CTX
    local_ids = shuffles[owner_ids, slot_ids]
    return (owner_ids * QT_DEV + local_ids).reshape(-1).astype(jnp.int32)


def block_scale(key, dims, pieces, smallest, largest):
    gain = 1.0
    for axis_at, parts in pieces:
        draws = jax.random.uniform(jax.random.fold_in(jax.random.fold_in(key, 6), axis_at), (parts,), jnp.float32, smallest / len(pieces), largest / len(pieces))
        gain = gain * jnp.repeat(jnp.exp(draws), dims[axis_at] // parts).reshape((-1,) + (1,) * (len(dims) - 1 - axis_at))
    return gain


def scatter_about(rng, dims, deviation, most, pieces=(), kind=jnp.bfloat16):
    level = block_scale(rng, dims, pieces, -0.22, 0.18) if pieces else 1.0
    values = jax.random.normal(rng, dims, jnp.float32) * deviation * level
    return jnp.minimum(jnp.maximum(values, -most), most).astype(kind)


def setup_inputs(seed: int = 0) -> dict:
    seeds = jax.random.split(jax.random.key(seed), 7)
    return {
        "queries": draw_queries(jax.random.fold_in(seeds[6], 71), 0),
        "keys": draw_keys(jax.random.fold_in(seeds[6], 71), 0),
        "values": scatter_about(seeds[2], (TOKENS, HEADS * HD), 1.0, 6.0, ((0, 256),)),
        "kv_tiles": draw_kv_tiles(jax.random.fold_in(seeds[6], 71), 0),
        "tile_count": draw_tile_count(jax.random.fold_in(seeds[6], 71), 0),
        "assign": draw_assign(jax.random.fold_in(seeds[6], 71), 0),
    }


def reference(queries, keys, values, kv_tiles, tile_count, assign):
    scaling = HD ** -0.5
    query_tiles = queries.astype(jnp.float32).reshape(QTILES, BLK, HEADS, HD)
    key_tiles = keys.astype(jnp.float32).reshape(QTILES, BLK, HEADS, HD)
    value_tiles = values.astype(jnp.float32).reshape(QTILES, BLK, HEADS, HD)

    def one_tile(packed):
        query_tile, listed, used_total = packed
        key_pick = key_tiles[listed].reshape(LIST * BLK, HEADS, HD)
        value_pick = value_tiles[listed].reshape(LIST * BLK, HEADS, HD)
        scores = jnp.einsum("qhd,khd->hqk", query_tile, key_pick) * scaling
        usable = (jnp.arange(LIST * BLK, dtype=jnp.int32) // BLK < used_total)[None, None, :]
        rowmax = jnp.max(jnp.where(usable, scores, -jnp.inf), axis=-1)
        weights = jnp.where(usable, jnp.exp(scores - rowmax[..., None]), 0.0)
        totals = jnp.sum(weights, axis=-1)
        probabilities = lax.optimization_barrier(weights.astype(jnp.bfloat16)).astype(jnp.float32)
        blended = jnp.einsum("hqk,khd->qhd", probabilities, value_pick)
        blended = blended / jnp.transpose(totals)[:, :, None]
        return blended.astype(jnp.bfloat16), rowmax + jnp.log(totals)

    blended_all, log_all = lax.map(one_tile, (query_tiles, kv_tiles, tile_count))
    attended = blended_all.reshape(TOKENS, HEADS * HD)
    log_totals = jnp.transpose(log_all, (1, 0, 2)).reshape(HEADS, TOKENS)
    row_ids = (assign[:, None] * BLK + jnp.arange(BLK, dtype=jnp.int32)[None, :]).reshape(-1)
    slot_lse = log_totals[:, row_ids]
    return attended, slot_lse
```

```python
import jax
import jax.numpy as jnp
from jax import lax
from jax.experimental import pallas as pl
from jax.experimental.pallas import tpu as pltpu
from jax.sharding import PartitionSpec as P

HD = 128
BLK = 128
LIST = 96
RING = 4
OWN = 12
KEYS = RING * OWN
CHUNK = 4
ROWS = OWN + 1
NEG = -1e30
SCALE = HD**-0.5
LOG2E = 1.4426950408889634
VMEM = pl.BlockSpec(memory_space=pltpu.VMEM)
SMEM = pl.BlockSpec(memory_space=pltpu.SMEM)
ANY = pl.BlockSpec(memory_space=pl.ANY)
GROUP = ("zh", "zl", "core")


def shift(array, axis, by):
    return lax.ppermute(array, axis, [(i, (i + by) % RING) for i in range(RING)])


def prepare_kernel(got_ref, k_ref, qt_ref, vt_ref):
    for part in range(RING):
        q, k, v = (
            got_ref[4 * part : 4 * part + 4, which].reshape(3, BLK, HD) for which in range(3)
        )
        k_ref[3 * part : 3 * part + 3] = k
        for i in range(3):
            qt_ref[3 * part + i] = q[i].T
            vt_ref[3 * part + i] = v[i].T


def prepare(got):
    tiles = jax.ShapeDtypeStruct((OWN, BLK, HD), jnp.bfloat16)
    return pl.pallas_call(
        prepare_kernel,
        out_shape=(tiles, tiles, tiles),
        in_specs=[VMEM],
        out_specs=(VMEM, VMEM, VMEM),
        name="prepare",
    )(got)


def attend_kernel(lists, counts, qa, qb, *refs):
    k_in, v_in = refs[0:4], refs[4:8]
    oa, ob, lse_a, lse_b = refs[8:12]
    ks, vs, sems = refs[12:15]
    states = (refs[15:19], refs[19:23])
    queries = (qa, qb)
    copies = []
    for b in range(RING):
        span = pl.ds(b * OWN, OWN)
        copies.append(pltpu.make_async_copy(k_in[b], ks.at[span], sems.at[b]))
        copies.append(pltpu.make_async_copy(v_in[b], vs.at[span], sems.at[RING + b]))
    for copy in copies:
        copy.start()
    for s_ref, m_ref, l_ref, acc_ref in states:
        m_ref[...] = jnp.full(m_ref.shape, NEG, jnp.float32)
        l_ref[...] = jnp.zeros(l_ref.shape, jnp.float32)
        acc_ref[...] = jnp.zeros(acc_ref.shape, jnp.float32)

    def steps_of(stream, t):
        return jnp.maximum((counts[stream * ROWS + t] + CHUNK - 1) // CHUNK, 1)

    totals = [sum(steps_of(stream, t) for t in range(OWN)) for stream in range(2)]
    steps = jnp.maximum(totals[0], totals[1])

    def advance(stream, t, j):
        more = j + 1 < steps_of(stream, t)
        return jnp.where(more, t, jnp.minimum(t + 1, OWN)), jnp.where(more, j + 1, 0)

    def listed(stream, t, j):
        base = (stream * ROWS + t) * KEYS + j * CHUNK
        return [lists[base + u] for u in range(CHUNK)]

    def score(stream, t, j):
        s_ref = states[stream][0]
        qt = queries[stream][jnp.minimum(t, OWN - 1)]
        for u, tile in enumerate(listed(stream, t, j)):
            s_ref[u * BLK : (u + 1) * BLK] = jnp.dot(
                ks[tile], qt, preferred_element_type=jnp.float32
            )

    def blend(stream, t, j):
        s_ref, m_ref, l_ref, acc_ref = states[stream]
        left = counts[stream * ROWS + t] - j * CHUNK
        top = jnp.full((8, BLK), NEG, jnp.float32)
        for u in range(CHUNK):
            s = s_ref[u * BLK : (u + 1) * BLK]
            top = jnp.maximum(top, jnp.where(u < left, jnp.max(s.reshape(16, 8, BLK), axis=0), NEG))
        m_old = m_ref[t]
        m_new = jnp.maximum(m_old, jnp.max(top, axis=0, keepdims=True))
        alpha = jnp.exp2((m_old - m_new) * (SCALE * LOG2E))
        base = m_new * (SCALE * LOG2E)
        total = l_ref[t] * alpha
        weights = []
        for u in range(CHUNK):
            s = s_ref[u * BLK : (u + 1) * BLK] * (SCALE * LOG2E)
            w = jnp.exp2(s - jnp.where(u < left, base, -NEG))
            total = total + jnp.sum(w.reshape(16, 8, BLK), axis=0)
            weights.append(w.astype(jnp.bfloat16))
        m_ref[t] = m_new
        l_ref[t] = total
        vt = jnp.concatenate([vs[tile] for tile in listed(stream, t, j)], axis=1)
        acc_ref[t] = acc_ref[t] * alpha + jnp.dot(
            vt, jnp.concatenate(weights, axis=0), preferred_element_type=jnp.float32
        )

    for copy in copies:
        copy.wait()
    zero = jnp.int32(0)
    score(0, zero, zero)

    def step(_, carry):
        ta, ja, tb, jb = carry
        score(1, tb, jb)
        blend(0, ta, ja)
        ta, ja = advance(0, ta, ja)
        score(0, ta, ja)
        blend(1, tb, jb)
        tb, jb = advance(1, tb, jb)
        return ta, ja, tb, jb

    lax.fori_loop(0, steps, step, (zero, zero, zero, zero))

    for stream, (o_ref, lse_ref) in enumerate(((oa, lse_a), (ob, lse_b))):
        _, m_ref, l_ref, acc_ref = states[stream]

        def finish(t, _):
            total = jnp.sum(l_ref[t], axis=0, keepdims=True)
            some = total > 0.0
            safe = jnp.where(some, total, 1.0)
            o_ref[t] = (acc_ref[t] * jnp.where(some, 1.0 / safe, 0.0)).astype(jnp.bfloat16)
            lse_ref[t] = jnp.where(some, m_ref[t] * SCALE + jnp.log(safe), NEG)
            return 0

        lax.fori_loop(0, OWN, finish, 0)


def attend(lists, counts, qa, qb, keys, values):
    tiles = jax.ShapeDtypeStruct((OWN, HD, BLK), jnp.bfloat16)
    rows = jax.ShapeDtypeStruct((OWN, 1, BLK), jnp.float32)
    state = [
        pltpu.VMEM((CHUNK * BLK, BLK), jnp.float32),
        pltpu.VMEM((ROWS, 1, BLK), jnp.float32),
        pltpu.VMEM((ROWS, 8, BLK), jnp.float32),
        pltpu.VMEM((ROWS, HD, BLK), jnp.float32),
    ]
    return pl.pallas_call(
        attend_kernel,
        out_shape=(tiles, tiles, rows, rows),
        in_specs=[SMEM, SMEM, VMEM, VMEM] + [ANY] * 8,
        out_specs=(VMEM, VMEM, VMEM, VMEM),
        scratch_shapes=[
            pltpu.VMEM((KEYS, BLK, HD), jnp.bfloat16),
            pltpu.VMEM((KEYS, HD, BLK), jnp.bfloat16),
            pltpu.SemaphoreType.DMA((2 * RING,)),
        ]
        + state
        + state,
        compiler_params=pltpu.CompilerParams(vmem_limit_bytes=32 * 1024 * 1024),
        cost_estimate=pl.CostEstimate(
            flops=360 * 4 * BLK * BLK * HD, bytes_accessed=6 << 20, transcendentals=360 * BLK * BLK
        ),
        name="attend",
    )(lists, counts, qa, qb, *keys, *values)


def combine_kernel(*refs):
    outs, lses = refs[0:4], refs[4:8]
    o_ref, lse_ref = refs[8:10]
    for t in range(OWN):
        parts = [lse[t] for lse in lses]
        top = jnp.maximum(jnp.maximum(parts[0], parts[1]), jnp.maximum(parts[2], parts[3]))
        shares = [jnp.exp(part - top) for part in parts]
        total = (shares[0] + shares[1]) + (shares[2] + shares[3])
        lse_ref[t] = top + jnp.log(total)
        mixed = sum(o[t].astype(jnp.float32) * (w / total) for o, w in zip(outs, shares))
        o_ref[t] = mixed.T.astype(jnp.bfloat16)


def combine(outs, lses):
    return pl.pallas_call(
        combine_kernel,
        out_shape=(
            jax.ShapeDtypeStruct((OWN, BLK, HD), jnp.bfloat16),
            jax.ShapeDtypeStruct((OWN, 1, BLK), jnp.float32),
        ),
        in_specs=[VMEM] * 8,
        out_specs=(VMEM, VMEM),
        name="combine",
    )(*outs, *lses)


def key_lists(kv_tiles, tile_count, xi, yi):
    rows = lax.dynamic_slice_in_dim(kv_tiles, xi * KEYS, KEYS).reshape(RING, RING, 3, LIST)
    used = lax.dynamic_slice_in_dim(tile_count, xi * KEYS, KEYS).reshape(RING, RING, 3)
    rows = lax.dynamic_slice_in_dim(jnp.concatenate([rows, rows], axis=1), yi, RING, axis=1)
    used = lax.dynamic_slice_in_dim(jnp.concatenate([used, used], axis=1), yi, RING, axis=1)
    rows = jnp.transpose(rows, (1, 0, 2, 3)).reshape(KEYS, LIST)
    used = jnp.transpose(used, (1, 0, 2)).reshape(KEYS)
    here = (rows % OWN // 3 == yi) & (jnp.arange(LIST, dtype=jnp.int32)[None, :] < used[:, None])
    place = (rows // KEYS - xi) % RING * OWN + rows % KEYS // OWN * 3 + rows % 3
    before = jnp.arange(LIST)[:, None] < jnp.arange(LIST)[None, :]
    rank = jnp.dot(
        here.astype(jnp.bfloat16), before.astype(jnp.bfloat16), preferred_element_type=jnp.float32
    ).astype(jnp.int32)
    at = here[:, None, :] & (rank[:, None, :] == jnp.arange(KEYS, dtype=jnp.int32)[None, :, None])
    lists = jnp.sum(jnp.where(at, place[:, None, :], 0), axis=2)
    return lists, jnp.sum(here.astype(jnp.int32), axis=1)


def for_streams(lists, counts, first, second):
    picked, sizes = [], []
    for block in (first, second):
        picked += [lists[block * OWN : (block + 1) * OWN], jnp.zeros((1, KEYS), jnp.int32)]
        sizes += [counts[block * OWN : (block + 1) * OWN], jnp.zeros((1,), jnp.int32)]
    return jnp.concatenate(picked).reshape(-1), jnp.concatenate(sizes)


def on_device(queries, keys, values, kv_tiles, tile_count, assign):
    xi, yi = lax.axis_index("x"), lax.axis_index("y")
    sent = jnp.stack([a.reshape(96, 16, HD) for a in (queries, keys, values)])
    got = lax.all_to_all(
        jnp.transpose(sent, (2, 0, 1, 3)), GROUP, split_axis=0, concat_axis=0, tiled=True
    )
    k0, q0, v0 = prepare(got)
    k1, k3 = shift(k0, "x", -1), shift(k0, "x", 1)
    v1, v3 = shift(v0, "x", -1), shift(v0, "x", 1)
    q1, q3 = shift(q0, "y", -1), shift(q0, "y", 1)
    k2, v2 = shift(k3, "x", 1), shift(v1, "x", -1)
    half = OWN // 2
    q2 = jnp.concatenate([shift(q3[:half], "y", 1), shift(q1[half:], "y", -1)])
    lists, counts = key_lists(kv_tiles, tile_count, xi, yi)
    all_keys, all_values = (k0, k1, k2, k3), (v0, v1, v2, v3)
    o2, o1, e2, e1 = attend(*for_streams(lists, counts, 2, 1), q2, q1, all_keys, all_values)
    o3, o0, e3, e0 = attend(*for_streams(lists, counts, 3, 0), q3, q0, all_keys, all_values)
    outs = [o0, shift(o1, "y", 1), shift(o2, "y", 2), shift(o3, "y", -1)]
    lses = [e0, shift(e1, "y", 1), shift(e2, "y", 2), shift(e3, "y", -1)]
    blended, lse = combine(outs, lses)
    back = lax.all_to_all(
        blended.reshape(16, 96, HD), GROUP, split_axis=0, concat_axis=0, tiled=True
    )
    attended = jnp.transpose(back, (1, 0, 2)).reshape(96, 16 * HD)
    every = lax.all_gather(lse.reshape(OWN, BLK), ("x", "y"), axis=0, tiled=True)
    tiles = lax.dynamic_slice_in_dim(assign, (xi * RING + yi) * OWN, OWN)
    spots = tiles // KEYS * KEYS + tiles % OWN // 3 * OWN + tiles % KEYS // OWN * 3 + tiles % 3
    chosen = jnp.take(every, spots, axis=0).reshape(1, OWN * BLK)
    turned = [(b * RING + a, a * RING + b) for a in range(RING) for b in range(RING)]
    return attended, lax.ppermute(chosen, ("zh", "y"), turned)


def solution(mesh):
    split = jax.sharding.Mesh(
        mesh.devices.reshape(RING, RING, RING, 2, 2), ("x", "zh", "y", "zl", "core")
    )
    tokens = P(("x", "zh", "y", "zl", "core"), None)
    return jax.shard_map(
        on_device,
        mesh=split,
        in_specs=(tokens, tokens, tokens, P(), P(), P()),
        out_specs=(tokens, P(("y", "zl", "core"), ("x", "zh"))),
        check_vma=False,
    )
```

```python
import functools

import jax
import jax.numpy as jnp
from jax import lax
from jax.experimental import pallas as pl
from jax.experimental.pallas import tpu as pltpu
from jax.sharding import PartitionSpec as P

HD = 128
BLK = 128
LIST = 96
RING = 4
OWN = 12
KEYS = RING * OWN
CHUNK = 4
WIDTH = 4
PAD = 16
NEG = -1e30
SCALE = HD**-0.5
LOG2E = 1.4426950408889634
VMEM = pl.BlockSpec(memory_space=pltpu.VMEM)
SMEM = pl.BlockSpec(memory_space=pltpu.SMEM)
ANY = pl.BlockSpec(memory_space=pl.ANY)
GROUP = ("zh", "zl", "core")


def shift(array, axis, by):
    return lax.ppermute(array, axis, [(i, (i + by) % RING) for i in range(RING)])


def prepare_kernel(got_ref, kv_ref):
    for part in range(RING):
        k, v = (
            got_ref[4 * part : 4 * part + 4, which].reshape(3, BLK, HD) for which in range(2)
        )
        kv_ref[0, 3 * part : 3 * part + 3] = k
        for i in range(3):
            kv_ref[1, 3 * part + i] = v[i].T


def prepare(got):
    return pl.pallas_call(
        prepare_kernel,
        out_shape=jax.ShapeDtypeStruct((2, OWN, BLK, HD), jnp.bfloat16),
        in_specs=[VMEM],
        out_specs=VMEM,
        name="prepare",
    )(got)


def attend_kernel(blocks, lists, counts, *refs):
    tiles = blocks * OWN
    q_in, refs = refs[:blocks], refs[blocks:]
    kv0, kv1, kv3, k2, v2 = refs[:5]
    refs = refs[5:]
    o_out, refs = refs[:blocks], refs[blocks:]
    qs, ks, vs, sems, m_ref, l_ref, acc_ref = refs[:7]
    s_refs, top_refs = refs[7 : 7 + WIDTH], refs[7 + WIDTH :]
    moves = [(q, qs, b) for b, q in enumerate(q_in)]
    for b, (k, v) in enumerate(
        ((kv0.at[0], kv0.at[1]), (kv1.at[0], kv1.at[1]), (k2, v2), (kv3.at[0], kv3.at[1]))
    ):
        moves += [(k, ks, b), (v, vs, b)]
    copies = [
        pltpu.make_async_copy(source, held.at[pl.ds(b * OWN, OWN)], sems.at[i])
        for i, (source, held, b) in enumerate(moves)
    ]
    for copy in copies:
        copy.start()
    m_ref[...] = jnp.full(m_ref.shape, NEG, jnp.float32)
    l_ref[...] = jnp.zeros(l_ref.shape, jnp.float32)
    acc_ref[...] = jnp.zeros(acc_ref.shape, jnp.float32)

    def steps_of(t):
        return jnp.maximum((counts[t] + CHUNK - 1) // CHUNK, 1)

    items = lax.fori_loop(0, tiles, lambda t, n: n + steps_of(t), jnp.int32(0))

    def advance(t, j):
        more = j + 1 < steps_of(t)
        return jnp.where(more, t, jnp.minimum(t + 1, tiles)), jnp.where(more, j + 1, 0)

    def listed(t, j):
        base = t * KEYS + j * CHUNK
        return [lists[base + u] for u in range(CHUNK)]

    def score(lane, t, j):
        left = counts[t] - j * CHUNK
        s = lax.dot_general(
            jnp.concatenate([ks[tile] for tile in listed(t, j)], axis=0),
            qs[jnp.minimum(t, tiles - 1)],
            (((1,), (1,)), ((), ())),
            preferred_element_type=jnp.float32,
        )
        s_refs[lane][...] = s
        top = jnp.full((8, BLK), NEG, jnp.float32)
        for u in range(CHUNK):
            part = jnp.max(s[u * BLK : (u + 1) * BLK].reshape(16, 8, BLK), axis=0)
            top = jnp.maximum(top, jnp.where(u < left, part, NEG))
        top_refs[lane][...] = jnp.max(top, axis=0, keepdims=True)

    def blend(lane, t, j):
        left = counts[t] - j * CHUNK
        m_old = m_ref[t]
        m_new = jnp.maximum(m_old, top_refs[lane][...])
        m_ref[t] = m_new
        alpha = jnp.exp2((m_old - m_new) * (SCALE * LOG2E))
        base = m_new * (SCALE * LOG2E)
        total = jnp.zeros((8, BLK), jnp.float32)
        weights = []
        for u in range(CHUNK):
            s = s_refs[lane][u * BLK : (u + 1) * BLK] * (SCALE * LOG2E)
            w = jnp.exp2(s - jnp.where(u < left, base, -NEG))
            total = total + jnp.sum(w.reshape(16, 8, BLK), axis=0)
            weights.append(w.astype(jnp.bfloat16))
        vt = jnp.concatenate([vs[tile] for tile in listed(t, j)], axis=1)
        mixed = jnp.dot(vt, jnp.concatenate(weights, axis=0), preferred_element_type=jnp.float32)
        l_ref[t] = l_ref[t] * alpha + total
        acc_ref[t] = acc_ref[t] * alpha + mixed

    def following(t, j):
        group = []
        for _ in range(WIDTH):
            t, j = advance(t, j)
            group += [t, j]
        return tuple(group)

    for copy in copies:
        copy.wait()
    first = [jnp.int32(0), jnp.int32(0)]
    for _ in range(WIDTH - 1):
        first += advance(*first[-2:])
    for lane in range(WIDTH):
        score(lane, first[2 * lane], first[2 * lane + 1])

    def step(_, now):
        later = following(*now[-2:])
        for lane in range(WIDTH):
            blend(lane, now[2 * lane], now[2 * lane + 1])
            score(lane, later[2 * lane], later[2 * lane + 1])
        return later

    lax.fori_loop(0, (items + WIDTH - 1) // WIDTH, step, tuple(first))

    for b in range(blocks):

        def finish(i, _):
            for u in range(4):
                t = i * 4 + u
                total = jnp.sum(l_ref[b * OWN + t], axis=0, keepdims=True)
                some = total > 0.0
                safe = jnp.where(some, total, 1.0)
                share = jnp.where(some, 1.0 / safe, 0.0)
                lse = jnp.where(some, m_ref[b * OWN + t] * SCALE + jnp.log(safe), NEG)
                high = lse.astype(jnp.bfloat16)
                middle = (lse - high.astype(jnp.float32)).astype(jnp.bfloat16)
                low = (lse - high.astype(jnp.float32) - middle.astype(jnp.float32)).astype(
                    jnp.bfloat16
                )
                o_out[b][t, :HD] = (acc_ref[b * OWN + t] * share).astype(jnp.bfloat16)
                o_out[b][t, HD:] = jnp.concatenate(
                    [high, middle, low, jnp.zeros((PAD - 3, BLK), jnp.bfloat16)], axis=0
                )
            return 0

        lax.fori_loop(0, OWN // 4, finish, 0)


def attend(lists, counts, queries, kv):
    blocks = len(queries)
    tiles = jax.ShapeDtypeStruct((OWN, HD + PAD, BLK), jnp.bfloat16)
    slots = blocks * OWN + 1
    pairs = blocks * OWN * 15
    return pl.pallas_call(
        functools.partial(attend_kernel, blocks),
        out_shape=(tiles,) * blocks,
        in_specs=[SMEM, SMEM] + [ANY] * (blocks + 5),
        out_specs=(VMEM,) * blocks,
        scratch_shapes=[
            pltpu.VMEM((blocks * OWN, BLK, HD), jnp.bfloat16),
            pltpu.VMEM((KEYS, BLK, HD), jnp.bfloat16),
            pltpu.VMEM((KEYS, HD, BLK), jnp.bfloat16),
            pltpu.SemaphoreType.DMA((blocks + 2 * RING,)),
            pltpu.VMEM((slots, 1, BLK), jnp.float32),
            pltpu.VMEM((slots, 8, BLK), jnp.float32),
            pltpu.VMEM((slots, HD, BLK), jnp.float32),
        ]
        + [pltpu.VMEM((CHUNK * BLK, BLK), jnp.float32)] * WIDTH
        + [pltpu.VMEM((1, BLK), jnp.float32)] * WIDTH,
        compiler_params=pltpu.CompilerParams(vmem_limit_bytes=32 * 1024 * 1024),
        cost_estimate=pl.CostEstimate(
            flops=pairs * 4 * BLK * BLK * HD,
            bytes_accessed=5 << 20,
            transcendentals=pairs * BLK * BLK,
        ),
        name="attend",
    )(lists, counts, *queries, *kv)


def combine_kernel(*refs):
    outs, (o_ref, lse_ref) = refs[:RING], refs[RING:]
    for t in range(OWN):
        parts = []
        for o in outs:
            split = o[t, HD:].astype(jnp.float32)
            parts.append(split[0:1] + split[1:2] + split[2:3])
        top = jnp.maximum(jnp.maximum(parts[0], parts[1]), jnp.maximum(parts[2], parts[3]))
        shares = [jnp.exp(part - top) for part in parts]
        total = (shares[0] + shares[1]) + (shares[2] + shares[3])
        lse_ref[t : t + 1] = top + jnp.log(total)
        mixed = sum(o[t, :HD].astype(jnp.float32) * (w / total) for o, w in zip(outs, shares))
        o_ref[t] = mixed.T.astype(jnp.bfloat16)


def combine(outs):
    return pl.pallas_call(
        combine_kernel,
        out_shape=(
            jax.ShapeDtypeStruct((OWN, BLK, HD), jnp.bfloat16),
            jax.ShapeDtypeStruct((OWN, BLK), jnp.float32),
        ),
        in_specs=[VMEM] * RING,
        out_specs=(VMEM, VMEM),
        name="combine",
    )(*outs)


def key_lists(kv_tiles, tile_count, xi, yi):
    rows = lax.dynamic_slice_in_dim(kv_tiles, xi * KEYS, KEYS).reshape(RING, RING, 3, LIST)
    used = lax.dynamic_slice_in_dim(tile_count, xi * KEYS, KEYS).reshape(RING, RING, 3)
    rows = lax.dynamic_slice_in_dim(jnp.concatenate([rows, rows], axis=1), yi, RING, axis=1)
    used = lax.dynamic_slice_in_dim(jnp.concatenate([used, used], axis=1), yi, RING, axis=1)
    rows = jnp.transpose(rows, (1, 0, 2, 3)).reshape(KEYS, LIST)
    used = jnp.transpose(used, (1, 0, 2)).reshape(KEYS)
    here = (rows % OWN // 3 == yi) & (jnp.arange(LIST, dtype=jnp.int32)[None, :] < used[:, None])
    place = (rows // KEYS - xi) % RING * OWN + rows % KEYS // OWN * 3 + rows % 3
    before = jnp.arange(LIST)[:, None] < jnp.arange(LIST)[None, :]
    rank = jnp.dot(
        here.astype(jnp.bfloat16), before.astype(jnp.bfloat16), preferred_element_type=jnp.float32
    ).astype(jnp.int32)
    at = here[:, None, :] & (rank[:, None, :] == jnp.arange(KEYS, dtype=jnp.int32)[None, :, None])
    lists = jnp.sum(jnp.where(at, place[:, None, :], 0), axis=2)
    return lists, jnp.sum(here.astype(jnp.int32), axis=1)


def for_blocks(lists, counts, blocks):
    picked = [lists[b * OWN : (b + 1) * OWN] for b in blocks] + [jnp.zeros((1, KEYS), jnp.int32)]
    sizes = [counts[b * OWN : (b + 1) * OWN] for b in blocks] + [jnp.zeros((1,), jnp.int32)]
    return jnp.concatenate(picked).reshape(-1), jnp.concatenate(sizes)


def exchange(array):
    return lax.all_to_all(array, GROUP, split_axis=0, concat_axis=0, tiled=True)


def on_device(queries, keys, values, kv_tiles, tile_count, assign):
    xi, yi = lax.axis_index("x"), lax.axis_index("y")
    sent = jnp.stack([a.reshape(96, 16, HD) for a in (keys, values)])
    kv0 = prepare(exchange(jnp.transpose(sent, (2, 0, 1, 3))))
    kv1, kv3 = shift(kv0, "x", -1), shift(kv0, "x", 1)
    queries, kv0 = lax.optimization_barrier((queries, kv0))
    q0 = exchange(jnp.transpose(queries.reshape(96, 16, HD), (1, 0, 2))).reshape(OWN, BLK, HD)
    k2, v2 = shift(kv3[0], "x", 1), shift(kv1[1], "x", -1)
    q1, q3 = shift(q0, "y", -1), shift(q0, "y", 1)
    half = OWN // 2
    q2 = jnp.concatenate([shift(q3[:half], "y", 1), shift(q1[half:], "y", -1)])
    lists, counts = key_lists(kv_tiles, tile_count, xi, yi)
    kv = (kv0, kv1, kv3, k2, v2)
    (o2,) = attend(*for_blocks(lists, counts, (2,)), (q2,), kv)
    o1, o3 = attend(*for_blocks(lists, counts, (1, 3)), (q1, q3), kv)
    (o0,) = attend(*for_blocks(lists, counts, (0,)), (q0,), kv)
    blended, lse = combine((o0, shift(o1, "y", 1), shift(o2, "y", 2), shift(o3, "y", -1)))
    back = exchange(blended.reshape(16, 96, HD))
    attended = jnp.transpose(back, (1, 0, 2)).reshape(96, 16 * HD)
    every = lax.all_to_all(
        jnp.broadcast_to(lse[None], (RING * RING, OWN, BLK)),
        ("x", "y"),
        split_axis=0,
        concat_axis=0,
        tiled=True,
    ).reshape(-1, BLK)
    tiles = lax.dynamic_slice_in_dim(assign, (xi * RING + yi) * OWN, OWN)
    spots = tiles // KEYS * KEYS + tiles % OWN // 3 * OWN + tiles % KEYS // OWN * 3 + tiles % 3
    chosen = jnp.take(every, spots, axis=0).reshape(1, OWN * BLK)
    turned = [(b * RING + a, a * RING + b) for a in range(RING) for b in range(RING)]
    return attended, lax.ppermute(chosen, ("zh", "y"), turned)


def solution(mesh):
    split = jax.sharding.Mesh(
        mesh.devices.reshape(RING, RING, RING, 2, 2), ("x", "zh", "y", "zl", "core")
    )
    tokens = P(("x", "zh", "y", "zl", "core"), None)
    return jax.shard_map(
        on_device,
        mesh=split,
        in_specs=(tokens, tokens, tokens, P(), P(), P()),
        out_specs=(tokens, P(("y", "zl", "core"), ("x", "zh"))),
        check_vma=False,
    )
```

```python
import functools

import jax
import jax.numpy as jnp
from jax import lax
from jax.experimental import pallas as pl
from jax.experimental.pallas import tpu as pltpu
from jax.sharding import PartitionSpec as P

HD = 128
BLK = 128
LIST = 96
RING = 4
OWN = 12
KEYS = RING * OWN
CHUNK = 4
WIDTH = 4
PAD = 16
NEG = -1e30
SCALE = HD**-0.5
LOG2E = 1.4426950408889634
VMEM = pl.BlockSpec(memory_space=pltpu.VMEM)
SMEM = pl.BlockSpec(memory_space=pltpu.SMEM)
ANY = pl.BlockSpec(memory_space=pl.ANY)
GROUP = ("zh", "zl", "core")


def shift(array, axis, by):
    return lax.ppermute(array, axis, [(i, (i + by) % RING) for i in range(RING)])


def prepare_kernel(got_ref, kv_ref):
    for part in range(RING):
        k, v = (
            got_ref[4 * part : 4 * part + 4, which].reshape(3, BLK, HD) for which in range(2)
        )
        kv_ref[0, 3 * part : 3 * part + 3] = k
        for i in range(3):
            kv_ref[1, 3 * part + i] = v[i].T


def prepare(got):
    return pl.pallas_call(
        prepare_kernel,
        out_shape=jax.ShapeDtypeStruct((2, OWN, BLK, HD), jnp.bfloat16),
        in_specs=[VMEM],
        out_specs=VMEM,
        name="prepare",
    )(got)


def pack_kernel(kv0, kv1, kv3, ks, vs, sems):
    copies = []
    for b, kv in ((0, kv0), (1, kv1), (3, kv3)):
        for which, held in enumerate((ks, vs)):
            span = pl.ds(b * OWN, OWN)
            copies.append(
                pltpu.make_async_copy(kv.at[which], held.at[span], sems.at[len(copies)])
            )
    for copy in copies:
        copy.start()
    for copy in copies:
        copy.wait()


def pack(kv0, kv1, kv3):
    tiles = jax.ShapeDtypeStruct((KEYS, BLK, HD), jnp.bfloat16)
    return pl.pallas_call(
        pack_kernel,
        out_shape=(tiles, tiles),
        in_specs=[VMEM] * 3,
        out_specs=(VMEM, VMEM),
        scratch_shapes=[pltpu.SemaphoreType.DMA((6,))],
        name="pack",
    )(kv0, kv1, kv3)


def attend_kernel(blocks, last, lists, counts, *refs):
    tiles = len(blocks) * OWN
    queries, refs = refs[: len(blocks)], refs[len(blocks) :]
    if last:
        k2, v2, _, _, ks, vs = refs[:6]
        o_out, refs = refs[6 : 6 + len(blocks)], refs[6 + len(blocks) :]
    else:
        ks, vs = refs[:2]
        o_out, refs = refs[2 : 2 + len(blocks)], refs[2 + len(blocks) :]
    sems, rows, sizes, qs, m_ref, l_ref, acc_ref = refs[:7]
    s_refs, top_refs = refs[7 : 7 + WIDTH], refs[7 + WIDTH :]
    moves = [(q, qs, b * OWN) for b, q in enumerate(queries)]
    if last:
        moves += [(k2, ks, 2 * OWN), (v2, vs, 2 * OWN)]
    copies = [
        pltpu.make_async_copy(source, held.at[pl.ds(at, OWN)], sems.at[i])
        for i, (source, held, at) in enumerate(moves)
    ]
    for copy in copies:
        copy.start()
    m_ref[...] = jnp.full(m_ref.shape, NEG, jnp.float32)
    l_ref[...] = jnp.zeros(l_ref.shape, jnp.float32)
    acc_ref[...] = jnp.zeros(acc_ref.shape, jnp.float32)
    yi = lax.axis_index("y")
    items = jnp.int32(0)
    for b, block in enumerate(blocks):
        owner = lax.rem(yi + block, RING) * 3
        for t in range(OWN):
            row = owner + (t // 3 * OWN + t % 3)
            rows[b * OWN + t] = row
            sizes[b * OWN + t] = counts[row]
            items += jnp.maximum((counts[row] + CHUNK - 1) // CHUNK, 1)
    rows[tiles] = 0
    sizes[tiles] = 0

    def advance(t, j):
        more = (j + 1) * CHUNK < sizes[t]
        return jnp.where(more, t, jnp.minimum(t + 1, tiles)), jnp.where(more, j + 1, 0)

    def listed(t, j):
        row = rows[t]
        return [lists[row, j * CHUNK + u] for u in range(CHUNK)]

    def score(lane, t, j):
        left = sizes[t] - j * CHUNK
        tile = listed(t, j)
        q = qs[jnp.minimum(t, tiles - 1)]
        none = jnp.zeros_like(q)
        twice = jnp.concatenate(
            [jnp.concatenate([q, none], axis=1), jnp.concatenate([none, q], axis=1)], axis=0
        )
        pairs = [
            jnp.concatenate([ks[tile[u]], ks[tile[u + 1]]], axis=1) for u in range(0, CHUNK, 2)
        ]
        s = lax.dot_general(
            jnp.concatenate(pairs, axis=0),
            twice,
            (((1,), (1,)), ((), ())),
            preferred_element_type=jnp.float32,
        )
        s_refs[lane][...] = s
        top = jnp.full((8, BLK), NEG, jnp.float32)
        for u in range(CHUNK):
            part = s[u // 2 * BLK : (u // 2 + 1) * BLK, u % 2 * BLK : (u % 2 + 1) * BLK]
            part = jnp.max(part.reshape(16, 8, BLK), axis=0)
            top = jnp.maximum(top, jnp.where(u < left, part, NEG))
        top_refs[lane][...] = jnp.max(top, axis=0, keepdims=True)

    def blend(lane, t, j):
        left = sizes[t] - j * CHUNK
        m_old = m_ref[t]
        m_new = jnp.maximum(m_old, top_refs[lane][...])
        m_ref[t] = m_new
        alpha = jnp.exp2((m_old - m_new) * (SCALE * LOG2E))
        base = m_new * (SCALE * LOG2E)
        total = jnp.zeros((8, BLK), jnp.float32)
        weights = []
        for u in range(CHUNK):
            s = s_refs[lane][u // 2 * BLK : (u // 2 + 1) * BLK, u % 2 * BLK : (u % 2 + 1) * BLK]
            w = jnp.exp2(s * (SCALE * LOG2E) - jnp.where(u < left, base, -NEG))
            total = total + jnp.sum(w.reshape(16, 8, BLK), axis=0)
            weights.append(w.astype(jnp.bfloat16))
        vt = jnp.concatenate([vs[tile] for tile in listed(t, j)], axis=1)
        mixed = jnp.dot(vt, jnp.concatenate(weights, axis=0), preferred_element_type=jnp.float32)
        l_ref[t] = l_ref[t] * alpha + total
        acc_ref[t] = acc_ref[t] * alpha + mixed

    def following(t, j):
        group = []
        for _ in range(WIDTH):
            t, j = advance(t, j)
            group += [t, j]
        return tuple(group)

    for copy in copies:
        copy.wait()
    first = [jnp.int32(0), jnp.int32(0)]
    for _ in range(WIDTH - 1):
        first += advance(*first[-2:])
    for lane in range(WIDTH):
        score(lane, first[2 * lane], first[2 * lane + 1])

    def step(_, now):
        later = following(*now[-2:])
        for lane in range(WIDTH):
            blend(lane, now[2 * lane], now[2 * lane + 1])
            score(lane, later[2 * lane], later[2 * lane + 1])
        return later

    lax.fori_loop(0, (items + WIDTH - 1) // WIDTH, step, tuple(first))

    for b in range(len(blocks)):

        def finish(i, _):
            for u in range(4):
                t = i * 4 + u
                total = jnp.sum(l_ref[b * OWN + t], axis=0, keepdims=True)
                some = total > 0.0
                safe = jnp.where(some, total, 1.0)
                share = jnp.where(some, 1.0 / safe, 0.0)
                lse = jnp.where(some, m_ref[b * OWN + t] * SCALE + jnp.log(safe), NEG)
                high = lse.astype(jnp.bfloat16)
                middle = (lse - high.astype(jnp.float32)).astype(jnp.bfloat16)
                low = (lse - high.astype(jnp.float32) - middle.astype(jnp.float32)).astype(
                    jnp.bfloat16
                )
                o_out[b][t, :HD] = (acc_ref[b * OWN + t] * share).astype(jnp.bfloat16)
                o_out[b][t, HD:] = jnp.concatenate(
                    [high, middle, low, jnp.zeros((PAD - 3, BLK), jnp.bfloat16)], axis=0
                )
            return 0

        lax.fori_loop(0, OWN // 4, finish, 0)


def attend(blocks, lists, counts, queries, keys, values, last=()):
    tiles = jax.ShapeDtypeStruct((OWN, HD + PAD, BLK), jnp.bfloat16)
    held = jax.ShapeDtypeStruct((KEYS, BLK, HD), jnp.bfloat16)
    count = len(blocks)
    slots = count * OWN + 1
    pairs = count * OWN * 15
    return pl.pallas_call(
        functools.partial(attend_kernel, blocks, bool(last)),
        out_shape=((held, held) if last else ()) + (tiles,) * count,
        in_specs=[SMEM, SMEM] + [VMEM] * (count + len(last) + 2),
        out_specs=(VMEM,) * (count + len(last)),
        input_output_aliases={count + 4: 0, count + 5: 1} if last else {},
        scratch_shapes=[
            pltpu.SemaphoreType.DMA((count + len(last),)),
            pltpu.SMEM((slots,), jnp.int32),
            pltpu.SMEM((slots,), jnp.int32),
            pltpu.VMEM((count * OWN, BLK, HD), jnp.bfloat16),
            pltpu.VMEM((slots, 1, BLK), jnp.float32),
            pltpu.VMEM((slots, 8, BLK), jnp.float32),
            pltpu.VMEM((slots, HD, BLK), jnp.float32),
        ]
        + [pltpu.VMEM((CHUNK // 2 * BLK, 2 * BLK), jnp.float32)] * WIDTH
        + [pltpu.VMEM((1, BLK), jnp.float32)] * WIDTH,
        compiler_params=pltpu.CompilerParams(vmem_limit_bytes=32 * 1024 * 1024),
        cost_estimate=pl.CostEstimate(
            flops=pairs * 4 * BLK * BLK * HD,
            bytes_accessed=5 << 20,
            transcendentals=pairs * BLK * BLK,
        ),
        name="attend",
    )(lists, counts, *queries, *last, keys, values)


def combine_kernel(*refs):
    outs, (o_ref, lse_ref) = refs[:RING], refs[RING:]
    for t in range(OWN):
        parts = []
        for o in outs:
            split = o[t, HD:].astype(jnp.float32)
            parts.append(split[0:1] + split[1:2] + split[2:3])
        top = jnp.maximum(jnp.maximum(parts[0], parts[1]), jnp.maximum(parts[2], parts[3]))
        shares = [jnp.exp(part - top) for part in parts]
        total = (shares[0] + shares[1]) + (shares[2] + shares[3])
        lse_ref[t : t + 1] = top + jnp.log(total)
        mixed = sum(o[t, :HD].astype(jnp.float32) * (w / total) for o, w in zip(outs, shares))
        o_ref[t] = mixed.T.astype(jnp.bfloat16)


def combine(outs):
    return pl.pallas_call(
        combine_kernel,
        out_shape=(
            jax.ShapeDtypeStruct((OWN, BLK, HD), jnp.bfloat16),
            jax.ShapeDtypeStruct((OWN, BLK), jnp.float32),
        ),
        in_specs=[VMEM] * RING,
        out_specs=(VMEM, VMEM),
        name="combine",
    )(*outs)


def key_lists(kv_tiles, tile_count, xi, yi):
    rows = lax.dynamic_slice_in_dim(kv_tiles, xi * KEYS, KEYS)
    used = lax.dynamic_slice_in_dim(tile_count, xi * KEYS, KEYS)
    here = (rows % OWN // 3 == yi) & (jnp.arange(LIST, dtype=jnp.int32)[None, :] < used[:, None])
    place = (rows // KEYS - xi) % RING * OWN + rows % KEYS // OWN * 3 + rows % 3
    before = jnp.arange(LIST)[:, None] < jnp.arange(LIST)[None, :]
    rank = jnp.dot(
        here.astype(jnp.bfloat16), before.astype(jnp.bfloat16), preferred_element_type=jnp.float32
    ).astype(jnp.int32)
    at = here[:, None, :] & (rank[:, None, :] == jnp.arange(KEYS, dtype=jnp.int32)[None, :, None])
    lists = jnp.sum(jnp.where(at, place[:, None, :], 0), axis=2)
    return lists, jnp.sum(here.astype(jnp.int32), axis=1)


def exchange(array):
    return lax.all_to_all(array, GROUP, split_axis=0, concat_axis=0, tiled=True)


def on_device(queries, keys, values, kv_tiles, tile_count, assign):
    xi, yi = lax.axis_index("x"), lax.axis_index("y")
    lists, counts = key_lists(kv_tiles, tile_count, xi, yi)
    sent = jnp.stack([a.reshape(96, 16, HD) for a in (keys, values)])
    got = exchange(jnp.transpose(sent, (2, 0, 1, 3)))
    got, lists, counts = lax.optimization_barrier((got, lists, counts))
    kv0 = prepare(got)
    kv1, kv3 = shift(kv0, "x", -1), shift(kv0, "x", 1)
    queries, kv0 = lax.optimization_barrier((queries, kv0))
    q0 = exchange(jnp.transpose(queries.reshape(96, 16, HD), (1, 0, 2))).reshape(OWN, BLK, HD)
    k2, v2 = shift(kv3[0], "x", 1), shift(kv1[1], "x", -1)
    q1, q3 = shift(q0, "y", -1), shift(q0, "y", 1)
    half = OWN // 2
    q2 = jnp.concatenate([shift(q3[:half], "y", 1), shift(q1[half:], "y", -1)])
    some_keys, some_values = pack(kv0, kv1, kv3)
    all_keys, all_values, o1, o3 = attend(
        (1, 3), lists, counts, (q1, q3), some_keys, some_values, (k2, v2)
    )
    (o2,) = attend((2,), lists, counts, (q2,), all_keys, all_values)
    (o0,) = attend((0,), lists, counts, (q0,), all_keys, all_values)
    blended, lse = combine((o0, shift(o1, "y", 1), shift(o2, "y", 2), shift(o3, "y", -1)))
    back = exchange(blended.reshape(16, 96, HD))
    attended = jnp.transpose(back, (1, 0, 2)).reshape(96, 16 * HD)
    every = lax.all_gather(lax.all_gather(lse, "y"), "x").reshape(-1, BLK)
    tiles = lax.dynamic_slice_in_dim(assign, (xi * RING + yi) * OWN, OWN)
    spots = tiles // KEYS * KEYS + tiles % OWN // 3 * OWN + tiles % KEYS // OWN * 3 + tiles % 3
    chosen = jnp.take(every, spots, axis=0).reshape(1, OWN * BLK)
    turned = [(b * RING + a, a * RING + b) for a in range(RING) for b in range(RING)]
    return attended, lax.ppermute(chosen, ("zh", "y"), turned)


def solution(mesh):
    split = jax.sharding.Mesh(
        mesh.devices.reshape(RING, RING, RING, 2, 2), ("x", "zh", "y", "zl", "core")
    )
    tokens = P(("x", "zh", "y", "zl", "core"), None)
    return jax.shard_map(
        on_device,
        mesh=split,
        in_specs=(tokens, tokens, tokens, P(), P(), P()),
        out_specs=(tokens, P(("y", "zl", "core"), ("x", "zh"))),
        check_vma=False,
    )
```

```python
import functools

import jax
import jax.numpy as jnp
from jax import lax
from jax.experimental import pallas as pl
from jax.experimental.pallas import tpu as pltpu
from jax.sharding import PartitionSpec as P

HD = 128
BLK = 128
LIST = 96
RING = 4
OWN = 12
KEYS = RING * OWN
CHUNK = 4
WIDTH = 4
PAD = 16
NEG = -1e30
SCALE = HD**-0.5
LOG2E = 1.4426950408889634
VMEM = pl.BlockSpec(memory_space=pltpu.VMEM)
SMEM = pl.BlockSpec(memory_space=pltpu.SMEM)
SPACE = pltpu.CompilerParams(vmem_limit_bytes=16 * 1024 * 1024)
GROUP = ("zh", "zl", "core")


def shift(array, axis, by):
    return lax.ppermute(array, axis, [(i, (i + by) % RING) for i in range(RING)])


def around(array, axis):
    return jnp.stack([array] + [shift(array, axis, -by) for by in range(1, RING)])


def prepare_kernel(got_ref, kv_ref):
    for part in range(RING):
        k, v = (
            got_ref[4 * part : 4 * part + 4, which].reshape(3, BLK, HD) for which in range(2)
        )
        kv_ref[0, 3 * part : 3 * part + 3] = k
        for i in range(3):
            kv_ref[1, 3 * part + i] = v[i].T


def prepare(got):
    return pl.pallas_call(
        prepare_kernel,
        out_shape=jax.ShapeDtypeStruct((2, OWN, BLK, HD), jnp.bfloat16),
        in_specs=[VMEM],
        out_specs=VMEM,
        compiler_params=SPACE,
        name="prepare",
    )(got)


def attend_kernel(blocks, first_call, lists, counts, *refs):
    tiles = len(blocks) * OWN
    queries, refs = refs[: len(blocks)], refs[len(blocks) :]
    if first_call:
        kv0, kv1, kv3, k2, v2, ks, vs = refs[:7]
        refs = refs[7:]
    else:
        ks, vs = refs[:2]
        refs = refs[2:]
    o_out, refs = refs[: len(blocks)], refs[len(blocks) :]
    rows, sizes, qs, m_ref, l_ref, acc_ref = refs[:6]
    s_refs, top_refs = refs[6 : 6 + WIDTH], refs[6 + WIDTH :]
    for b, q in enumerate(queries):
        qs[b * OWN : (b + 1) * OWN] = q[...]
    if first_call:
        for b, k, v in (
            (0, kv0.at[0], kv0.at[1]),
            (1, kv1.at[0], kv1.at[1]),
            (2, k2, v2),
            (3, kv3.at[0], kv3.at[1]),
        ):
            ks[b * OWN : (b + 1) * OWN] = k[...]
            vs[b * OWN : (b + 1) * OWN] = v[...]
    m_ref[...] = jnp.full(m_ref.shape, NEG, jnp.float32)
    l_ref[...] = jnp.zeros(l_ref.shape, jnp.float32)
    acc_ref[...] = jnp.zeros(acc_ref.shape, jnp.float32)
    yi = lax.axis_index("y")
    items = jnp.int32(0)
    for b, block in enumerate(blocks):
        owner = lax.rem(yi + block, RING) * 3
        for t in range(OWN):
            row = owner + (t // 3 * OWN + t % 3)
            rows[b * OWN + t] = row
            sizes[b * OWN + t] = counts[row]
            items += jnp.maximum((counts[row] + CHUNK - 1) // CHUNK, 1)
    rows[tiles] = 0
    sizes[tiles] = 0

    def advance(t, j):
        more = (j + 1) * CHUNK < sizes[t]
        return jnp.where(more, t, jnp.minimum(t + 1, tiles)), jnp.where(more, j + 1, 0)

    def listed(t, j):
        row = rows[t]
        return [lists[row, j * CHUNK + u] for u in range(CHUNK)]

    def score(lane, t, j):
        left = sizes[t] - j * CHUNK
        tile = listed(t, j)
        s = lax.dot_general(
            jnp.concatenate([ks[u] for u in tile], axis=0),
            qs[jnp.minimum(t, tiles - 1)],
            (((1,), (1,)), ((), ())),
            preferred_element_type=jnp.float32,
        )
        s_refs[lane][...] = s
        top = jnp.full((8, BLK), NEG, jnp.float32)
        for u in range(CHUNK):
            part = jnp.max(s[u * BLK : (u + 1) * BLK].reshape(16, 8, BLK), axis=0)
            top = jnp.maximum(top, jnp.where(u < left, part, NEG))
        top_refs[lane][...] = jnp.max(top, axis=0, keepdims=True)

    def blend(lane, t, j):
        left = sizes[t] - j * CHUNK
        m_old = m_ref[t]
        m_new = jnp.maximum(m_old, top_refs[lane][...])
        m_ref[t] = m_new
        alpha = jnp.exp2((m_old - m_new) * (SCALE * LOG2E))
        base = m_new * (SCALE * LOG2E)
        total = jnp.zeros((8, BLK), jnp.float32)
        weights = []
        for u in range(CHUNK):
            s = s_refs[lane][u * BLK : (u + 1) * BLK] * (SCALE * LOG2E)
            w = jnp.exp2(s - jnp.where(u < left, base, -NEG))
            total = total + jnp.sum(w.reshape(16, 8, BLK), axis=0)
            weights.append(w.astype(jnp.bfloat16))
        vt = jnp.concatenate([vs[tile] for tile in listed(t, j)], axis=1)
        mixed = jnp.dot(vt, jnp.concatenate(weights, axis=0), preferred_element_type=jnp.float32)
        l_ref[t] = l_ref[t] * alpha + total
        acc_ref[t] = acc_ref[t] * alpha + mixed

    def following(t, j):
        group = []
        for _ in range(WIDTH):
            t, j = advance(t, j)
            group += [t, j]
        return tuple(group)

    first = [jnp.int32(0), jnp.int32(0)]
    for _ in range(WIDTH - 1):
        first += advance(*first[-2:])
    for lane in range(WIDTH):
        score(lane, first[2 * lane], first[2 * lane + 1])

    def step(_, now):
        later = following(*now[-2:])
        for lane in range(WIDTH):
            blend(lane, now[2 * lane], now[2 * lane + 1])
            score(lane, later[2 * lane], later[2 * lane + 1])
        return later

    lax.fori_loop(0, (items + WIDTH - 1) // WIDTH, step, tuple(first))

    for b in range(len(blocks)):

        def finish(i, _):
            for u in range(4):
                t = i * 4 + u
                total = jnp.sum(l_ref[b * OWN + t], axis=0, keepdims=True)
                some = total > 0.0
                safe = jnp.where(some, total, 1.0)
                share = jnp.where(some, 1.0 / safe, 0.0)
                lse = jnp.where(some, m_ref[b * OWN + t] * SCALE + jnp.log(safe), NEG)
                high = lse.astype(jnp.bfloat16)
                middle = (lse - high.astype(jnp.float32)).astype(jnp.bfloat16)
                low = (lse - high.astype(jnp.float32) - middle.astype(jnp.float32)).astype(
                    jnp.bfloat16
                )
                o_out[b][t, :HD] = (acc_ref[b * OWN + t] * share).astype(jnp.bfloat16)
                o_out[b][t, HD:] = jnp.concatenate(
                    [high, middle, low, jnp.zeros((PAD - 3, BLK), jnp.bfloat16)], axis=0
                )
            return 0

        lax.fori_loop(0, OWN // 4, finish, 0)


def attend(blocks, lists, counts, queries, keys_values, first_call=False):
    tiles = jax.ShapeDtypeStruct((OWN, HD + PAD, BLK), jnp.bfloat16)
    held = (jax.ShapeDtypeStruct((KEYS, BLK, HD), jnp.bfloat16),) * 2 if first_call else ()
    count = len(blocks)
    slots = count * OWN + 1
    pairs = count * OWN * 15
    return pl.pallas_call(
        functools.partial(attend_kernel, blocks, first_call),
        out_shape=held + (tiles,) * count,
        in_specs=[SMEM, SMEM] + [VMEM] * (count + len(keys_values)),
        out_specs=(VMEM,) * (count + len(held)),
        scratch_shapes=[
            pltpu.SMEM((slots,), jnp.int32),
            pltpu.SMEM((slots,), jnp.int32),
            pltpu.VMEM((count * OWN, BLK, HD), jnp.bfloat16),
            pltpu.VMEM((slots, 1, BLK), jnp.float32),
            pltpu.VMEM((slots, 8, BLK), jnp.float32),
            pltpu.VMEM((slots, HD, BLK), jnp.float32),
        ]
        + [pltpu.VMEM((CHUNK * BLK, BLK), jnp.float32)] * WIDTH
        + [pltpu.VMEM((1, BLK), jnp.float32)] * WIDTH,
        compiler_params=SPACE,
        cost_estimate=pl.CostEstimate(
            flops=pairs * 4 * BLK * BLK * HD,
            bytes_accessed=5 << 20,
            transcendentals=pairs * BLK * BLK,
        ),
        name="attend",
    )(lists, counts, *queries, *keys_values)


def combine_kernel(*refs):
    outs, (o_ref, lse_ref) = refs[:RING], refs[RING:]
    for t in range(OWN):
        parts = []
        for o in outs:
            split = o[t, HD:].astype(jnp.float32)
            parts.append(split[0:1] + split[1:2] + split[2:3])
        top = jnp.maximum(jnp.maximum(parts[0], parts[1]), jnp.maximum(parts[2], parts[3]))
        shares = [jnp.exp(part - top) for part in parts]
        total = (shares[0] + shares[1]) + (shares[2] + shares[3])
        lse_ref[t : t + 1] = top + jnp.log(total)
        mixed = sum(o[t, :HD].astype(jnp.float32) * (w / total) for o, w in zip(outs, shares))
        o_ref[t] = mixed.T.astype(jnp.bfloat16)


def combine(outs):
    return pl.pallas_call(
        combine_kernel,
        out_shape=(
            jax.ShapeDtypeStruct((OWN, BLK, HD), jnp.bfloat16),
            jax.ShapeDtypeStruct((OWN, BLK), jnp.float32),
        ),
        in_specs=[VMEM] * RING,
        out_specs=(VMEM, VMEM),
        compiler_params=SPACE,
        name="combine",
    )(*outs)


def key_lists(kv_tiles, tile_count, xi, yi):
    rows = lax.dynamic_slice_in_dim(kv_tiles, xi * KEYS, KEYS)
    used = lax.dynamic_slice_in_dim(tile_count, xi * KEYS, KEYS)
    here = (rows % OWN // 3 == yi) & (jnp.arange(LIST, dtype=jnp.int32)[None, :] < used[:, None])
    place = (rows // KEYS - xi) % RING * OWN + rows % KEYS // OWN * 3 + rows % 3
    before = jnp.arange(LIST)[:, None] < jnp.arange(LIST)[None, :]
    rank = jnp.dot(
        here.astype(jnp.bfloat16), before.astype(jnp.bfloat16), preferred_element_type=jnp.float32
    ).astype(jnp.int32)
    at = here[:, None, :] & (rank[:, None, :] == jnp.arange(KEYS, dtype=jnp.int32)[None, :, None])
    lists = jnp.sum(jnp.where(at, place[:, None, :], 0), axis=2)
    return lists, jnp.sum(here.astype(jnp.int32), axis=1)


def exchange(array):
    return lax.all_to_all(array, GROUP, split_axis=0, concat_axis=0, tiled=True)


def on_device(queries, keys, values, kv_tiles, tile_count, assign):
    xi, yi = lax.axis_index("x"), lax.axis_index("y")
    lists, counts = key_lists(kv_tiles, tile_count, xi, yi)
    sent = jnp.stack([a.reshape(96, 16, HD) for a in (keys, values)])
    got = exchange(jnp.transpose(sent, (2, 0, 1, 3)))
    got, lists, counts = lax.optimization_barrier((got, lists, counts))
    kv0 = prepare(got)
    kv1, kv3 = shift(kv0, "x", -1), shift(kv0, "x", 1)
    queries, kv0 = lax.optimization_barrier((queries, kv0))
    q0 = exchange(jnp.transpose(queries.reshape(96, 16, HD), (1, 0, 2))).reshape(OWN, BLK, HD)
    k2, v2 = shift(kv3[0], "x", 1), shift(kv1[1], "x", -1)
    q1, q3 = shift(q0, "y", -1), shift(q0, "y", 1)
    half = OWN // 2
    q2 = jnp.concatenate([shift(q3[:half], "y", 1), shift(q1[half:], "y", -1)])
    all_keys, all_values, o1, o3 = attend(
        (1, 3), lists, counts, (q1, q3), (kv0, kv1, kv3, k2, v2), first_call=True
    )
    (o2,) = attend((2,), lists, counts, (q2,), (all_keys, all_values))
    (o0,) = attend((0,), lists, counts, (q0,), (all_keys, all_values))
    blended, lse = combine((o0, shift(o1, "y", 1), shift(o2, "y", 2), shift(o3, "y", -1)))
    back = exchange(blended.reshape(16, 96, HD))
    attended = jnp.transpose(back, (1, 0, 2)).reshape(96, 16 * HD)
    every = around(around(lse, "y"), "x").reshape(-1, BLK)
    tiles = lax.dynamic_slice_in_dim(assign, (xi * RING + yi) * OWN, OWN)
    spots = (tiles // KEYS - xi) % RING * KEYS + (tiles % OWN // 3 - yi) % RING * OWN
    spots = spots + tiles % KEYS // OWN * 3 + tiles % 3
    chosen = jnp.take(every, spots, axis=0).reshape(1, OWN * BLK)
    turned = [(b * RING + a, a * RING + b) for a in range(RING) for b in range(RING)]
    return attended, lax.ppermute(chosen, ("zh", "y"), turned)


def solution(mesh):
    split = jax.sharding.Mesh(
        mesh.devices.reshape(RING, RING, RING, 2, 2), ("x", "zh", "y", "zl", "core")
    )
    tokens = P(("x", "zh", "y", "zl", "core"), None)
    return jax.shard_map(
        on_device,
        mesh=split,
        in_specs=(tokens, tokens, tokens, P(), P(), P()),
        out_specs=(tokens, P(("y", "zl", "core"), ("x", "zh"))),
        check_vma=False,
    )
```

```python
import functools

import jax
import jax.numpy as jnp
from jax import lax
from jax.experimental import pallas as pl
from jax.experimental.pallas import tpu as pltpu
from jax.sharding import PartitionSpec as P

HD = 128
BLK = 128
LIST = 96
RING = 4
OWN = 12
KEYS = RING * OWN
CHUNK = 4
WIDTH = 4
PAD = 16
NEG = -1e30
SCALE = HD**-0.5
LOG2E = 1.4426950408889634
VMEM = pl.BlockSpec(memory_space=pltpu.VMEM)
SMEM = pl.BlockSpec(memory_space=pltpu.SMEM)
SPACE = pltpu.CompilerParams(vmem_limit_bytes=16 * 1024 * 1024)
GROUP = ("zh", "zl", "core")


def shift(array, axis, by):
    return lax.ppermute(array, axis, [(i, (i + by) % RING) for i in range(RING)])


def around(array, axis):
    return [array] + [shift(array, axis, -by) for by in range(1, RING)]


def spread_kernel(keys, values, out, sems):
    copies = [
        pltpu.make_async_copy(
            array.at[:, pl.ds(head * HD, HD)], out.at[head, which], sems.at[which, head]
        )
        for which, array in enumerate((keys, values))
        for head in range(16)
    ]
    for copy in copies:
        copy.start()
    for copy in copies:
        copy.wait()


def spread(keys, values):
    return pl.pallas_call(
        spread_kernel,
        out_shape=jax.ShapeDtypeStruct((16, 2, 96, HD), jnp.bfloat16),
        in_specs=[pl.BlockSpec(memory_space=pl.ANY)] * 2,
        out_specs=VMEM,
        scratch_shapes=[pltpu.SemaphoreType.DMA((2, 16))],
        compiler_params=SPACE,
        name="spread",
    )(keys, values)


def prepare_kernel(got_ref, kv_ref):
    for part in range(RING):
        k, v = (
            got_ref[4 * part : 4 * part + 4, which].reshape(3, BLK, HD) for which in range(2)
        )
        kv_ref[0, 3 * part : 3 * part + 3] = k
        for i in range(3):
            kv_ref[1, 3 * part + i] = v[i].T


def prepare(got):
    return pl.pallas_call(
        prepare_kernel,
        out_shape=jax.ShapeDtypeStruct((2, OWN, BLK, HD), jnp.bfloat16),
        in_specs=[VMEM],
        out_specs=VMEM,
        compiler_params=SPACE,
        name="prepare",
    )(got)


def attend_kernel(blocks, first_call, lists, counts, *refs):
    tiles = len(blocks) * OWN
    queries, refs = refs[: len(blocks)], refs[len(blocks) :]
    if first_call:
        kv0, kv1, kv3, k2, v2, ks, vs = refs[:7]
        refs = refs[7:]
    else:
        ks, vs = refs[:2]
        refs = refs[2:]
    o_out, refs = refs[: len(blocks)], refs[len(blocks) :]
    e_out, refs = refs[: len(blocks)], refs[len(blocks) :]
    rows, sizes, qs, m_ref, l_ref, acc_ref = refs[:6]
    s_refs, top_refs = refs[6 : 6 + WIDTH], refs[6 + WIDTH :]
    for b, q in enumerate(queries):
        qs[b * OWN : (b + 1) * OWN] = q[...]
    if first_call:
        for b, k, v in (
            (0, kv0.at[0], kv0.at[1]),
            (1, kv1.at[0], kv1.at[1]),
            (2, k2, v2),
            (3, kv3.at[0], kv3.at[1]),
        ):
            ks[b * OWN : (b + 1) * OWN] = k[...]
            vs[b * OWN : (b + 1) * OWN] = v[...]
    m_ref[...] = jnp.full(m_ref.shape, NEG, jnp.float32)
    l_ref[...] = jnp.zeros(l_ref.shape, jnp.float32)
    acc_ref[...] = jnp.zeros(acc_ref.shape, jnp.float32)
    yi = lax.axis_index("y")
    items = jnp.int32(0)
    for b, block in enumerate(blocks):
        owner = lax.rem(yi + block, RING) * 3
        for t in range(OWN):
            row = owner + (t // 3 * OWN + t % 3)
            rows[b * OWN + t] = row
            sizes[b * OWN + t] = counts[row]
            items += jnp.maximum((counts[row] + CHUNK - 1) // CHUNK, 1)
    rows[tiles] = 0
    sizes[tiles] = 0

    def advance(t, j):
        more = (j + 1) * CHUNK < sizes[t]
        return jnp.where(more, t, jnp.minimum(t + 1, tiles)), jnp.where(more, j + 1, 0)

    def listed(t, j):
        row = rows[t]
        word = lists[row * (KEYS // CHUNK) + j]
        return [(word >> (8 * u)) & 255 for u in range(CHUNK)]

    def score(lane, t, j):
        left = sizes[t] - j * CHUNK
        tile = listed(t, j)
        s = lax.dot_general(
            jnp.concatenate([ks[u] for u in tile], axis=0),
            qs[jnp.minimum(t, tiles - 1)],
            (((1,), (1,)), ((), ())),
            preferred_element_type=jnp.float32,
        )
        s_refs[lane][...] = s
        top = jnp.full((8, BLK), NEG, jnp.float32)
        for u in range(CHUNK):
            part = jnp.max(s[u * BLK : (u + 1) * BLK].reshape(16, 8, BLK), axis=0)
            top = jnp.maximum(top, jnp.where(u < left, part, NEG))
        top_refs[lane][...] = jnp.max(top, axis=0, keepdims=True)

    def blend(lane, t, j):
        left = sizes[t] - j * CHUNK
        m_old = m_ref[t]
        m_new = jnp.maximum(m_old, top_refs[lane][...])
        m_ref[t] = m_new
        alpha = jnp.exp2((m_old - m_new) * (SCALE * LOG2E))
        base = m_new * (SCALE * LOG2E)
        total = jnp.zeros((8, BLK), jnp.float32)
        weights = []
        for u in range(CHUNK):
            s = s_refs[lane][u * BLK : (u + 1) * BLK] * (SCALE * LOG2E)
            w = jnp.exp2(s - jnp.where(u < left, base, -NEG))
            total = total + jnp.sum(w.reshape(16, 8, BLK), axis=0)
            weights.append(w.astype(jnp.bfloat16))
        vt = jnp.concatenate([vs[tile] for tile in listed(t, j)], axis=1)
        mixed = jnp.dot(vt, jnp.concatenate(weights, axis=0), preferred_element_type=jnp.float32)
        l_ref[t] = l_ref[t] * alpha + total
        acc_ref[t] = acc_ref[t] * alpha + mixed

    def following(t, j):
        group = []
        for _ in range(WIDTH):
            t, j = advance(t, j)
            group += [t, j]
        return tuple(group)

    first = [jnp.int32(0), jnp.int32(0)]
    for _ in range(WIDTH - 1):
        first += advance(*first[-2:])
    for lane in range(WIDTH):
        score(lane, first[2 * lane], first[2 * lane + 1])

    def step(_, now):
        later = following(*now[-2:])
        for lane in range(WIDTH):
            blend(lane, now[2 * lane], now[2 * lane + 1])
            score(lane, later[2 * lane], later[2 * lane + 1])
        return later

    lax.fori_loop(0, (items + WIDTH - 1) // WIDTH, step, tuple(first))

    for b in range(len(blocks)):

        def finish(i, _):
            for u in range(4):
                t = i * 4 + u
                total = jnp.sum(l_ref[b * OWN + t], axis=0, keepdims=True)
                some = total > 0.0
                safe = jnp.where(some, total, 1.0)
                share = jnp.where(some, 1.0 / safe, 0.0)
                lse = jnp.where(some, m_ref[b * OWN + t] * SCALE + jnp.log(safe), NEG)
                e_out[b][pl.ds(t, 1)] = lse
                high = lse.astype(jnp.bfloat16)
                middle = (lse - high.astype(jnp.float32)).astype(jnp.bfloat16)
                low = (lse - high.astype(jnp.float32) - middle.astype(jnp.float32)).astype(
                    jnp.bfloat16
                )
                o_out[b][t, :HD] = (acc_ref[b * OWN + t] * share).astype(jnp.bfloat16)
                o_out[b][t, HD:] = jnp.concatenate(
                    [high, middle, low, jnp.zeros((PAD - 3, BLK), jnp.bfloat16)], axis=0
                )
            return 0

        lax.fori_loop(0, OWN // 4, finish, 0)


def attend(blocks, lists, counts, queries, keys_values, first_call=False):
    tiles = jax.ShapeDtypeStruct((OWN, HD + PAD, BLK), jnp.bfloat16)
    logs = jax.ShapeDtypeStruct((OWN, BLK), jnp.float32)
    held = (jax.ShapeDtypeStruct((KEYS, BLK, HD), jnp.bfloat16),) * 2 if first_call else ()
    count = len(blocks)
    slots = count * OWN + 1
    pairs = count * OWN * 15
    return pl.pallas_call(
        functools.partial(attend_kernel, blocks, first_call),
        out_shape=held + (tiles,) * count + (logs,) * count,
        in_specs=[SMEM, SMEM] + [VMEM] * (count + len(keys_values)),
        out_specs=(VMEM,) * (2 * count + len(held)),
        scratch_shapes=[
            pltpu.SMEM((slots,), jnp.int32),
            pltpu.SMEM((slots,), jnp.int32),
            pltpu.VMEM((count * OWN, BLK, HD), jnp.bfloat16),
            pltpu.VMEM((slots, 1, BLK), jnp.float32),
            pltpu.VMEM((slots, 8, BLK), jnp.float32),
            pltpu.VMEM((slots, HD, BLK), jnp.float32),
        ]
        + [pltpu.VMEM((CHUNK * BLK, BLK), jnp.float32)] * WIDTH
        + [pltpu.VMEM((1, BLK), jnp.float32)] * WIDTH,
        compiler_params=SPACE,
        cost_estimate=pl.CostEstimate(
            flops=pairs * 4 * BLK * BLK * HD,
            bytes_accessed=5 << 20,
            transcendentals=pairs * BLK * BLK,
        ),
        name="attend",
    )(lists, counts, *queries, *keys_values)


def combine_kernel(*refs):
    outs, o_ref = refs[:-1], refs[-1]
    for t in range(OWN):
        parts = []
        for o in outs:
            split = o[t, HD:].astype(jnp.float32)
            parts.append(split[0:1] + split[1:2] + split[2:3])
        top = jnp.maximum(jnp.maximum(parts[0], parts[1]), jnp.maximum(parts[2], parts[3]))
        shares = [jnp.exp(part - top) for part in parts]
        total = (shares[0] + shares[1]) + (shares[2] + shares[3])
        mixed = sum(o[t, :HD].astype(jnp.float32) * (w / total) for o, w in zip(outs, shares))
        o_ref[t] = mixed.T.astype(jnp.bfloat16)


def combine(outs):
    return pl.pallas_call(
        combine_kernel,
        out_shape=jax.ShapeDtypeStruct((OWN, BLK, HD), jnp.bfloat16),
        in_specs=[VMEM] * RING,
        out_specs=VMEM,
        compiler_params=SPACE,
        name="combine",
    )(*outs)


def settle_kernel(spots, e0, e1, e2, e3, *refs):
    outs, merged = refs[:RING], refs[RING]
    parts = (e0, e1, e2, e3)
    for block in range(RING):
        part = [
            parts[s][(block - s) % RING * OWN : ((block - s) % RING + 1) * OWN] for s in range(RING)
        ]
        top = jnp.maximum(jnp.maximum(part[0], part[1]), jnp.maximum(part[2], part[3]))
        total = sum(jnp.exp(p - top) for p in part)
        merged[block * OWN : (block + 1) * OWN] = top + jnp.log(total)
    merged[KEYS : KEYS + 8] = jnp.zeros((8, BLK), jnp.float32)
    for away, out in enumerate(outs):
        for slot in range(OWN):
            out[slot : slot + 1] = merged[pl.ds(spots[away * OWN + slot], 1)]


def settle(spots, parts):
    return pl.pallas_call(
        settle_kernel,
        out_shape=(jax.ShapeDtypeStruct((OWN, BLK), jnp.float32),) * RING,
        in_specs=[SMEM] + [VMEM] * RING,
        out_specs=(VMEM,) * RING,
        scratch_shapes=[pltpu.VMEM((KEYS + 8, BLK), jnp.float32)],
        compiler_params=SPACE,
        name="settle",
    )(spots, *parts)


def slot_spots(assign, xi, yi):
    away = jnp.arange(RING * OWN, dtype=jnp.int32) // OWN
    slots = ((xi + away) % RING * RING + yi) * OWN + jnp.arange(RING * OWN, dtype=jnp.int32) % OWN
    match = slots[:, None] == jnp.arange(assign.shape[0], dtype=jnp.int32)[None, :]
    tiles = jnp.sum(jnp.where(match, assign[None, :], 0), axis=1)
    spots = (tiles % OWN // 3 - yi) % RING * OWN + tiles % KEYS // OWN * 3 + tiles % 3
    return jnp.where(tiles // KEYS == xi, spots, KEYS)


def deliver(array, away):
    pairs = []
    for x in range(RING):
        for zh in range(RING):
            for y in range(RING):
                source = (x * RING + zh) * RING + y
                pairs.append((source, ((x + away) % RING * RING + y) * RING + zh))
    return lax.ppermute(array, ("x", "zh", "y"), pairs)


def key_lists(kv_tiles, tile_count, xi, yi):
    rows = lax.dynamic_slice_in_dim(kv_tiles, xi * KEYS, KEYS)
    used = lax.dynamic_slice_in_dim(tile_count, xi * KEYS, KEYS)
    here = (rows % OWN // 3 == yi) & (jnp.arange(LIST, dtype=jnp.int32)[None, :] < used[:, None])
    place = (rows // KEYS - xi) % RING * OWN + rows % KEYS // OWN * 3 + rows % 3
    before = jnp.arange(LIST)[:, None] < jnp.arange(LIST)[None, :]
    rank = jnp.dot(
        here.astype(jnp.bfloat16), before.astype(jnp.bfloat16), preferred_element_type=jnp.float32
    ).astype(jnp.int32)
    step = jnp.arange(KEYS // CHUNK, dtype=jnp.int32)[None, :, None]
    at = here[:, None, :] & (rank[:, None, :] // CHUNK == step)
    word = place << (8 * (rank % CHUNK))
    lists = jnp.sum(jnp.where(at, word[:, None, :], 0), axis=2).reshape(-1)
    return lists, jnp.sum(here.astype(jnp.int32), axis=1)


def exchange(array):
    return lax.all_to_all(array, GROUP, split_axis=0, concat_axis=0, tiled=True)


def on_device(queries, keys, values, kv_tiles, tile_count, assign):
    xi, yi = lax.axis_index("x"), lax.axis_index("y")
    lists, counts = key_lists(kv_tiles, tile_count, xi, yi)
    spots = slot_spots(assign, xi, yi)
    by_head = jnp.transpose(queries.reshape(96, 16, HD), (1, 0, 2))
    got = exchange(spread(keys, values))
    got, lists, counts, spots, by_head = lax.optimization_barrier(
        (got, lists, counts, spots, by_head)
    )
    kv0 = prepare(got)
    kv1, kv3 = shift(kv0, "x", -1), shift(kv0, "x", 1)
    q0 = exchange(by_head).reshape(OWN, BLK, HD)
    k2, v2 = shift(kv3[0], "x", 1), shift(kv1[1], "x", -1)
    q1, q3 = shift(q0, "y", -1), shift(q0, "y", 1)
    half = OWN // 2
    q2 = jnp.concatenate([shift(q3[:half], "y", 1), shift(q1[half:], "y", -1)])
    all_keys, all_values, o1, o3, e1, e3 = attend(
        (1, 3), lists, counts, (q1, q3), (kv0, kv1, kv3, k2, v2), first_call=True
    )
    o2, e2 = attend((2,), lists, counts, (q2,), (all_keys, all_values))
    o0, e0 = attend((0,), lists, counts, (q0,), (all_keys, all_values))
    picked = settle(spots, around(jnp.concatenate([e0, e1, e2, e3]), "y"))
    blended = combine((o0, shift(o1, "y", 1), shift(o2, "y", 2), shift(o3, "y", -1)))
    back = exchange(blended.reshape(16, 96, HD))
    attended = jnp.transpose(back, (1, 0, 2)).reshape(96, 16 * HD)
    slot_lse = sum(deliver(array, away) for away, array in enumerate(picked))
    return attended, slot_lse.reshape(1, OWN * BLK)


def solution(mesh):
    split = jax.sharding.Mesh(
        mesh.devices.reshape(RING, RING, RING, 2, 2), ("x", "zh", "y", "zl", "core")
    )
    tokens = P(("x", "zh", "y", "zl", "core"), None)
    return jax.shard_map(
        on_device,
        mesh=split,
        in_specs=(tokens, tokens, tokens, P(), P(), P()),
        out_specs=(tokens, P(("y", "zl", "core"), ("x", "zh"))),
        check_vma=False,
    )
```

```python
import functools

import jax
import jax.numpy as jnp
from jax import lax
from jax.experimental import pallas as pl
from jax.experimental.pallas import tpu as pltpu
from jax.sharding import PartitionSpec as P

HD = 128
BLK = 128
LIST = 96
RING = 4
OWN = 12
KEYS = RING * OWN
CHUNK = 4
WIDTH = 4
PAD = 16
NEG = -1e30
SCALE = HD**-0.5
LOG2E = 1.4426950408889634
VMEM = pl.BlockSpec(memory_space=pltpu.VMEM)
SMEM = pl.BlockSpec(memory_space=pltpu.SMEM)
SPACE = pltpu.CompilerParams(vmem_limit_bytes=16 * 1024 * 1024)
GROUP = ("zh", "zl", "core")


def shift(array, axis, by):
    return lax.ppermute(array, axis, [(i, (i + by) % RING) for i in range(RING)])


def around(array, axis):
    return [array] + [shift(array, axis, -by) for by in range(1, RING)]


def spread_kernel(keys, values, out, sems):
    copies = [
        pltpu.make_async_copy(
            array.at[:, pl.ds(head * HD, HD)], out.at[head, which], sems.at[which, head]
        )
        for which, array in enumerate((keys, values))
        for head in range(16)
    ]
    for copy in copies:
        copy.start()
    for copy in copies:
        copy.wait()


def spread(keys, values):
    return pl.pallas_call(
        spread_kernel,
        out_shape=jax.ShapeDtypeStruct((16, 2, 96, HD), jnp.bfloat16),
        in_specs=[pl.BlockSpec(memory_space=pltpu.HBM)] * 2,
        out_specs=VMEM,
        scratch_shapes=[pltpu.SemaphoreType.DMA((2, 16))],
        compiler_params=SPACE,
        name="spread",
    )(keys, values)


def prepare_kernel(got_ref, kv_ref):
    for part in range(RING):
        k, v = (
            got_ref[4 * part : 4 * part + 4, which].reshape(3, BLK, HD) for which in range(2)
        )
        kv_ref[0, 3 * part : 3 * part + 3] = k
        for i in range(3):
            kv_ref[1, 3 * part + i] = v[i].T


def prepare(got):
    return pl.pallas_call(
        prepare_kernel,
        out_shape=jax.ShapeDtypeStruct((2, OWN, BLK, HD), jnp.bfloat16),
        in_specs=[VMEM],
        out_specs=VMEM,
        compiler_params=SPACE,
        name="prepare",
    )(got)


def attend_kernel(blocks, first_call, lists, counts, *refs):
    tiles = len(blocks) * OWN
    queries, refs = refs[: len(blocks)], refs[len(blocks) :]
    if first_call:
        kv0, kv1, kv3, k2, v2, ks, vs = refs[:7]
        refs = refs[7:]
    else:
        ks, vs = refs[:2]
        refs = refs[2:]
    o_out, refs = refs[: len(blocks)], refs[len(blocks) :]
    e_out, refs = refs[: len(blocks)], refs[len(blocks) :]
    rows, sizes, qs, m_ref, l_ref, acc_ref = refs[:6]
    s_refs, top_refs = refs[6 : 6 + WIDTH], refs[6 + WIDTH :]
    for b, q in enumerate(queries):
        qs[b * OWN : (b + 1) * OWN] = q[...]
    if first_call:
        for b, k, v in (
            (0, kv0.at[0], kv0.at[1]),
            (1, kv1.at[0], kv1.at[1]),
            (2, k2, v2),
            (3, kv3.at[0], kv3.at[1]),
        ):
            ks[b * OWN : (b + 1) * OWN] = k[...]
            vs[b * OWN : (b + 1) * OWN] = v[...]
    m_ref[...] = jnp.full(m_ref.shape, NEG, jnp.float32)
    l_ref[...] = jnp.zeros(l_ref.shape, jnp.float32)
    acc_ref[...] = jnp.zeros(acc_ref.shape, jnp.float32)
    yi = lax.axis_index("y")
    items = jnp.int32(0)
    for b, block in enumerate(blocks):
        owner = lax.rem(yi + block, RING) * 3
        for t in range(OWN):
            row = owner + (t // 3 * OWN + t % 3)
            rows[b * OWN + t] = row
            sizes[b * OWN + t] = counts[row]
            items += jnp.maximum((counts[row] + CHUNK - 1) // CHUNK, 1)
    rows[tiles] = 0
    sizes[tiles] = 0

    def advance(t, j):
        more = (j + 1) * CHUNK < sizes[t]
        return jnp.where(more, t, jnp.minimum(t + 1, tiles)), jnp.where(more, j + 1, 0)

    def listed(t, j):
        row = rows[t]
        return [lists[row, j * CHUNK + u] for u in range(CHUNK)]

    def score(lane, t, j):
        left = sizes[t] - j * CHUNK
        tile = listed(t, j)
        s = lax.dot_general(
            jnp.concatenate([ks[u] for u in tile], axis=0),
            qs[jnp.minimum(t, tiles - 1)],
            (((1,), (1,)), ((), ())),
            preferred_element_type=jnp.float32,
        )
        s_refs[lane][...] = s
        top = jnp.full((8, BLK), NEG, jnp.float32)
        for u in range(CHUNK):
            part = jnp.max(s[u * BLK : (u + 1) * BLK].reshape(16, 8, BLK), axis=0)
            top = jnp.maximum(top, jnp.where(u < left, part, NEG))
        top_refs[lane][...] = jnp.max(top, axis=0, keepdims=True)

    def blend(lane, t, j):
        left = sizes[t] - j * CHUNK
        m_old = m_ref[t]
        m_new = jnp.maximum(m_old, top_refs[lane][...])
        m_ref[t] = m_new
        alpha = jnp.exp2((m_old - m_new) * (SCALE * LOG2E))
        base = m_new * (SCALE * LOG2E)
        total = jnp.zeros((8, BLK), jnp.float32)
        weights = []
        for u in range(CHUNK):
            s = s_refs[lane][u * BLK : (u + 1) * BLK] * (SCALE * LOG2E)
            w = jnp.exp2(s - jnp.where(u < left, base, -NEG))
            total = total + jnp.sum(w.reshape(16, 8, BLK), axis=0)
            weights.append(w.astype(jnp.bfloat16))
        vt = jnp.concatenate([vs[tile] for tile in listed(t, j)], axis=1)
        mixed = jnp.dot(vt, jnp.concatenate(weights, axis=0), preferred_element_type=jnp.float32)
        l_ref[t] = l_ref[t] * alpha + total
        acc_ref[t] = acc_ref[t] * alpha + mixed

    def following(t, j):
        group = []
        for _ in range(WIDTH):
            t, j = advance(t, j)
            group += [t, j]
        return tuple(group)

    first = [jnp.int32(0), jnp.int32(0)]
    for _ in range(WIDTH - 1):
        first += advance(*first[-2:])
    for lane in range(WIDTH):
        score(lane, first[2 * lane], first[2 * lane + 1])

    def step(_, now):
        later = following(*now[-2:])
        for lane in range(WIDTH):
            blend(lane, now[2 * lane], now[2 * lane + 1])
            score(lane, later[2 * lane], later[2 * lane + 1])
        return later

    lax.fori_loop(0, (items + WIDTH - 1) // WIDTH, step, tuple(first))

    for b in range(len(blocks)):

        def finish(i, _):
            for u in range(4):
                t = i * 4 + u
                total = jnp.sum(l_ref[b * OWN + t], axis=0, keepdims=True)
                some = total > 0.0
                safe = jnp.where(some, total, 1.0)
                share = jnp.where(some, 1.0 / safe, 0.0)
                lse = jnp.where(some, m_ref[b * OWN + t] * SCALE + jnp.log(safe), NEG)
                e_out[b][pl.ds(t, 1)] = lse
                high = lse.astype(jnp.bfloat16)
                middle = (lse - high.astype(jnp.float32)).astype(jnp.bfloat16)
                low = (lse - high.astype(jnp.float32) - middle.astype(jnp.float32)).astype(
                    jnp.bfloat16
                )
                o_out[b][t, :HD] = (acc_ref[b * OWN + t] * share).astype(jnp.bfloat16)
                o_out[b][t, HD:] = jnp.concatenate(
                    [high, middle, low, jnp.zeros((PAD - 3, BLK), jnp.bfloat16)], axis=0
                )
            return 0

        lax.fori_loop(0, OWN // 4, finish, 0)


def attend(blocks, lists, counts, queries, keys_values, first_call=False):
    tiles = jax.ShapeDtypeStruct((OWN, HD + PAD, BLK), jnp.bfloat16)
    logs = jax.ShapeDtypeStruct((OWN, BLK), jnp.float32)
    held = (jax.ShapeDtypeStruct((KEYS, BLK, HD), jnp.bfloat16),) * 2 if first_call else ()
    count = len(blocks)
    slots = count * OWN + 1
    pairs = count * OWN * 15
    return pl.pallas_call(
        functools.partial(attend_kernel, blocks, first_call),
        out_shape=held + (tiles,) * count + (logs,) * count,
        in_specs=[SMEM, SMEM] + [VMEM] * (count + len(keys_values)),
        out_specs=(VMEM,) * (2 * count + len(held)),
        scratch_shapes=[
            pltpu.SMEM((slots,), jnp.int32),
            pltpu.SMEM((slots,), jnp.int32),
            pltpu.VMEM((count * OWN, BLK, HD), jnp.bfloat16),
            pltpu.VMEM((slots, 1, BLK), jnp.float32),
            pltpu.VMEM((slots, 8, BLK), jnp.float32),
            pltpu.VMEM((slots, HD, BLK), jnp.float32),
        ]
        + [pltpu.VMEM((CHUNK * BLK, BLK), jnp.float32)] * WIDTH
        + [pltpu.VMEM((1, BLK), jnp.float32)] * WIDTH,
        compiler_params=SPACE,
        cost_estimate=pl.CostEstimate(
            flops=pairs * 4 * BLK * BLK * HD,
            bytes_accessed=5 << 20,
            transcendentals=pairs * BLK * BLK,
        ),
        name="attend",
    )(lists, counts, *queries, *keys_values)


def combine_kernel(*refs):
    outs, o_ref = refs[:-1], refs[-1]
    for t in range(OWN):
        parts = []
        for o in outs:
            split = o[t, HD:].astype(jnp.float32)
            parts.append(split[0:1] + split[1:2] + split[2:3])
        top = jnp.maximum(jnp.maximum(parts[0], parts[1]), jnp.maximum(parts[2], parts[3]))
        shares = [jnp.exp(part - top) for part in parts]
        total = (shares[0] + shares[1]) + (shares[2] + shares[3])
        mixed = sum(o[t, :HD].astype(jnp.float32) * (w / total) for o, w in zip(outs, shares))
        o_ref[t] = mixed.T.astype(jnp.bfloat16)


def combine(outs):
    return pl.pallas_call(
        combine_kernel,
        out_shape=jax.ShapeDtypeStruct((OWN, BLK, HD), jnp.bfloat16),
        in_specs=[VMEM] * RING,
        out_specs=VMEM,
        compiler_params=SPACE,
        name="combine",
    )(*outs)


def settle_kernel(e0, e1, e2, e3, out):
    parts = (e0, e1, e2, e3)
    for block in range(RING):
        part = [
            parts[s][(block - s) % RING * OWN : ((block - s) % RING + 1) * OWN] for s in range(RING)
        ]
        top = jnp.maximum(jnp.maximum(part[0], part[1]), jnp.maximum(part[2], part[3]))
        total = sum(jnp.exp(p - top) for p in part)
        out[block * OWN : (block + 1) * OWN] = top + jnp.log(total)


def settle(parts):
    return pl.pallas_call(
        settle_kernel,
        out_shape=jax.ShapeDtypeStruct((KEYS, BLK), jnp.float32),
        in_specs=[VMEM] * RING,
        out_specs=VMEM,
        compiler_params=SPACE,
        name="settle",
    )(*parts)


def choose_kernel(spots, *refs):
    logs, outs, every = refs[:RING], refs[RING : 2 * RING], refs[2 * RING]
    for away, log in enumerate(logs):
        every[away * KEYS : (away + 1) * KEYS] = log[...]
    for away, out in enumerate(outs):
        for slot in range(OWN):
            out[slot : slot + 1] = every[pl.ds(spots[away * OWN + slot], 1)]


def choose(spots, logs):
    return pl.pallas_call(
        choose_kernel,
        out_shape=(jax.ShapeDtypeStruct((OWN, BLK), jnp.float32),) * RING,
        in_specs=[SMEM] + [VMEM] * RING,
        out_specs=(VMEM,) * RING,
        scratch_shapes=[pltpu.VMEM((RING * KEYS, BLK), jnp.float32)],
        compiler_params=SPACE,
        name="choose",
    )(spots, *logs)


def slot_spots(assign, xi, yi, zi):
    away = jnp.arange(RING * OWN, dtype=jnp.int32) // OWN
    slots = (xi * RING + (zi + away) % RING) * OWN + jnp.arange(RING * OWN, dtype=jnp.int32) % OWN
    match = slots[:, None] == jnp.arange(assign.shape[0], dtype=jnp.int32)[None, :]
    tiles = jnp.sum(jnp.where(match, assign[None, :], 0), axis=1)
    spots = (tiles // KEYS - xi) % RING * KEYS + (tiles % OWN // 3 - yi) % RING * OWN
    return spots + tiles % KEYS // OWN * 3 + tiles % 3


def key_lists(kv_tiles, tile_count, xi, yi):
    rows = lax.dynamic_slice_in_dim(kv_tiles, xi * KEYS, KEYS)
    used = lax.dynamic_slice_in_dim(tile_count, xi * KEYS, KEYS)
    here = (rows % OWN // 3 == yi) & (jnp.arange(LIST, dtype=jnp.int32)[None, :] < used[:, None])
    place = (rows // KEYS - xi) % RING * OWN + rows % KEYS // OWN * 3 + rows % 3
    before = jnp.arange(LIST)[:, None] < jnp.arange(LIST)[None, :]
    rank = jnp.dot(
        here.astype(jnp.bfloat16), before.astype(jnp.bfloat16), preferred_element_type=jnp.float32
    ).astype(jnp.int32)
    at = here[:, None, :] & (rank[:, None, :] == jnp.arange(KEYS, dtype=jnp.int32)[None, :, None])
    lists = jnp.sum(jnp.where(at, place[:, None, :], 0), axis=2)
    return lists, jnp.sum(here.astype(jnp.int32), axis=1)


def exchange(array):
    return lax.all_to_all(array, GROUP, split_axis=0, concat_axis=0, tiled=True)


def on_device(queries, keys, values, kv_tiles, tile_count, assign):
    xi, yi, zi = lax.axis_index("x"), lax.axis_index("y"), lax.axis_index("zh")
    lists, counts = key_lists(kv_tiles, tile_count, xi, yi)
    spots = slot_spots(assign, xi, yi, zi)
    by_head = jnp.transpose(queries.reshape(96, 16, HD), (1, 0, 2))
    got = exchange(spread(keys, values))
    got, lists, counts, spots, by_head = lax.optimization_barrier(
        (got, lists, counts, spots, by_head)
    )
    kv0 = prepare(got)
    kv1, kv3 = shift(kv0, "x", -1), shift(kv0, "x", 1)
    q0 = exchange(by_head).reshape(OWN, BLK, HD)
    k2, v2 = shift(kv3[0], "x", 1), shift(kv1[1], "x", -1)
    q1, q3 = shift(q0, "y", -1), shift(q0, "y", 1)
    q2 = shift(q0, "y", -2)
    all_keys, all_values, o2, e2 = attend(
        (2,), lists, counts, (q2,), (kv0, kv1, kv3, k2, v2), first_call=True
    )
    o1, o3, e1, e3 = attend((1, 3), lists, counts, (q1, q3), (all_keys, all_values))
    q0, o1 = lax.optimization_barrier((q0, o1))
    o0, e0 = attend((0,), lists, counts, (q0,), (all_keys, all_values))
    parts = around(jnp.concatenate([e0, e1, e2, e3]), "y")
    *parts, o0 = lax.optimization_barrier((*parts, o0))
    blended = combine((o0, shift(o1, "y", 1), shift(o2, "y", 2), shift(o3, "y", -1)))
    back = exchange(blended.reshape(16, 96, HD))
    attended = jnp.transpose(back, (1, 0, 2)).reshape(96, 16 * HD)
    picked = choose(spots, around(settle(parts), "x"))
    slot_lse = sum(
        jnp.where((zi - yi) % RING == away, shift(array, "zh", away), 0.0)
        for away, array in enumerate(picked)
    )
    return attended, slot_lse.reshape(1, OWN * BLK)


def solution(mesh):
    split = jax.sharding.Mesh(
        mesh.devices.reshape(RING, RING, RING, 2, 2), ("x", "zh", "y", "zl", "core")
    )
    tokens = P(("x", "zh", "y", "zl", "core"), None)
    return jax.shard_map(
        on_device,
        mesh=split,
        in_specs=(tokens, tokens, tokens, P(), P(), P()),
        out_specs=(tokens, P(("y", "zl", "core"), ("x", "zh"))),
        check_vma=False,
    )
```

```python
import functools

import jax
import jax.numpy as jnp
from jax import lax
from jax.experimental import pallas as pl
from jax.experimental.pallas import tpu as pltpu
from jax.sharding import PartitionSpec as P

HD = 128
BLK = 128
LIST = 96
RING = 4
OWN = 12
KEYS = RING * OWN
NEAR = 3 * OWN
CHUNK = 4
WIDTH = 4
PAD = 16
NEG = -1e30
SCALE = HD**-0.5
LOG2E = 1.4426950408889634
VMEM = pl.BlockSpec(memory_space=pltpu.VMEM)
SMEM = pl.BlockSpec(memory_space=pltpu.SMEM)
SPACE = pltpu.CompilerParams(vmem_limit_bytes=16 * 1024 * 1024)
GROUP = ("zh", "zl", "core")


def shift(array, axis, by):
    return lax.ppermute(array, axis, [(i, (i + by) % RING) for i in range(RING)])


def around(array, axis):
    return [array] + [shift(array, axis, -by) for by in range(1, RING)]


def spread_kernel(keys, values, out, sems):
    copies = [
        pltpu.make_async_copy(
            array.at[:, pl.ds(head * HD, HD)], out.at[head, which], sems.at[which, head]
        )
        for which, array in enumerate((keys, values))
        for head in range(16)
    ]
    for copy in copies:
        copy.start()
    for copy in copies:
        copy.wait()


def spread(keys, values):
    return pl.pallas_call(
        spread_kernel,
        out_shape=jax.ShapeDtypeStruct((16, 2, 96, HD), jnp.bfloat16),
        in_specs=[pl.BlockSpec(memory_space=pltpu.HBM)] * 2,
        out_specs=VMEM,
        scratch_shapes=[pltpu.SemaphoreType.DMA((2, 16))],
        compiler_params=SPACE,
        name="spread",
    )(keys, values)


def prepare_kernel(got_ref, kv_ref):
    for part in range(RING):
        k, v = (
            got_ref[4 * part : 4 * part + 4, which].reshape(3, BLK, HD) for which in range(2)
        )
        kv_ref[0, 3 * part : 3 * part + 3] = k
        for i in range(3):
            kv_ref[1, 3 * part + i] = v[i].T


def prepare(got):
    return pl.pallas_call(
        prepare_kernel,
        out_shape=jax.ShapeDtypeStruct((2, OWN, BLK, HD), jnp.bfloat16),
        in_specs=[VMEM],
        out_specs=VMEM,
        compiler_params=SPACE,
        name="prepare",
    )(got)


def split(log):
    high = log.astype(jnp.bfloat16)
    rest = log - high.astype(jnp.float32)
    middle = rest.astype(jnp.bfloat16)
    return [high, middle, (rest - middle.astype(jnp.float32)).astype(jnp.bfloat16)]


def joined(rows, block):
    parts = [rows[3 * block + i : 3 * block + i + 1] for i in range(3)]
    return parts[0] + parts[1] + parts[2]


def attend_kernel(blocks, mode, last, lists, nears, counts, *refs):
    count = len(blocks)
    tiles = count * OWN
    queries, refs = refs[:count], refs[count:]
    if mode != "far":
        for_near, refs = refs[:3], refs[3:]
    if mode != "near":
        (k2, v2), refs = refs[:2], refs[2:]
    if mode == "far":
        states, refs = refs[: 3 * count], refs[3 * count :]
    if last:
        (e0, e2), refs = refs[:2], refs[2:]
    size = (3 if mode == "near" else 2) * count + last
    outs, refs = refs[:size], refs[size:]
    rows, begins, sizes, qs, ks, vs, m_ref, l_ref, acc_ref = refs[:9]
    s_refs, top_refs = refs[9 : 9 + WIDTH], refs[9 + WIDTH :]
    for b, q in enumerate(queries):
        qs[b * OWN : (b + 1) * OWN] = q[...]
    if mode != "far":
        for b, kv in enumerate(for_near):
            ks[b * OWN : (b + 1) * OWN] = kv[0]
            vs[b * OWN : (b + 1) * OWN] = kv[1]
    if mode != "near":
        at = 0 if mode == "far" else NEAR
        ks[at : at + OWN] = k2[...]
        vs[at : at + OWN] = v2[...]
    m_ref[...] = jnp.full(m_ref.shape, NEG, jnp.float32)
    l_ref[...] = jnp.zeros(l_ref.shape, jnp.float32)
    acc_ref[...] = jnp.zeros(acc_ref.shape, jnp.float32)
    if mode == "far":
        for b in range(count):
            for held, state in zip((m_ref, l_ref, acc_ref), states[3 * b : 3 * b + 3]):
                held[b * OWN : (b + 1) * OWN] = state[...]
    yi = lax.axis_index("y")
    items = jnp.int32(0)
    for b, block in enumerate(blocks):
        owner = lax.rem(yi + block, RING) * 3
        for t in range(OWN):
            row = owner + (t // 3 * OWN + t % 3)
            begin = nears[row] if mode == "far" else jnp.int32(0)
            total = (nears[row] if mode == "near" else counts[row]) - begin
            rows[b * OWN + t] = row
            begins[b * OWN + t] = begin
            sizes[b * OWN + t] = total
            items += jnp.maximum((total + CHUNK - 1) // CHUNK, 1)
    rows[tiles] = 0
    begins[tiles] = 0
    sizes[tiles] = 0

    def advance(t, j):
        more = (j + 1) * CHUNK < sizes[t]
        return jnp.where(more, t, jnp.minimum(t + 1, tiles)), jnp.where(more, j + 1, 0)

    def listed(t, j):
        row = rows[t]
        at = begins[t] + j * CHUNK
        found = [lists[row, at + u] for u in range(CHUNK)]
        if mode == "near":
            return [jnp.minimum(u, NEAR - 1) for u in found]
        return [jnp.maximum(u - NEAR, 0) for u in found] if mode == "far" else found

    def score(lane, t, j):
        left = sizes[t] - j * CHUNK
        tile = listed(t, j)
        s = lax.dot_general(
            jnp.concatenate([ks[u] for u in tile], axis=0),
            qs[jnp.minimum(t, tiles - 1)],
            (((1,), (1,)), ((), ())),
            preferred_element_type=jnp.float32,
        )
        s_refs[lane][...] = s
        top = jnp.full((8, BLK), NEG, jnp.float32)
        for u in range(CHUNK):
            part = jnp.max(s[u * BLK : (u + 1) * BLK].reshape(16, 8, BLK), axis=0)
            top = jnp.maximum(top, jnp.where(u < left, part, NEG))
        top_refs[lane][...] = jnp.max(top, axis=0, keepdims=True)

    def blend(lane, t, j):
        left = sizes[t] - j * CHUNK
        m_old = m_ref[t]
        m_new = jnp.maximum(m_old, top_refs[lane][...])
        m_ref[t] = m_new
        alpha = jnp.exp2((m_old - m_new) * (SCALE * LOG2E))
        base = m_new * (SCALE * LOG2E)
        total = jnp.zeros((8, BLK), jnp.float32)
        weights = []
        for u in range(CHUNK):
            s = s_refs[lane][u * BLK : (u + 1) * BLK] * (SCALE * LOG2E)
            w = jnp.exp2(s - jnp.where(u < left, base, -NEG))
            total = total + jnp.sum(w.reshape(16, 8, BLK), axis=0)
            weights.append(w.astype(jnp.bfloat16))
        vt = jnp.concatenate([vs[tile] for tile in listed(t, j)], axis=1)
        mixed = jnp.dot(vt, jnp.concatenate(weights, axis=0), preferred_element_type=jnp.float32)
        l_ref[t] = l_ref[t] * alpha + total
        acc_ref[t] = acc_ref[t] * alpha + mixed

    def following(t, j):
        group = []
        for _ in range(WIDTH):
            t, j = advance(t, j)
            group += [t, j]
        return tuple(group)

    start = [jnp.int32(0), jnp.int32(0)]
    for _ in range(WIDTH - 1):
        start += advance(*start[-2:])
    for lane in range(WIDTH):
        score(lane, start[2 * lane], start[2 * lane + 1])

    def step(_, now):
        later = following(*now[-2:])
        for lane in range(WIDTH):
            blend(lane, now[2 * lane], now[2 * lane + 1])
            score(lane, later[2 * lane], later[2 * lane + 1])
        return later

    lax.fori_loop(0, (items + WIDTH - 1) // WIDTH, step, tuple(start))

    if mode == "near":
        for b in range(count):
            for held, out in zip((m_ref, l_ref, acc_ref), outs[3 * b : 3 * b + 3]):
                out[...] = held[b * OWN : (b + 1) * OWN]
        return

    def finish(i, _):
        for u in range(4):
            t = i * 4 + u
            logs = {}
            for b, block in enumerate(blocks):
                total = jnp.sum(l_ref[b * OWN + t], axis=0, keepdims=True)
                some = total > 0.0
                safe = jnp.where(some, total, 1.0)
                share = jnp.where(some, 1.0 / safe, 0.0)
                outs[b][t, :HD] = (acc_ref[b * OWN + t] * share).astype(jnp.bfloat16)
                logs[block] = jnp.where(some, m_ref[b * OWN + t] * SCALE + jnp.log(safe), NEG)
                outs[count + b][pl.ds(t, 1)] = logs[block]
            if last:
                logs[0], logs[2] = e0[pl.ds(t, 1)], e2[pl.ds(t, 1)]
                for block in range(RING):
                    outs[2 * count][pl.ds(block * OWN + t, 1)] = logs[block]
            none = [jnp.zeros((1, BLK), jnp.bfloat16)] * 3
            below = [row for b in range(RING) for row in (split(logs[b]) if b in logs else none)]
            below.append(jnp.zeros((PAD - 3 * RING, BLK), jnp.bfloat16))
            for b in range(count):
                outs[b][t, HD:] = jnp.concatenate(below, axis=0)
        return 0

    lax.fori_loop(0, OWN // 4, finish, 0)


def attend(blocks, mode, lists, queries, keys_values, states=(), logs=()):
    last = bool(logs)
    count = len(blocks)
    slots = count * OWN + 1
    keys = {"near": NEAR, "far": OWN, "full": KEYS}[mode]
    pairs = count * keys * 4
    shapes = ((1, BLK), (8, BLK), (HD, BLK))
    if mode == "near":
        out_shape = [jax.ShapeDtypeStruct((OWN, *shape), jnp.float32) for shape in shapes] * count
    else:
        out_shape = [jax.ShapeDtypeStruct((OWN, HD + PAD, BLK), jnp.bfloat16)] * count
        out_shape += [jax.ShapeDtypeStruct((OWN, BLK), jnp.float32)] * count
        out_shape += [jax.ShapeDtypeStruct((KEYS, BLK), jnp.float32)] * last
    operands = (*queries, *keys_values, *states, *logs)
    return pl.pallas_call(
        functools.partial(attend_kernel, blocks, mode, last),
        out_shape=tuple(out_shape),
        in_specs=[SMEM] * 3 + [VMEM] * len(operands),
        out_specs=(VMEM,) * len(out_shape),
        scratch_shapes=[pltpu.SMEM((slots,), jnp.int32)] * 3
        + [
            pltpu.VMEM((count * OWN, BLK, HD), jnp.bfloat16),
            pltpu.VMEM((keys, BLK, HD), jnp.bfloat16),
            pltpu.VMEM((keys, HD, BLK), jnp.bfloat16),
        ]
        + [pltpu.VMEM((slots, *shape), jnp.float32) for shape in shapes]
        + [pltpu.VMEM((CHUNK * BLK, BLK), jnp.float32)] * WIDTH
        + [pltpu.VMEM((1, BLK), jnp.float32)] * WIDTH,
        compiler_params=SPACE,
        cost_estimate=pl.CostEstimate(
            flops=pairs * 4 * BLK * BLK * HD,
            bytes_accessed=5 << 20,
            transcendentals=pairs * BLK * BLK,
        ),
        name=mode,
    )(*lists, *operands)


def combine_kernel(e0, *refs):
    outs, o_ref = refs[:-1], refs[-1]
    for t in range(OWN):
        parts = [e0[t : t + 1]]
        for block in range(1, RING):
            parts.append(joined(outs[block][t, HD:].astype(jnp.float32), block))
        top = jnp.maximum(jnp.maximum(parts[0], parts[1]), jnp.maximum(parts[2], parts[3]))
        shares = [jnp.exp(part - top) for part in parts]
        total = (shares[0] + shares[1]) + (shares[2] + shares[3])
        mixed = sum(o[t, :HD].astype(jnp.float32) * (w / total) for o, w in zip(outs, shares))
        o_ref[t] = mixed.T.astype(jnp.bfloat16)


def combine(e0, outs):
    return pl.pallas_call(
        combine_kernel,
        out_shape=jax.ShapeDtypeStruct((OWN, BLK, HD), jnp.bfloat16),
        in_specs=[VMEM] * (RING + 1),
        out_specs=VMEM,
        compiler_params=SPACE,
        name="combine",
    )(e0, *outs)


def settle_kernel(own, further, two, before, out, spread_out):
    for s, o in ((1, further), (3, before)):
        for t in range(OWN):
            rows = o[t, HD:].astype(jnp.float32)
            for block in range(RING):
                spread_out[s // 2, block * OWN + t : block * OWN + t + 1] = joined(rows, block)
    for block in range(RING):
        part = []
        for s, logs in enumerate((own, spread_out.at[0], two, spread_out.at[1])):
            at = (block - s) % RING * OWN
            part.append(logs[at : at + OWN])
        top = jnp.maximum(jnp.maximum(part[0], part[1]), jnp.maximum(part[2], part[3]))
        total = sum(jnp.exp(p - top) for p in part)
        out[block * OWN : (block + 1) * OWN] = top + jnp.log(total)


def settle(own, further, two, before):
    return pl.pallas_call(
        settle_kernel,
        out_shape=jax.ShapeDtypeStruct((KEYS, BLK), jnp.float32),
        in_specs=[VMEM] * 4,
        out_specs=VMEM,
        scratch_shapes=[pltpu.VMEM((2, KEYS, BLK), jnp.float32)],
        compiler_params=SPACE,
        name="settle",
    )(own, further, two, before)


def choose_kernel(spots, e0, e1, e2, e3, out, every):
    for away, log in enumerate((e0, e1, e2, e3)):
        every[away * KEYS : (away + 1) * KEYS] = log[...]
    for slot in range(OWN):
        out[slot : slot + 1] = every[pl.ds(spots[slot], 1)]


def choose(spots, logs):
    return pl.pallas_call(
        choose_kernel,
        out_shape=jax.ShapeDtypeStruct((OWN, BLK), jnp.float32),
        in_specs=[SMEM] + [VMEM] * RING,
        out_specs=VMEM,
        scratch_shapes=[pltpu.VMEM((RING * KEYS, BLK), jnp.float32)],
        compiler_params=SPACE,
        name="choose",
    )(spots, *logs)


def slot_spots(assign, xi, yi):
    tiles = lax.dynamic_slice_in_dim(assign, (xi * RING + yi) * OWN, OWN)
    spots = (tiles // KEYS - xi) % RING * KEYS + (tiles % OWN // 3 - yi) % RING * OWN
    return spots + tiles % KEYS // OWN * 3 + tiles % 3


def key_lists(kv_tiles, tile_count, xi, yi):
    rows = lax.dynamic_slice_in_dim(kv_tiles, xi * KEYS, KEYS)
    used = lax.dynamic_slice_in_dim(tile_count, xi * KEYS, KEYS)
    here = (rows % OWN // 3 == yi) & (jnp.arange(LIST, dtype=jnp.int32)[None, :] < used[:, None])
    away = (rows // KEYS - xi) % RING
    block = jnp.where(away == 2, 3, jnp.minimum(away, 2))
    place = block * OWN + rows % KEYS // OWN * 3 + rows % 3
    near, far = here & (away != 2), here & (away == 2)
    nears = jnp.sum(near.astype(jnp.int32), axis=1)
    before = (jnp.arange(LIST)[:, None] < jnp.arange(LIST)[None, :]).astype(jnp.bfloat16)
    rank_near = jnp.dot(near.astype(jnp.bfloat16), before, preferred_element_type=jnp.float32)
    rank_far = jnp.dot(far.astype(jnp.bfloat16), before, preferred_element_type=jnp.float32)
    rank = jnp.where(
        near, rank_near.astype(jnp.int32), nears[:, None] + rank_far.astype(jnp.int32)
    )
    spot = jnp.arange(KEYS + CHUNK, dtype=jnp.int32)[None, :, None]
    at = here[:, None, :] & (rank[:, None, :] == spot)
    lists = jnp.sum(jnp.where(at, place[:, None, :], 0), axis=2)
    return lists, nears, jnp.sum(here.astype(jnp.int32), axis=1)


def exchange(array):
    return lax.all_to_all(array, GROUP, split_axis=0, concat_axis=0, tiled=True)


def on_device(queries, keys, values, kv_tiles, tile_count, assign):
    xi, yi = lax.axis_index("x"), lax.axis_index("y")
    lists = key_lists(kv_tiles, tile_count, xi, yi)
    spots = slot_spots(assign, xi, yi)
    by_head = jnp.transpose(queries.reshape(96, 16, HD), (1, 0, 2))
    got = exchange(spread(keys, values))
    got, by_head, spots, *lists = lax.optimization_barrier((got, by_head, spots, *lists))
    kv0 = prepare(got)
    kv1, kv3 = shift(kv0, "x", -1), shift(kv0, "x", 1)
    q0 = exchange(by_head).reshape(OWN, BLK, HD)
    k2, v2 = shift(kv3[0], "x", 1), shift(kv1[1], "x", -1)
    q0, q1, q2, q3 = around(q0, "y")
    state = attend((0,), "near", lists, (q0,), (kv0, kv1, kv3))
    o0, e0 = attend((0,), "far", lists, (q0,), (k2, v2), state)
    q2, o0 = lax.optimization_barrier((q2, o0))
    kv = (kv0, kv1, kv3, k2, v2)
    o2, e2 = attend((2,), "full", lists, (q2,), kv)
    o1, o3, _, _, logs = attend((1, 3), "full", lists, (q1, q3), kv, logs=(e0, e2))
    o1, o2, o3, logs2 = (
        shift(o1, "y", 1),
        shift(o2, "y", 2),
        shift(o3, "y", -1),
        shift(logs, "y", 2),
    )
    o1, logs2 = lax.optimization_barrier((o1, logs2))
    blended = combine(e0, (o0, o1, o2, o3))
    back = exchange(blended.reshape(16, 96, HD))
    attended = jnp.transpose(back, (1, 0, 2)).reshape(96, 16 * HD)
    chosen = choose(spots, around(settle(logs, o3, logs2, o1), "x"))
    turned = [(b * RING + a, a * RING + b) for a in range(RING) for b in range(RING)]
    return attended, lax.ppermute(chosen.reshape(1, OWN * BLK), ("zh", "y"), turned)


def solution(mesh):
    split = jax.sharding.Mesh(
        mesh.devices.reshape(RING, RING, RING, 2, 2), ("x", "zh", "y", "zl", "core")
    )
    tokens = P(("x", "zh", "y", "zl", "core"), None)
    return jax.shard_map(
        on_device,
        mesh=split,
        in_specs=(tokens, tokens, tokens, P(), P(), P()),
        out_specs=(tokens, P(("y", "zl", "core"), ("x", "zh"))),
        check_vma=False,
    )
```

```python
import functools

import jax
import jax.numpy as jnp
from jax import lax
from jax.experimental import pallas as pl
from jax.experimental.pallas import tpu as pltpu
from jax.sharding import PartitionSpec as P

HD = 128
BLK = 128
LIST = 96
RING = 4
OWN = 12
KEYS = RING * OWN
NEAR = 3 * OWN
CHUNK = 4
WIDTH = 4
PAD = 16
NEG = -1e30
SCALE = HD**-0.5
LOG2E = 1.4426950408889634
VMEM = pl.BlockSpec(memory_space=pltpu.VMEM)
SMEM = pl.BlockSpec(memory_space=pltpu.SMEM)
SPACE = pltpu.CompilerParams(vmem_limit_bytes=16 * 1024 * 1024)
GROUP = ("zh", "zl", "core")


def shift(array, axis, by):
    return lax.ppermute(array, axis, [(i, (i + by) % RING) for i in range(RING)])


def around(array, axis):
    return [array] + [shift(array, axis, -by) for by in range(1, RING)]


def spread_kernel(keys, values, out, sems):
    copies = [
        pltpu.make_async_copy(
            array.at[:, pl.ds(head * HD, HD)], out.at[head, which], sems.at[which, head]
        )
        for which, array in enumerate((keys, values))
        for head in range(16)
    ]
    for copy in copies:
        copy.start()
    for copy in copies:
        copy.wait()


def spread(keys, values):
    return pl.pallas_call(
        spread_kernel,
        out_shape=jax.ShapeDtypeStruct((16, 2, 96, HD), jnp.bfloat16),
        in_specs=[pl.BlockSpec(memory_space=pltpu.HBM)] * 2,
        out_specs=VMEM,
        scratch_shapes=[pltpu.SemaphoreType.DMA((2, 16))],
        compiler_params=SPACE,
        name="spread",
    )(keys, values)


def prepare_kernel(got_ref, kv_ref):
    for part in range(RING):
        k, v = (
            got_ref[4 * part : 4 * part + 4, which].reshape(3, BLK, HD) for which in range(2)
        )
        kv_ref[0, 3 * part : 3 * part + 3] = k
        for i in range(3):
            kv_ref[1, 3 * part + i] = v[i].T


def prepare(got):
    return pl.pallas_call(
        prepare_kernel,
        out_shape=jax.ShapeDtypeStruct((2, OWN, BLK, HD), jnp.bfloat16),
        in_specs=[VMEM],
        out_specs=VMEM,
        compiler_params=SPACE,
        name="prepare",
    )(got)


def split(log):
    high = log.astype(jnp.bfloat16)
    rest = log - high.astype(jnp.float32)
    middle = rest.astype(jnp.bfloat16)
    return [high, middle, (rest - middle.astype(jnp.float32)).astype(jnp.bfloat16)]


def joined(rows, block):
    parts = [rows[3 * block + i : 3 * block + i + 1] for i in range(3)]
    return parts[0] + parts[1] + parts[2]


def attend_kernel(blocks, mode, last, lists, nears, counts, *refs):
    count = len(blocks)
    tiles = count * OWN
    queries, refs = refs[:count], refs[count:]
    if mode != "far":
        for_near, refs = refs[:3], refs[3:]
    if mode != "near":
        (k2, v2), refs = refs[:2], refs[2:]
    if mode == "far":
        states, refs = refs[: 3 * count], refs[3 * count :]
    if last:
        known, refs = refs[:3], refs[3:]
    size = (3 if mode == "near" else 2) * count + last
    outs, refs = refs[:size], refs[size:]
    rows, begins, sizes, qs, ks, vs, m_ref, l_ref, acc_ref = refs[:9]
    s_refs, top_refs = refs[9 : 9 + WIDTH], refs[9 + WIDTH :]
    for b, q in enumerate(queries):
        qs[b * OWN : (b + 1) * OWN] = q[...]
    if mode != "far":
        for b, kv in enumerate(for_near):
            ks[b * OWN : (b + 1) * OWN] = kv[0]
            vs[b * OWN : (b + 1) * OWN] = kv[1]
    if mode != "near":
        at = 0 if mode == "far" else NEAR
        ks[at : at + OWN] = k2[...]
        vs[at : at + OWN] = v2[...]
    m_ref[...] = jnp.full(m_ref.shape, NEG, jnp.float32)
    l_ref[...] = jnp.zeros(l_ref.shape, jnp.float32)
    acc_ref[...] = jnp.zeros(acc_ref.shape, jnp.float32)
    if mode == "far":
        for b in range(count):
            for held, state in zip((m_ref, l_ref, acc_ref), states[3 * b : 3 * b + 3]):
                held[b * OWN : (b + 1) * OWN] = state[...]
    yi = lax.axis_index("y")
    items = jnp.int32(0)
    for b, block in enumerate(blocks):
        owner = lax.rem(yi + block, RING) * 3
        for t in range(OWN):
            row = owner + (t // 3 * OWN + t % 3)
            begin = nears[row] if mode == "far" else jnp.int32(0)
            total = (nears[row] if mode == "near" else counts[row]) - begin
            rows[b * OWN + t] = row
            begins[b * OWN + t] = begin
            sizes[b * OWN + t] = total
            items += jnp.maximum((total + CHUNK - 1) // CHUNK, 1)
    rows[tiles] = 0
    begins[tiles] = 0
    sizes[tiles] = 0

    def advance(t, j):
        more = (j + 1) * CHUNK < sizes[t]
        return jnp.where(more, t, jnp.minimum(t + 1, tiles)), jnp.where(more, j + 1, 0)

    def listed(t, j):
        row = rows[t]
        at = begins[t] + j * CHUNK
        found = [lists[row, at + u] for u in range(CHUNK)]
        if mode == "near":
            return [jnp.minimum(u, NEAR - 1) for u in found]
        return [jnp.maximum(u - NEAR, 0) for u in found] if mode == "far" else found

    def score(lane, t, j):
        left = sizes[t] - j * CHUNK
        tile = listed(t, j)
        s = lax.dot_general(
            jnp.concatenate([ks[u] for u in tile], axis=0),
            qs[jnp.minimum(t, tiles - 1)],
            (((1,), (1,)), ((), ())),
            preferred_element_type=jnp.float32,
        )
        s_refs[lane][...] = s
        top = jnp.full((8, BLK), NEG, jnp.float32)
        for u in range(CHUNK):
            part = jnp.max(s[u * BLK : (u + 1) * BLK].reshape(16, 8, BLK), axis=0)
            top = jnp.maximum(top, jnp.where(u < left, part, NEG))
        top_refs[lane][...] = jnp.max(top, axis=0, keepdims=True)

    def blend(lane, t, j):
        left = sizes[t] - j * CHUNK
        m_old = m_ref[t]
        m_new = jnp.maximum(m_old, top_refs[lane][...])
        m_ref[t] = m_new
        alpha = jnp.exp2((m_old - m_new) * (SCALE * LOG2E))
        base = m_new * (SCALE * LOG2E)
        total = jnp.zeros((8, BLK), jnp.float32)
        weights = []
        for u in range(CHUNK):
            s = s_refs[lane][u * BLK : (u + 1) * BLK] * (SCALE * LOG2E)
            w = jnp.exp2(s - jnp.where(u < left, base, -NEG))
            total = total + jnp.sum(w.reshape(16, 8, BLK), axis=0)
            weights.append(w.astype(jnp.bfloat16))
        vt = jnp.concatenate([vs[tile] for tile in listed(t, j)], axis=1)
        mixed = jnp.dot(vt, jnp.concatenate(weights, axis=0), preferred_element_type=jnp.float32)
        l_ref[t] = l_ref[t] * alpha + total
        acc_ref[t] = acc_ref[t] * alpha + mixed

    def following(t, j):
        group = []
        for _ in range(WIDTH):
            t, j = advance(t, j)
            group += [t, j]
        return tuple(group)

    start = [jnp.int32(0), jnp.int32(0)]
    for _ in range(WIDTH - 1):
        start += advance(*start[-2:])
    for lane in range(WIDTH):
        score(lane, start[2 * lane], start[2 * lane + 1])

    def step(_, now):
        later = following(*now[-2:])
        for lane in range(WIDTH):
            blend(lane, now[2 * lane], now[2 * lane + 1])
            score(lane, later[2 * lane], later[2 * lane + 1])
        return later

    lax.fori_loop(0, (items + WIDTH - 1) // WIDTH, step, tuple(start))

    if mode == "near":
        for b in range(count):
            for held, out in zip((m_ref, l_ref, acc_ref), outs[3 * b : 3 * b + 3]):
                out[...] = held[b * OWN : (b + 1) * OWN]
        return

    def finish(i, _):
        for u in range(4):
            t = i * 4 + u
            logs = {}
            for b, block in enumerate(blocks):
                total = jnp.sum(l_ref[b * OWN + t], axis=0, keepdims=True)
                some = total > 0.0
                safe = jnp.where(some, total, 1.0)
                share = jnp.where(some, 1.0 / safe, 0.0)
                outs[b][t, :HD] = (acc_ref[b * OWN + t] * share).astype(jnp.bfloat16)
                logs[block] = jnp.where(some, m_ref[b * OWN + t] * SCALE + jnp.log(safe), NEG)
                outs[count + b][pl.ds(t, 1)] = logs[block]
            if last:
                for block, log in enumerate((*known, outs[count])):
                    outs[2][pl.ds(block * OWN + t, 1)] = log[pl.ds(t, 1)]
            none = [jnp.zeros((1, BLK), jnp.bfloat16)] * 3
            below = [row for b in range(RING) for row in (split(logs[b]) if b in logs else none)]
            below.append(jnp.zeros((PAD - 3 * RING, BLK), jnp.bfloat16))
            for b in range(count):
                outs[b][t, HD:] = jnp.concatenate(below, axis=0)
        return 0

    lax.fori_loop(0, OWN // 4, finish, 0)


def attend(blocks, mode, lists, queries, keys_values, states=(), logs=()):
    last = bool(logs)
    count = len(blocks)
    slots = count * OWN + 1
    keys = {"near": NEAR, "far": OWN, "full": KEYS}[mode]
    pairs = count * keys * 4
    shapes = ((1, BLK), (8, BLK), (HD, BLK))
    if mode == "near":
        out_shape = [jax.ShapeDtypeStruct((OWN, *shape), jnp.float32) for shape in shapes] * count
    else:
        out_shape = [jax.ShapeDtypeStruct((OWN, HD + PAD, BLK), jnp.bfloat16)] * count
        out_shape += [jax.ShapeDtypeStruct((OWN, BLK), jnp.float32)] * count
        out_shape += [jax.ShapeDtypeStruct((KEYS, BLK), jnp.float32)] * last
    operands = (*queries, *keys_values, *states, *logs)
    return pl.pallas_call(
        functools.partial(attend_kernel, blocks, mode, last),
        out_shape=tuple(out_shape),
        in_specs=[SMEM] * 3 + [VMEM] * len(operands),
        out_specs=(VMEM,) * len(out_shape),
        scratch_shapes=[pltpu.SMEM((slots,), jnp.int32)] * 3
        + [
            pltpu.VMEM((count * OWN, BLK, HD), jnp.bfloat16),
            pltpu.VMEM((keys, BLK, HD), jnp.bfloat16),
            pltpu.VMEM((keys, HD, BLK), jnp.bfloat16),
        ]
        + [pltpu.VMEM((slots, *shape), jnp.float32) for shape in shapes]
        + [pltpu.VMEM((CHUNK * BLK, BLK), jnp.float32)] * WIDTH
        + [pltpu.VMEM((1, BLK), jnp.float32)] * WIDTH,
        compiler_params=SPACE,
        cost_estimate=pl.CostEstimate(
            flops=pairs * 4 * BLK * BLK * HD,
            bytes_accessed=5 << 20,
            transcendentals=pairs * BLK * BLK,
        ),
        name=mode,
    )(*lists, *operands)


def combine_kernel(e0, *refs):
    outs, o_ref = refs[:-1], refs[-1]
    for t in range(OWN):
        parts = [e0[t : t + 1]]
        for block in range(1, RING):
            parts.append(joined(outs[block][t, HD:].astype(jnp.float32), block))
        top = jnp.maximum(jnp.maximum(parts[0], parts[1]), jnp.maximum(parts[2], parts[3]))
        shares = [jnp.exp(part - top) for part in parts]
        total = (shares[0] + shares[1]) + (shares[2] + shares[3])
        mixed = sum(o[t, :HD].astype(jnp.float32) * (w / total) for o, w in zip(outs, shares))
        o_ref[t] = mixed.T.astype(jnp.bfloat16)


def combine(e0, outs):
    return pl.pallas_call(
        combine_kernel,
        out_shape=jax.ShapeDtypeStruct((OWN, BLK, HD), jnp.bfloat16),
        in_specs=[VMEM] * (RING + 1),
        out_specs=VMEM,
        compiler_params=SPACE,
        name="combine",
    )(e0, *outs)


def settle_kernel(e0, e1, e2, e3, out):
    parts = (e0, e1, e2, e3)
    for block in range(RING):
        part = [
            parts[s][(block - s) % RING * OWN : ((block - s) % RING + 1) * OWN] for s in range(RING)
        ]
        top = jnp.maximum(jnp.maximum(part[0], part[1]), jnp.maximum(part[2], part[3]))
        total = sum(jnp.exp(p - top) for p in part)
        out[block * OWN : (block + 1) * OWN] = top + jnp.log(total)


def settle(parts):
    return pl.pallas_call(
        settle_kernel,
        out_shape=jax.ShapeDtypeStruct((KEYS, BLK), jnp.float32),
        in_specs=[VMEM] * RING,
        out_specs=VMEM,
        compiler_params=SPACE,
        name="settle",
    )(*parts)


def choose_kernel(spots, e0, e1, e2, e3, out, every):
    for away, log in enumerate((e0, e1, e2, e3)):
        every[away * KEYS : (away + 1) * KEYS] = log[...]
    for slot in range(OWN):
        out[slot : slot + 1] = every[pl.ds(spots[slot], 1)]


def choose(spots, logs):
    return pl.pallas_call(
        choose_kernel,
        out_shape=jax.ShapeDtypeStruct((OWN, BLK), jnp.float32),
        in_specs=[SMEM] + [VMEM] * RING,
        out_specs=VMEM,
        scratch_shapes=[pltpu.VMEM((RING * KEYS, BLK), jnp.float32)],
        compiler_params=SPACE,
        name="choose",
    )(spots, *logs)


def slot_spots(assign, xi, yi):
    tiles = lax.dynamic_slice_in_dim(assign, (xi * RING + yi) * OWN, OWN)
    spots = (tiles // KEYS - xi) % RING * KEYS + (tiles % OWN // 3 - yi) % RING * OWN
    return spots + tiles % KEYS // OWN * 3 + tiles % 3


def key_lists(kv_tiles, tile_count, xi, yi):
    rows = lax.dynamic_slice_in_dim(kv_tiles, xi * KEYS, KEYS)
    used = lax.dynamic_slice_in_dim(tile_count, xi * KEYS, KEYS)
    here = (rows % OWN // 3 == yi) & (jnp.arange(LIST, dtype=jnp.int32)[None, :] < used[:, None])
    away = (rows // KEYS - xi) % RING
    block = jnp.where(away == 2, 3, jnp.minimum(away, 2))
    place = block * OWN + rows % KEYS // OWN * 3 + rows % 3
    near, far = here & (away != 2), here & (away == 2)
    nears = jnp.sum(near.astype(jnp.int32), axis=1)
    before = (jnp.arange(LIST)[:, None] < jnp.arange(LIST)[None, :]).astype(jnp.bfloat16)
    rank_near = jnp.dot(near.astype(jnp.bfloat16), before, preferred_element_type=jnp.float32)
    rank_far = jnp.dot(far.astype(jnp.bfloat16), before, preferred_element_type=jnp.float32)
    rank = jnp.where(
        near, rank_near.astype(jnp.int32), nears[:, None] + rank_far.astype(jnp.int32)
    )
    spot = jnp.arange(KEYS + CHUNK, dtype=jnp.int32)[None, :, None]
    at = here[:, None, :] & (rank[:, None, :] == spot)
    lists = jnp.sum(jnp.where(at, place[:, None, :], 0), axis=2)
    return lists, nears, jnp.sum(here.astype(jnp.int32), axis=1)


def exchange(array):
    return lax.all_to_all(array, GROUP, split_axis=0, concat_axis=0, tiled=True)


def on_device(queries, keys, values, kv_tiles, tile_count, assign):
    xi, yi = lax.axis_index("x"), lax.axis_index("y")
    lists = key_lists(kv_tiles, tile_count, xi, yi)
    spots = slot_spots(assign, xi, yi)
    by_head = jnp.transpose(queries.reshape(96, 16, HD), (1, 0, 2))
    got = exchange(spread(keys, values))
    got, by_head, spots, *lists = lax.optimization_barrier((got, by_head, spots, *lists))
    kv0 = prepare(got)
    kv1, kv3 = shift(kv0, "x", -1), shift(kv0, "x", 1)
    q0 = exchange(by_head).reshape(OWN, BLK, HD)
    k2, v2 = shift(kv3[0], "x", 1), shift(kv1[1], "x", -1)
    q0, q1, q2, q3 = around(q0, "y")
    kv = (kv0, kv1, kv3, k2, v2)
    barrier = lax.optimization_barrier
    state = attend((0,), "near", lists, (q0,), (kv0, kv1, kv3))
    q2, state = barrier((q2, state))
    o2, e2 = attend((2,), "full", lists, (q2,), kv)
    state, o2 = barrier((state, o2))
    o0, e0 = attend((0,), "far", lists, (q0,), (k2, v2), state)
    q1, o0 = barrier((q1, o0))
    o1, e1 = attend((1,), "full", lists, (q1,), kv)
    q3, o1, o2 = barrier((q3, o1, shift(o2, "y", 2)))
    o3, _, logs = attend((3,), "full", lists, (q3,), kv, logs=(e0, e1, e2))
    every = around(settle(around(logs, "y")), "x")
    o0, *every = barrier((o0, *every))
    blended = combine(e0, (o0, shift(o1, "y", 1), o2, shift(o3, "y", -1)))
    back = exchange(blended.reshape(16, 96, HD))
    attended = jnp.transpose(back, (1, 0, 2)).reshape(96, 16 * HD)
    chosen = choose(spots, every)
    turned = [(b * RING + a, a * RING + b) for a in range(RING) for b in range(RING)]
    return attended, lax.ppermute(chosen.reshape(1, OWN * BLK), ("zh", "y"), turned)


def solution(mesh):
    split = jax.sharding.Mesh(
        mesh.devices.reshape(RING, RING, RING, 2, 2), ("x", "zh", "y", "zl", "core")
    )
    tokens = P(("x", "zh", "y", "zl", "core"), None)
    return jax.shard_map(
        on_device,
        mesh=split,
        in_specs=(tokens, tokens, tokens, P(), P(), P()),
        out_specs=(tokens, P(("y", "zl", "core"), ("x", "zh"))),
        check_vma=False,
    )
```

```python
import functools

import jax
import jax.numpy as jnp
from jax import lax
from jax.experimental import pallas as pl
from jax.experimental.pallas import tpu as pltpu
from jax.sharding import PartitionSpec as P

HD = 128
BLK = 128
LIST = 96
RING = 4
OWN = 12
KEYS = RING * OWN
NEAR = 3 * OWN
CHUNK = 4
WIDTH = 4
PAD = 16
NEG = -1e30
SCALE = HD**-0.5
LOG2E = 1.4426950408889634
VMEM = pl.BlockSpec(memory_space=pltpu.VMEM)
SMEM = pl.BlockSpec(memory_space=pltpu.SMEM)
SPACE = pltpu.CompilerParams(vmem_limit_bytes=16 * 1024 * 1024)
GROUP = ("zh", "zl", "core")


def shift(array, axis, by):
    return lax.ppermute(array, axis, [(i, (i + by) % RING) for i in range(RING)])


def around(array, axis):
    return [array] + [shift(array, axis, -by) for by in range(1, RING)]


def spread_kernel(keys, values, out, sems):
    copies = [
        pltpu.make_async_copy(
            array.at[:, pl.ds(head * HD, HD)], out.at[head, which], sems.at[which, head]
        )
        for which, array in enumerate((keys, values))
        for head in range(16)
    ]
    for copy in copies:
        copy.start()
    for copy in copies:
        copy.wait()


def spread(keys, values):
    return pl.pallas_call(
        spread_kernel,
        out_shape=jax.ShapeDtypeStruct((16, 2, 96, HD), jnp.bfloat16),
        in_specs=[pl.BlockSpec(memory_space=pltpu.HBM)] * 2,
        out_specs=VMEM,
        scratch_shapes=[pltpu.SemaphoreType.DMA((2, 16))],
        compiler_params=SPACE,
        name="spread",
    )(keys, values)


def prepare_kernel(got_ref, kv_ref):
    for part in range(RING):
        k, v = (
            got_ref[4 * part : 4 * part + 4, which].reshape(3, BLK, HD) for which in range(2)
        )
        kv_ref[0, 3 * part : 3 * part + 3] = k
        for i in range(3):
            kv_ref[1, 3 * part + i] = v[i].T


def prepare(got):
    return pl.pallas_call(
        prepare_kernel,
        out_shape=jax.ShapeDtypeStruct((2, OWN, BLK, HD), jnp.bfloat16),
        in_specs=[VMEM],
        out_specs=VMEM,
        compiler_params=SPACE,
        name="prepare",
    )(got)


def split(log):
    high = log.astype(jnp.bfloat16)
    rest = log - high.astype(jnp.float32)
    middle = rest.astype(jnp.bfloat16)
    return [high, middle, (rest - middle.astype(jnp.float32)).astype(jnp.bfloat16)]


def joined(rows, block):
    parts = [rows[3 * block + i : 3 * block + i + 1] for i in range(3)]
    return parts[0] + parts[1] + parts[2]


def attend_kernel(blocks, mode, lists, nears, counts, *refs):
    count = len(blocks)
    tiles = count * OWN
    queries, refs = refs[:count], refs[count:]
    if mode != "far":
        for_near, refs = refs[:3], refs[3:]
    if mode != "near":
        (k2, v2), refs = refs[:2], refs[2:]
    if mode == "far":
        states, refs = refs[: 3 * count], refs[3 * count :]
    size = (3 if mode == "near" else 2) * count
    outs, refs = refs[:size], refs[size:]
    rows, begins, sizes, qs, ks, vs, m_ref, l_ref, acc_ref = refs[:9]
    s_refs, top_refs = refs[9 : 9 + WIDTH], refs[9 + WIDTH :]
    for b, q in enumerate(queries):
        qs[b * OWN : (b + 1) * OWN] = q[...]
    if mode != "far":
        for b, kv in enumerate(for_near):
            ks[b * OWN : (b + 1) * OWN] = kv[0]
            vs[b * OWN : (b + 1) * OWN] = kv[1]
    if mode != "near":
        at = 0 if mode == "far" else NEAR
        ks[at : at + OWN] = k2[...]
        vs[at : at + OWN] = v2[...]
    m_ref[...] = jnp.full(m_ref.shape, NEG, jnp.float32)
    l_ref[...] = jnp.zeros(l_ref.shape, jnp.float32)
    acc_ref[...] = jnp.zeros(acc_ref.shape, jnp.float32)
    if mode == "far":
        for b in range(count):
            for held, state in zip((m_ref, l_ref, acc_ref), states[3 * b : 3 * b + 3]):
                held[b * OWN : (b + 1) * OWN] = state[...]
    yi = lax.axis_index("y")
    items = jnp.int32(0)
    for b, block in enumerate(blocks):
        owner = lax.rem(yi + block, RING) * 3
        for t in range(OWN):
            row = owner + (t // 3 * OWN + t % 3)
            begin = nears[row] if mode == "far" else jnp.int32(0)
            total = (nears[row] if mode == "near" else counts[row]) - begin
            rows[b * OWN + t] = row
            begins[b * OWN + t] = begin
            sizes[b * OWN + t] = total
            items += jnp.maximum((total + CHUNK - 1) // CHUNK, 1)
    rows[tiles] = 0
    begins[tiles] = 0
    sizes[tiles] = 0

    def advance(t, j):
        more = (j + 1) * CHUNK < sizes[t]
        return jnp.where(more, t, jnp.minimum(t + 1, tiles)), jnp.where(more, j + 1, 0)

    def listed(t, j):
        row = rows[t]
        at = begins[t] + j * CHUNK
        found = [lists[row, at + u] for u in range(CHUNK)]
        if mode == "near":
            return [jnp.minimum(u, NEAR - 1) for u in found]
        return [jnp.maximum(u - NEAR, 0) for u in found] if mode == "far" else found

    def score(lane, t, j):
        left = sizes[t] - j * CHUNK
        tile = listed(t, j)
        s = lax.dot_general(
            jnp.concatenate([ks[u] for u in tile], axis=0),
            qs[jnp.minimum(t, tiles - 1)],
            (((1,), (1,)), ((), ())),
            preferred_element_type=jnp.float32,
        )
        s_refs[lane][...] = s
        top = jnp.full((8, BLK), NEG, jnp.float32)
        for u in range(CHUNK):
            part = jnp.max(s[u * BLK : (u + 1) * BLK].reshape(16, 8, BLK), axis=0)
            top = jnp.maximum(top, jnp.where(u < left, part, NEG))
        top_refs[lane][...] = jnp.max(top, axis=0, keepdims=True)

    def blend(lane, t, j):
        left = sizes[t] - j * CHUNK
        m_old = m_ref[t]
        m_new = jnp.maximum(m_old, top_refs[lane][...])
        m_ref[t] = m_new
        alpha = jnp.exp2((m_old - m_new) * (SCALE * LOG2E))
        base = m_new * (SCALE * LOG2E)
        total = jnp.zeros((8, BLK), jnp.float32)
        weights = []
        for u in range(CHUNK):
            s = s_refs[lane][u * BLK : (u + 1) * BLK] * (SCALE * LOG2E)
            w = jnp.exp2(s - jnp.where(u < left, base, -NEG))
            total = total + jnp.sum(w.reshape(16, 8, BLK), axis=0)
            weights.append(w.astype(jnp.bfloat16))
        vt = jnp.concatenate([vs[tile] for tile in listed(t, j)], axis=1)
        mixed = jnp.dot(vt, jnp.concatenate(weights, axis=0), preferred_element_type=jnp.float32)
        l_ref[t] = l_ref[t] * alpha + total
        acc_ref[t] = acc_ref[t] * alpha + mixed

    def following(t, j):
        group = []
        for _ in range(WIDTH):
            t, j = advance(t, j)
            group += [t, j]
        return tuple(group)

    start = [jnp.int32(0), jnp.int32(0)]
    for _ in range(WIDTH - 1):
        start += advance(*start[-2:])
    for lane in range(WIDTH):
        score(lane, start[2 * lane], start[2 * lane + 1])

    def step(_, now):
        later = following(*now[-2:])
        for lane in range(WIDTH):
            blend(lane, now[2 * lane], now[2 * lane + 1])
            score(lane, later[2 * lane], later[2 * lane + 1])
        return later

    lax.fori_loop(0, (items + WIDTH - 1) // WIDTH, step, tuple(start))

    if mode == "near":
        for b in range(count):
            for held, out in zip((m_ref, l_ref, acc_ref), outs[3 * b : 3 * b + 3]):
                out[...] = held[b * OWN : (b + 1) * OWN]
        return

    def finish(i, _):
        for u in range(4):
            t = i * 4 + u
            logs = {}
            for b, block in enumerate(blocks):
                total = jnp.sum(l_ref[b * OWN + t], axis=0, keepdims=True)
                some = total > 0.0
                safe = jnp.where(some, total, 1.0)
                share = jnp.where(some, 1.0 / safe, 0.0)
                outs[b][t, :HD] = (acc_ref[b * OWN + t] * share).astype(jnp.bfloat16)
                logs[block] = jnp.where(some, m_ref[b * OWN + t] * SCALE + jnp.log(safe), NEG)
                outs[count + b][pl.ds(t, 1)] = logs[block]
            none = [jnp.zeros((1, BLK), jnp.bfloat16)] * 3
            below = [row for b in range(RING) for row in (split(logs[b]) if b in logs else none)]
            below.append(jnp.zeros((PAD - 3 * RING, BLK), jnp.bfloat16))
            for b in range(count):
                outs[b][t, HD:] = jnp.concatenate(below, axis=0)
        return 0

    lax.fori_loop(0, OWN // 4, finish, 0)


def attend(blocks, mode, lists, queries, keys_values, states=()):
    count = len(blocks)
    slots = count * OWN + 1
    keys = {"near": NEAR, "far": OWN, "full": KEYS}[mode]
    pairs = count * keys * 4
    shapes = ((1, BLK), (8, BLK), (HD, BLK))
    if mode == "near":
        out_shape = [jax.ShapeDtypeStruct((OWN, *shape), jnp.float32) for shape in shapes] * count
    else:
        out_shape = [jax.ShapeDtypeStruct((OWN, HD + PAD, BLK), jnp.bfloat16)] * count
        out_shape += [jax.ShapeDtypeStruct((OWN, BLK), jnp.float32)] * count
    operands = (*queries, *keys_values, *states)
    return pl.pallas_call(
        functools.partial(attend_kernel, blocks, mode),
        out_shape=tuple(out_shape),
        in_specs=[SMEM] * 3 + [VMEM] * len(operands),
        out_specs=(VMEM,) * len(out_shape),
        scratch_shapes=[pltpu.SMEM((slots,), jnp.int32)] * 3
        + [
            pltpu.VMEM((count * OWN, BLK, HD), jnp.bfloat16),
            pltpu.VMEM((keys, BLK, HD), jnp.bfloat16),
            pltpu.VMEM((keys, HD, BLK), jnp.bfloat16),
        ]
        + [pltpu.VMEM((slots, *shape), jnp.float32) for shape in shapes]
        + [pltpu.VMEM((CHUNK * BLK, BLK), jnp.float32)] * WIDTH
        + [pltpu.VMEM((1, BLK), jnp.float32)] * WIDTH,
        compiler_params=SPACE,
        cost_estimate=pl.CostEstimate(
            flops=pairs * 4 * BLK * BLK * HD,
            bytes_accessed=5 << 20,
            transcendentals=pairs * BLK * BLK,
        ),
        name=mode,
    )(*lists, *operands)


def combine_kernel(e0, *refs):
    outs, o_ref = refs[:-1], refs[-1]
    for t in range(OWN):
        parts = [e0[t : t + 1]]
        for block in range(1, RING):
            parts.append(joined(outs[block][t, HD:].astype(jnp.float32), block))
        top = jnp.maximum(jnp.maximum(parts[0], parts[1]), jnp.maximum(parts[2], parts[3]))
        shares = [jnp.exp(part - top) for part in parts]
        total = (shares[0] + shares[1]) + (shares[2] + shares[3])
        mixed = sum(o[t, :HD].astype(jnp.float32) * (w / total) for o, w in zip(outs, shares))
        o_ref[t] = mixed.T.astype(jnp.bfloat16)


def combine(e0, outs):
    return pl.pallas_call(
        combine_kernel,
        out_shape=jax.ShapeDtypeStruct((OWN, BLK, HD), jnp.bfloat16),
        in_specs=[VMEM] * (RING + 1),
        out_specs=VMEM,
        compiler_params=SPACE,
        name="combine",
    )(e0, *outs)


def pick_kernel(spots, e0, e1, e2, e3, out, every):
    for block, log in enumerate((e0, e1, e2, e3)):
        every[block * OWN : (block + 1) * OWN] = log[...]
    every[KEYS : KEYS + 8] = jnp.full((8, BLK), NEG, jnp.float32)
    for ctx in range(RING * RING):
        for slot in range(OWN):
            out[ctx, slot : slot + 1] = every[pl.ds(spots[ctx * OWN + slot], 1)]


def pick(spots, logs):
    return pl.pallas_call(
        pick_kernel,
        out_shape=jax.ShapeDtypeStruct((RING * RING, OWN, BLK), jnp.float32),
        in_specs=[SMEM] + [VMEM] * RING,
        out_specs=VMEM,
        scratch_shapes=[pltpu.VMEM((KEYS + 8, BLK), jnp.float32)],
        compiler_params=SPACE,
        name="pick",
    )(spots, *logs)


def merge_kernel(parts, out):
    top = jnp.max(parts[...], axis=0)
    out[...] = top + jnp.log(jnp.sum(jnp.exp(parts[...] - top[None]), axis=0))


def merge(parts):
    return pl.pallas_call(
        merge_kernel,
        out_shape=jax.ShapeDtypeStruct((OWN, BLK), jnp.float32),
        in_specs=[VMEM],
        out_specs=VMEM,
        compiler_params=SPACE,
        name="merge",
    )(parts)


def slot_spots(assign, xi, yi):
    spots = (assign % OWN // 3 - yi) % RING * OWN + assign % KEYS // OWN * 3 + assign % 3
    return jnp.where(assign // KEYS == xi, spots, KEYS)


def key_lists(kv_tiles, tile_count, xi, yi):
    rows = lax.dynamic_slice_in_dim(kv_tiles, xi * KEYS, KEYS)
    used = lax.dynamic_slice_in_dim(tile_count, xi * KEYS, KEYS)
    here = (rows % OWN // 3 == yi) & (jnp.arange(LIST, dtype=jnp.int32)[None, :] < used[:, None])
    away = (rows // KEYS - xi) % RING
    block = jnp.where(away == 2, 3, jnp.minimum(away, 2))
    place = block * OWN + rows % KEYS // OWN * 3 + rows % 3
    near, far = here & (away != 2), here & (away == 2)
    nears = jnp.sum(near.astype(jnp.int32), axis=1)
    before = (jnp.arange(LIST)[:, None] < jnp.arange(LIST)[None, :]).astype(jnp.bfloat16)
    rank_near = jnp.dot(near.astype(jnp.bfloat16), before, preferred_element_type=jnp.float32)
    rank_far = jnp.dot(far.astype(jnp.bfloat16), before, preferred_element_type=jnp.float32)
    rank = jnp.where(
        near, rank_near.astype(jnp.int32), nears[:, None] + rank_far.astype(jnp.int32)
    )
    spot = jnp.arange(KEYS + CHUNK, dtype=jnp.int32)[None, :, None]
    at = here[:, None, :] & (rank[:, None, :] == spot)
    lists = jnp.sum(jnp.where(at, place[:, None, :], 0), axis=2)
    return lists, nears, jnp.sum(here.astype(jnp.int32), axis=1)


def exchange(array):
    return lax.all_to_all(array, GROUP, split_axis=0, concat_axis=0, tiled=True)


def on_device(queries, keys, values, kv_tiles, tile_count, assign):
    xi, yi = lax.axis_index("x"), lax.axis_index("y")
    lists = key_lists(kv_tiles, tile_count, xi, yi)
    spots = slot_spots(assign, xi, yi)
    by_head = jnp.transpose(queries.reshape(96, 16, HD), (1, 0, 2))
    got = exchange(spread(keys, values))
    got, by_head, spots, *lists = lax.optimization_barrier((got, by_head, spots, *lists))
    kv0 = prepare(got)
    kv1, kv3 = shift(kv0, "x", -1), shift(kv0, "x", 1)
    q0 = exchange(by_head).reshape(OWN, BLK, HD)
    k2, v2 = shift(kv3[0], "x", 1), shift(kv1[1], "x", -1)
    q0, q1, q2, q3 = around(q0, "y")
    state = attend((0,), "near", lists, (q0,), (kv0, kv1, kv3))
    o0, e0 = attend((0,), "far", lists, (q0,), (k2, v2), state)
    q2, o0 = lax.optimization_barrier((q2, o0))
    kv = (kv0, kv1, kv3, k2, v2)
    o2, e2 = attend((2,), "full", lists, (q2,), kv)
    o1, o3, e1, e3 = attend((1, 3), "full", lists, (q1, q3), kv)
    parts = lax.all_to_all(
        pick(spots, (e0, e1, e2, e3)), ("x", "y"), split_axis=0, concat_axis=0, tiled=True
    )
    o0, parts = lax.optimization_barrier((o0, parts))
    blended = combine(e0, (o0, shift(o1, "y", 1), shift(o2, "y", 2), shift(o3, "y", -1)))
    back = exchange(blended.reshape(16, 96, HD))
    attended = jnp.transpose(back, (1, 0, 2)).reshape(96, 16 * HD)
    turned = [(b * RING + a, a * RING + b) for a in range(RING) for b in range(RING)]
    return attended, lax.ppermute(merge(parts).reshape(1, OWN * BLK), ("zh", "y"), turned)


def solution(mesh):
    split = jax.sharding.Mesh(
        mesh.devices.reshape(RING, RING, RING, 2, 2), ("x", "zh", "y", "zl", "core")
    )
    tokens = P(("x", "zh", "y", "zl", "core"), None)
    return jax.shard_map(
        on_device,
        mesh=split,
        in_specs=(tokens, tokens, tokens, P(), P(), P()),
        out_specs=(tokens, P(("y", "zl", "core"), ("x", "zh"))),
        check_vma=False,
    )
```

```python
import functools

import jax
import jax.numpy as jnp
from jax import lax
from jax.experimental import pallas as pl
from jax.experimental.pallas import tpu as pltpu
from jax.sharding import PartitionSpec as P

HD = 128
BLK = 128
LIST = 96
RING = 4
OWN = 12
KEYS = RING * OWN
NEAR = 3 * OWN
CHUNK = 4
WIDTH = 4
PAD = 16
NEG = -1e30
SCALE = HD**-0.5
LOG2E = 1.4426950408889634
VMEM = pl.BlockSpec(memory_space=pltpu.VMEM)
SMEM = pl.BlockSpec(memory_space=pltpu.SMEM)
SPACE = pltpu.CompilerParams(vmem_limit_bytes=16 * 1024 * 1024)
GROUP = ("zh", "zl", "core")


def shift(array, axis, by):
    return lax.ppermute(array, axis, [(i, (i + by) % RING) for i in range(RING)])


def around(array, axis):
    return [array] + [shift(array, axis, -by) for by in range(1, RING)]


def prepare_kernel(got_ref, kv_ref):
    for part in range(RING):
        k, v = (
            got_ref[4 * part : 4 * part + 4, which].reshape(3, BLK, HD) for which in range(2)
        )
        kv_ref[0, 3 * part : 3 * part + 3] = k
        for i in range(3):
            kv_ref[1, 3 * part + i] = v[i].T


def prepare(got):
    return pl.pallas_call(
        prepare_kernel,
        out_shape=jax.ShapeDtypeStruct((2, OWN, BLK, HD), jnp.bfloat16),
        in_specs=[VMEM],
        out_specs=VMEM,
        compiler_params=SPACE,
        name="prepare",
    )(got)


def split(log):
    high = log.astype(jnp.bfloat16)
    rest = log - high.astype(jnp.float32)
    middle = rest.astype(jnp.bfloat16)
    return [high, middle, (rest - middle.astype(jnp.float32)).astype(jnp.bfloat16)]


def joined(rows, block):
    parts = [rows[3 * block + i : 3 * block + i + 1] for i in range(3)]
    return parts[0] + parts[1] + parts[2]


def attend_kernel(blocks, mode, lists, nears, counts, *refs):
    count = len(blocks)
    tiles = count * OWN
    queries, refs = refs[:count], refs[count:]
    if mode != "far":
        for_near, refs = refs[:3], refs[3:]
    if mode != "near":
        (k2, v2), refs = refs[:2], refs[2:]
    if mode == "far":
        states, refs = refs[: 3 * count], refs[3 * count :]
    size = (3 if mode == "near" else 2) * count
    outs, refs = refs[:size], refs[size:]
    rows, begins, sizes, qs, ks, vs, m_ref, l_ref, acc_ref = refs[:9]
    s_refs, top_refs = refs[9 : 9 + WIDTH], refs[9 + WIDTH :]
    for b, q in enumerate(queries):
        qs[b * OWN : (b + 1) * OWN] = q[...]
    if mode != "far":
        for b, kv in enumerate(for_near):
            ks[b * OWN : (b + 1) * OWN] = kv[0]
            vs[b * OWN : (b + 1) * OWN] = kv[1]
    if mode != "near":
        at = 0 if mode == "far" else NEAR
        ks[at : at + OWN] = k2[...]
        vs[at : at + OWN] = v2[...]
    m_ref[...] = jnp.full(m_ref.shape, NEG, jnp.float32)
    l_ref[...] = jnp.zeros(l_ref.shape, jnp.float32)
    acc_ref[...] = jnp.zeros(acc_ref.shape, jnp.float32)
    if mode == "far":
        for b in range(count):
            for held, state in zip((m_ref, l_ref, acc_ref), states[3 * b : 3 * b + 3]):
                held[b * OWN : (b + 1) * OWN] = state[...]
    yi = lax.axis_index("y")
    items = jnp.int32(0)
    for b, block in enumerate(blocks):
        owner = lax.rem(yi + block, RING) * 3
        for t in range(OWN):
            row = owner + (t // 3 * OWN + t % 3)
            begin = nears[row] if mode == "far" else jnp.int32(0)
            total = (nears[row] if mode == "near" else counts[row]) - begin
            rows[b * OWN + t] = row
            begins[b * OWN + t] = begin
            sizes[b * OWN + t] = total
            items += jnp.maximum((total + CHUNK - 1) // CHUNK, 1)
    rows[tiles] = 0
    begins[tiles] = 0
    sizes[tiles] = 0

    def advance(t, j):
        more = (j + 1) * CHUNK < sizes[t]
        return jnp.where(more, t, jnp.minimum(t + 1, tiles)), jnp.where(more, j + 1, 0)

    def listed(t, j):
        row = rows[t]
        at = begins[t] + j * CHUNK
        found = [lists[row, at + u] for u in range(CHUNK)]
        if mode == "near":
            return [jnp.minimum(u, NEAR - 1) for u in found]
        return [jnp.maximum(u - NEAR, 0) for u in found] if mode == "far" else found

    def score(lane, t, j):
        left = sizes[t] - j * CHUNK
        tile = listed(t, j)
        s = lax.dot_general(
            jnp.concatenate([ks[u] for u in tile], axis=0),
            qs[jnp.minimum(t, tiles - 1)],
            (((1,), (1,)), ((), ())),
            preferred_element_type=jnp.float32,
        )
        s_refs[lane][...] = s
        top = jnp.full((8, BLK), NEG, jnp.float32)
        for u in range(CHUNK):
            part = jnp.max(s[u * BLK : (u + 1) * BLK].reshape(16, 8, BLK), axis=0)
            top = jnp.maximum(top, jnp.where(u < left, part, NEG))
        top_refs[lane][...] = jnp.max(top, axis=0, keepdims=True)

    def blend(lane, t, j):
        left = sizes[t] - j * CHUNK
        m_old = m_ref[t]
        m_new = jnp.maximum(m_old, top_refs[lane][...])
        m_ref[t] = m_new
        alpha = jnp.exp2((m_old - m_new) * (SCALE * LOG2E))
        base = m_new * (SCALE * LOG2E)
        total = jnp.zeros((8, BLK), jnp.float32)
        weights = []
        for u in range(CHUNK):
            s = s_refs[lane][u * BLK : (u + 1) * BLK] * (SCALE * LOG2E)
            w = jnp.exp2(s - jnp.where(u < left, base, -NEG))
            total = total + jnp.sum(w.reshape(16, 8, BLK), axis=0)
            weights.append(w.astype(jnp.bfloat16))
        vt = jnp.concatenate([vs[tile] for tile in listed(t, j)], axis=1)
        mixed = jnp.dot(vt, jnp.concatenate(weights, axis=0), preferred_element_type=jnp.float32)
        l_ref[t] = l_ref[t] * alpha + total
        acc_ref[t] = acc_ref[t] * alpha + mixed

    def following(t, j):
        group = []
        for _ in range(WIDTH):
            t, j = advance(t, j)
            group += [t, j]
        return tuple(group)

    start = [jnp.int32(0), jnp.int32(0)]
    for _ in range(WIDTH - 1):
        start += advance(*start[-2:])
    for lane in range(WIDTH):
        score(lane, start[2 * lane], start[2 * lane + 1])

    def step(_, now):
        later = following(*now[-2:])
        for lane in range(WIDTH):
            blend(lane, now[2 * lane], now[2 * lane + 1])
            score(lane, later[2 * lane], later[2 * lane + 1])
        return later

    lax.fori_loop(0, (items + WIDTH - 1) // WIDTH, step, tuple(start))

    if mode == "near":
        for b in range(count):
            for held, out in zip((m_ref, l_ref, acc_ref), outs[3 * b : 3 * b + 3]):
                out[...] = held[b * OWN : (b + 1) * OWN]
        return

    def finish(i, _):
        for u in range(4):
            t = i * 4 + u
            logs = {}
            for b, block in enumerate(blocks):
                total = jnp.sum(l_ref[b * OWN + t], axis=0, keepdims=True)
                some = total > 0.0
                safe = jnp.where(some, total, 1.0)
                share = jnp.where(some, 1.0 / safe, 0.0)
                outs[b][t, :HD] = (acc_ref[b * OWN + t] * share).astype(jnp.bfloat16)
                logs[block] = jnp.where(some, m_ref[b * OWN + t] * SCALE + jnp.log(safe), NEG)
                outs[count + b][pl.ds(t, 1)] = logs[block]
            none = [jnp.zeros((1, BLK), jnp.bfloat16)] * 3
            below = [row for b in range(RING) for row in (split(logs[b]) if b in logs else none)]
            below.append(jnp.zeros((PAD - 3 * RING, BLK), jnp.bfloat16))
            for b in range(count):
                outs[b][t, HD:] = jnp.concatenate(below, axis=0)
        return 0

    lax.fori_loop(0, OWN // 4, finish, 0)


def attend(blocks, mode, lists, queries, keys_values, states=()):
    count = len(blocks)
    slots = count * OWN + 1
    keys = {"near": NEAR, "far": OWN, "full": KEYS}[mode]
    pairs = count * keys * 4
    shapes = ((1, BLK), (8, BLK), (HD, BLK))
    if mode == "near":
        out_shape = [jax.ShapeDtypeStruct((OWN, *shape), jnp.float32) for shape in shapes] * count
    else:
        out_shape = [jax.ShapeDtypeStruct((OWN, HD + PAD, BLK), jnp.bfloat16)] * count
        out_shape += [jax.ShapeDtypeStruct((OWN, BLK), jnp.float32)] * count
    operands = (*queries, *keys_values, *states)
    return pl.pallas_call(
        functools.partial(attend_kernel, blocks, mode),
        out_shape=tuple(out_shape),
        in_specs=[SMEM] * 3 + [VMEM] * len(operands),
        out_specs=(VMEM,) * len(out_shape),
        scratch_shapes=[pltpu.SMEM((slots,), jnp.int32)] * 3
        + [
            pltpu.VMEM((count * OWN, BLK, HD), jnp.bfloat16),
            pltpu.VMEM((keys, BLK, HD), jnp.bfloat16),
            pltpu.VMEM((keys, HD, BLK), jnp.bfloat16),
        ]
        + [pltpu.VMEM((slots, *shape), jnp.float32) for shape in shapes]
        + [pltpu.VMEM((CHUNK * BLK, BLK), jnp.float32)] * WIDTH
        + [pltpu.VMEM((1, BLK), jnp.float32)] * WIDTH,
        compiler_params=SPACE,
        cost_estimate=pl.CostEstimate(
            flops=pairs * 4 * BLK * BLK * HD,
            bytes_accessed=5 << 20,
            transcendentals=pairs * BLK * BLK,
        ),
        name=mode,
    )(*lists, *operands)


def combine_kernel(e0, *refs):
    outs, o_ref = refs[:-1], refs[-1]
    for t in range(OWN):
        parts = [e0[t : t + 1]]
        for block in range(1, RING):
            parts.append(joined(outs[block][t, HD:].astype(jnp.float32), block))
        top = jnp.maximum(jnp.maximum(parts[0], parts[1]), jnp.maximum(parts[2], parts[3]))
        shares = [jnp.exp(part - top) for part in parts]
        total = (shares[0] + shares[1]) + (shares[2] + shares[3])
        mixed = sum(o[t, :HD].astype(jnp.float32) * (w / total) for o, w in zip(outs, shares))
        o_ref[t] = mixed.T.astype(jnp.bfloat16)


def combine(e0, outs):
    return pl.pallas_call(
        combine_kernel,
        out_shape=jax.ShapeDtypeStruct((OWN, BLK, HD), jnp.bfloat16),
        in_specs=[VMEM] * (RING + 1),
        out_specs=VMEM,
        compiler_params=SPACE,
        name="combine",
    )(e0, *outs)


def pick_kernel(spots, e0, e1, e2, e3, out, every):
    for block, log in enumerate((e0, e1, e2, e3)):
        every[block * OWN : (block + 1) * OWN] = log[...]
    every[KEYS : KEYS + 8] = jnp.full((8, BLK), NEG, jnp.float32)
    for ctx in range(RING * RING):
        for slot in range(OWN):
            out[ctx, slot : slot + 1] = every[pl.ds(spots[ctx * OWN + slot], 1)]


def pick(spots, logs):
    return pl.pallas_call(
        pick_kernel,
        out_shape=jax.ShapeDtypeStruct((RING * RING, OWN, BLK), jnp.float32),
        in_specs=[SMEM] + [VMEM] * RING,
        out_specs=VMEM,
        scratch_shapes=[pltpu.VMEM((KEYS + 8, BLK), jnp.float32)],
        compiler_params=SPACE,
        name="pick",
    )(spots, *logs)


def merge_kernel(parts, out):
    top = jnp.max(parts[...], axis=0)
    out[...] = top + jnp.log(jnp.sum(jnp.exp(parts[...] - top[None]), axis=0))


def merge(parts):
    return pl.pallas_call(
        merge_kernel,
        out_shape=jax.ShapeDtypeStruct((OWN, BLK), jnp.float32),
        in_specs=[VMEM],
        out_specs=VMEM,
        compiler_params=SPACE,
        name="merge",
    )(parts)


def slot_spots(assign, xi, yi):
    spots = (assign % OWN // 3 - yi) % RING * OWN + assign % KEYS // OWN * 3 + assign % 3
    return jnp.where(assign // KEYS == xi, spots, KEYS)


def key_lists(kv_tiles, tile_count, xi, yi):
    rows = lax.dynamic_slice_in_dim(kv_tiles, xi * KEYS, KEYS)
    used = lax.dynamic_slice_in_dim(tile_count, xi * KEYS, KEYS)
    here = (rows % OWN // 3 == yi) & (jnp.arange(LIST, dtype=jnp.int32)[None, :] < used[:, None])
    away = (rows // KEYS - xi) % RING
    block = jnp.where(away == 2, 3, jnp.minimum(away, 2))
    place = block * OWN + rows % KEYS // OWN * 3 + rows % 3
    near, far = here & (away != 2), here & (away == 2)
    nears = jnp.sum(near.astype(jnp.int32), axis=1)
    before = (jnp.arange(LIST)[:, None] < jnp.arange(LIST)[None, :]).astype(jnp.bfloat16)
    rank_near = jnp.dot(near.astype(jnp.bfloat16), before, preferred_element_type=jnp.float32)
    rank_far = jnp.dot(far.astype(jnp.bfloat16), before, preferred_element_type=jnp.float32)
    rank = jnp.where(
        near, rank_near.astype(jnp.int32), nears[:, None] + rank_far.astype(jnp.int32)
    )
    spot = jnp.arange(KEYS + CHUNK, dtype=jnp.int32)[None, :, None]
    at = here[:, None, :] & (rank[:, None, :] == spot)
    lists = jnp.sum(jnp.where(at, place[:, None, :], 0), axis=2)
    return lists, nears, jnp.sum(here.astype(jnp.int32), axis=1)


def exchange(array):
    return lax.all_to_all(array, GROUP, split_axis=0, concat_axis=0, tiled=True)


def on_device(queries, keys, values, kv_tiles, tile_count, assign):
    xi, yi = lax.axis_index("x"), lax.axis_index("y")
    lists = key_lists(kv_tiles, tile_count, xi, yi)
    spots = slot_spots(assign, xi, yi)
    by_head = jnp.transpose(queries.reshape(96, 16, HD), (1, 0, 2))
    sent = jnp.stack([a.reshape(96, 16, HD) for a in (keys, values)])
    got = exchange(jnp.transpose(sent, (2, 0, 1, 3)))
    got, by_head, spots, *lists = lax.optimization_barrier((got, by_head, spots, *lists))
    kv0 = prepare(got)
    kv1, kv3 = shift(kv0, "x", -1), shift(kv0, "x", 1)
    q0 = exchange(by_head).reshape(OWN, BLK, HD)
    k2, v2 = shift(kv3[0], "x", 1), shift(kv1[1], "x", -1)
    q0, q1, q2, q3 = around(q0, "y")
    state = attend((0,), "near", lists, (q0,), (kv0, kv1, kv3))
    o0, e0 = attend((0,), "far", lists, (q0,), (k2, v2), state)
    q2, o0 = lax.optimization_barrier((q2, o0))
    kv = (kv0, kv1, kv3, k2, v2)
    o2, e2 = attend((2,), "full", lists, (q2,), kv)
    q1, o2 = lax.optimization_barrier((q1, o2))
    o2 = shift(o2, "y", 2)
    o1, o3, e1, e3 = attend((1, 3), "full", lists, (q1, q3), kv)
    e1, o2 = lax.optimization_barrier((e1, o2))
    parts = lax.all_to_all(
        pick(spots, (e0, e1, e2, e3)), ("x", "y"), split_axis=0, concat_axis=0, tiled=True
    )
    o0, parts = lax.optimization_barrier((o0, parts))
    blended = combine(e0, (o0, shift(o1, "y", 1), o2, shift(o3, "y", -1)))
    back = exchange(blended.reshape(16, 96, HD))
    attended = jnp.transpose(back, (1, 0, 2)).reshape(96, 16 * HD)
    turned = [(b * RING + a, a * RING + b) for a in range(RING) for b in range(RING)]
    return attended, lax.ppermute(merge(parts).reshape(1, OWN * BLK), ("zh", "y"), turned)


def solution(mesh):
    split = jax.sharding.Mesh(
        mesh.devices.reshape(RING, RING, RING, 2, 2), ("x", "zh", "y", "zl", "core")
    )
    tokens = P(("x", "zh", "y", "zl", "core"), None)
    return jax.shard_map(
        on_device,
        mesh=split,
        in_specs=(tokens, tokens, tokens, P(), P(), P()),
        out_specs=(tokens, P(("y", "zl", "core"), ("x", "zh"))),
        check_vma=False,
    )
```

```python
import functools

import jax
import jax.numpy as jnp
from jax import lax
from jax.experimental import pallas as pl
from jax.experimental.pallas import tpu as pltpu
from jax.sharding import PartitionSpec as P

HD = 128
BLK = 128
LIST = 96
RING = 4
OWN = 12
KEYS = RING * OWN
NEAR = 3 * OWN
CHUNK = 4
WIDTH = 4
PAD = 16
NEG = -1e30
SCALE = HD**-0.5
LOG2E = 1.4426950408889634
VMEM = pl.BlockSpec(memory_space=pltpu.VMEM)
SMEM = pl.BlockSpec(memory_space=pltpu.SMEM)
SPACE = pltpu.CompilerParams(vmem_limit_bytes=16 * 1024 * 1024)
GROUP = ("zh", "zl", "core")


def shift(array, axis, by):
    return lax.ppermute(array, axis, [(i, (i + by) % RING) for i in range(RING)])


def around(array, axis):
    return [array] + [shift(array, axis, -by) for by in range(1, RING)]


def prepare_kernel(got_ref, k_ref, vt_ref):
    for part in range(RING):
        k, v = (
            got_ref[4 * part : 4 * part + 4, which].reshape(3, BLK, HD) for which in range(2)
        )
        k_ref[3 * part : 3 * part + 3] = k
        for i in range(3):
            vt_ref[3 * part + i] = v[i].T


def prepare(got):
    return pl.pallas_call(
        prepare_kernel,
        out_shape=(jax.ShapeDtypeStruct((OWN, BLK, HD), jnp.bfloat16),) * 2,
        in_specs=[VMEM],
        out_specs=(VMEM, VMEM),
        compiler_params=SPACE,
        name="prepare",
    )(got)


def split(log):
    high = log.astype(jnp.bfloat16)
    rest = log - high.astype(jnp.float32)
    middle = rest.astype(jnp.bfloat16)
    return [high, middle, (rest - middle.astype(jnp.float32)).astype(jnp.bfloat16)]


def joined(rows, block):
    parts = [rows[3 * block + i : 3 * block + i + 1] for i in range(3)]
    return parts[0] + parts[1] + parts[2]


def attend_kernel(blocks, mode, lists, nears, counts, *refs):
    count = len(blocks)
    tiles = count * OWN
    queries, refs = refs[:count], refs[count:]
    if mode != "far":
        for_near, refs = refs[:6], refs[6:]
    if mode != "near":
        (k2, v2), refs = refs[:2], refs[2:]
    if mode == "far":
        states, refs = refs[: 3 * count], refs[3 * count :]
    size = (3 if mode == "near" else 2) * count
    outs, refs = refs[:size], refs[size:]
    rows, begins, sizes, qs, ks, vs, m_ref, l_ref, acc_ref = refs[:9]
    s_refs, top_refs = refs[9 : 9 + WIDTH], refs[9 + WIDTH :]
    for b, q in enumerate(queries):
        qs[b * OWN : (b + 1) * OWN] = q[...]
    if mode != "far":
        for b in range(3):
            ks[b * OWN : (b + 1) * OWN] = for_near[2 * b][...]
            vs[b * OWN : (b + 1) * OWN] = for_near[2 * b + 1][...]
    if mode != "near":
        at = 0 if mode == "far" else NEAR
        ks[at : at + OWN] = k2[...]
        vs[at : at + OWN] = v2[...]
    m_ref[...] = jnp.full(m_ref.shape, NEG, jnp.float32)
    l_ref[...] = jnp.zeros(l_ref.shape, jnp.float32)
    acc_ref[...] = jnp.zeros(acc_ref.shape, jnp.float32)
    if mode == "far":
        for b in range(count):
            for held, state in zip((m_ref, l_ref, acc_ref), states[3 * b : 3 * b + 3]):
                held[b * OWN : (b + 1) * OWN] = state[...]
    yi = lax.axis_index("y")
    items = jnp.int32(0)
    for b, block in enumerate(blocks):
        owner = lax.rem(yi + block, RING) * 3
        for t in range(OWN):
            row = owner + (t // 3 * OWN + t % 3)
            begin = nears[row] if mode == "far" else jnp.int32(0)
            total = (nears[row] if mode == "near" else counts[row]) - begin
            rows[b * OWN + t] = row
            begins[b * OWN + t] = begin
            sizes[b * OWN + t] = total
            items += jnp.maximum((total + CHUNK - 1) // CHUNK, 1)
    rows[tiles] = 0
    begins[tiles] = 0
    sizes[tiles] = 0

    def advance(t, j):
        more = (j + 1) * CHUNK < sizes[t]
        return jnp.where(more, t, jnp.minimum(t + 1, tiles)), jnp.where(more, j + 1, 0)

    def listed(t, j):
        row = rows[t]
        at = begins[t] + j * CHUNK
        found = [lists[row, at + u] for u in range(CHUNK)]
        if mode == "near":
            return [jnp.minimum(u, NEAR - 1) for u in found]
        return [jnp.maximum(u - NEAR, 0) for u in found] if mode == "far" else found

    def score(lane, t, j):
        left = sizes[t] - j * CHUNK
        tile = listed(t, j)
        s = lax.dot_general(
            jnp.concatenate([ks[u] for u in tile], axis=0),
            qs[jnp.minimum(t, tiles - 1)],
            (((1,), (1,)), ((), ())),
            preferred_element_type=jnp.float32,
        )
        s_refs[lane][...] = s
        top = jnp.full((8, BLK), NEG, jnp.float32)
        for u in range(CHUNK):
            part = jnp.max(s[u * BLK : (u + 1) * BLK].reshape(16, 8, BLK), axis=0)
            top = jnp.maximum(top, jnp.where(u < left, part, NEG))
        top_refs[lane][...] = jnp.max(top, axis=0, keepdims=True)

    def blend(lane, t, j):
        left = sizes[t] - j * CHUNK
        m_old = m_ref[t]
        m_new = jnp.maximum(m_old, top_refs[lane][...])
        m_ref[t] = m_new
        alpha = jnp.exp2((m_old - m_new) * (SCALE * LOG2E))
        base = m_new * (SCALE * LOG2E)
        total = jnp.zeros((8, BLK), jnp.float32)
        weights = []
        for u in range(CHUNK):
            s = s_refs[lane][u * BLK : (u + 1) * BLK] * (SCALE * LOG2E)
            w = jnp.exp2(s - jnp.where(u < left, base, -NEG))
            total = total + jnp.sum(w.reshape(16, 8, BLK), axis=0)
            weights.append(w.astype(jnp.bfloat16))
        vt = jnp.concatenate([vs[tile] for tile in listed(t, j)], axis=1)
        mixed = jnp.dot(vt, jnp.concatenate(weights, axis=0), preferred_element_type=jnp.float32)
        l_ref[t] = l_ref[t] * alpha + total
        acc_ref[t] = acc_ref[t] * alpha + mixed

    def following(t, j):
        group = []
        for _ in range(WIDTH):
            t, j = advance(t, j)
            group += [t, j]
        return tuple(group)

    start = [jnp.int32(0), jnp.int32(0)]
    for _ in range(WIDTH - 1):
        start += advance(*start[-2:])
    for lane in range(WIDTH):
        score(lane, start[2 * lane], start[2 * lane + 1])

    def step(_, now):
        later = following(*now[-2:])
        for lane in range(WIDTH):
            blend(lane, now[2 * lane], now[2 * lane + 1])
            score(lane, later[2 * lane], later[2 * lane + 1])
        return later

    lax.fori_loop(0, (items + WIDTH - 1) // WIDTH, step, tuple(start))

    if mode == "near":
        for b in range(count):
            for held, out in zip((m_ref, l_ref, acc_ref), outs[3 * b : 3 * b + 3]):
                out[...] = held[b * OWN : (b + 1) * OWN]
        return

    def finish(i, _):
        for u in range(4):
            t = i * 4 + u
            logs = {}
            for b, block in enumerate(blocks):
                total = jnp.sum(l_ref[b * OWN + t], axis=0, keepdims=True)
                some = total > 0.0
                safe = jnp.where(some, total, 1.0)
                share = jnp.where(some, 1.0 / safe, 0.0)
                outs[b][t, :HD] = (acc_ref[b * OWN + t] * share).astype(jnp.bfloat16)
                logs[block] = jnp.where(some, m_ref[b * OWN + t] * SCALE + jnp.log(safe), NEG)
                outs[count + b][pl.ds(t, 1)] = logs[block]
            none = [jnp.zeros((1, BLK), jnp.bfloat16)] * 3
            below = [row for b in range(RING) for row in (split(logs[b]) if b in logs else none)]
            below.append(jnp.zeros((PAD - 3 * RING, BLK), jnp.bfloat16))
            for b in range(count):
                outs[b][t, HD:] = jnp.concatenate(below, axis=0)
        return 0

    lax.fori_loop(0, OWN // 4, finish, 0)


def attend(blocks, mode, lists, queries, keys_values, states=()):
    count = len(blocks)
    slots = count * OWN + 1
    keys = {"near": NEAR, "far": OWN, "full": KEYS}[mode]
    pairs = count * keys * 4
    shapes = ((1, BLK), (8, BLK), (HD, BLK))
    if mode == "near":
        out_shape = [jax.ShapeDtypeStruct((OWN, *shape), jnp.float32) for shape in shapes] * count
    else:
        out_shape = [jax.ShapeDtypeStruct((OWN, HD + PAD, BLK), jnp.bfloat16)] * count
        out_shape += [jax.ShapeDtypeStruct((OWN, BLK), jnp.float32)] * count
    operands = (*queries, *keys_values, *states)
    return pl.pallas_call(
        functools.partial(attend_kernel, blocks, mode),
        out_shape=tuple(out_shape),
        in_specs=[SMEM] * 3 + [VMEM] * len(operands),
        out_specs=(VMEM,) * len(out_shape),
        scratch_shapes=[pltpu.SMEM((slots,), jnp.int32)] * 3
        + [
            pltpu.VMEM((count * OWN, BLK, HD), jnp.bfloat16),
            pltpu.VMEM((keys, BLK, HD), jnp.bfloat16),
            pltpu.VMEM((keys, HD, BLK), jnp.bfloat16),
        ]
        + [pltpu.VMEM((slots, *shape), jnp.float32) for shape in shapes]
        + [pltpu.VMEM((CHUNK * BLK, BLK), jnp.float32)] * WIDTH
        + [pltpu.VMEM((1, BLK), jnp.float32)] * WIDTH,
        compiler_params=SPACE,
        cost_estimate=pl.CostEstimate(
            flops=pairs * 4 * BLK * BLK * HD,
            bytes_accessed=5 << 20,
            transcendentals=pairs * BLK * BLK,
        ),
        name=mode,
    )(*lists, *operands)


def combine_kernel(e0, *refs):
    outs, o_ref = refs[:-1], refs[-1]
    for t in range(OWN):
        parts = [e0[t : t + 1]]
        for block in range(1, RING):
            parts.append(joined(outs[block][t, HD:].astype(jnp.float32), block))
        top = jnp.maximum(jnp.maximum(parts[0], parts[1]), jnp.maximum(parts[2], parts[3]))
        shares = [jnp.exp(part - top) for part in parts]
        total = (shares[0] + shares[1]) + (shares[2] + shares[3])
        mixed = sum(o[t, :HD].astype(jnp.float32) * (w / total) for o, w in zip(outs, shares))
        o_ref[t] = mixed.T.astype(jnp.bfloat16)


def combine(e0, outs):
    return pl.pallas_call(
        combine_kernel,
        out_shape=jax.ShapeDtypeStruct((OWN, BLK, HD), jnp.bfloat16),
        in_specs=[VMEM] * (RING + 1),
        out_specs=VMEM,
        compiler_params=SPACE,
        name="combine",
    )(e0, *outs)


def pick_kernel(spots, e0, e1, e2, e3, out, every):
    for block, log in enumerate((e0, e1, e2, e3)):
        every[block * OWN : (block + 1) * OWN] = log[...]
    every[KEYS : KEYS + 8] = jnp.full((8, BLK), NEG, jnp.float32)
    for ctx in range(RING * RING):
        for slot in range(OWN):
            out[ctx, slot : slot + 1] = every[pl.ds(spots[ctx * OWN + slot], 1)]


def pick(spots, logs):
    return pl.pallas_call(
        pick_kernel,
        out_shape=jax.ShapeDtypeStruct((RING * RING, OWN, BLK), jnp.float32),
        in_specs=[SMEM] + [VMEM] * RING,
        out_specs=VMEM,
        scratch_shapes=[pltpu.VMEM((KEYS + 8, BLK), jnp.float32)],
        compiler_params=SPACE,
        name="pick",
    )(spots, *logs)


def merge_kernel(parts, out):
    top = jnp.max(parts[...], axis=0)
    out[...] = top + jnp.log(jnp.sum(jnp.exp(parts[...] - top[None]), axis=0))


def merge(parts):
    return pl.pallas_call(
        merge_kernel,
        out_shape=jax.ShapeDtypeStruct((OWN, BLK), jnp.float32),
        in_specs=[VMEM],
        out_specs=VMEM,
        compiler_params=SPACE,
        name="merge",
    )(parts)


def slot_spots(assign, xi, yi):
    spots = (assign % OWN // 3 - yi) % RING * OWN + assign % KEYS // OWN * 3 + assign % 3
    return jnp.where(assign // KEYS == xi, spots, KEYS)


def key_lists(kv_tiles, tile_count, xi, yi):
    rows = lax.dynamic_slice_in_dim(kv_tiles, xi * KEYS, KEYS)
    used = lax.dynamic_slice_in_dim(tile_count, xi * KEYS, KEYS)
    here = (rows % OWN // 3 == yi) & (jnp.arange(LIST, dtype=jnp.int32)[None, :] < used[:, None])
    away = (rows // KEYS - xi) % RING
    block = jnp.where(away == 2, 3, jnp.minimum(away, 2))
    place = block * OWN + rows % KEYS // OWN * 3 + rows % 3
    near, far = here & (away != 2), here & (away == 2)
    nears = jnp.sum(near.astype(jnp.int32), axis=1)
    before = (jnp.arange(LIST)[:, None] < jnp.arange(LIST)[None, :]).astype(jnp.bfloat16)
    rank_near = jnp.dot(near.astype(jnp.bfloat16), before, preferred_element_type=jnp.float32)
    rank_far = jnp.dot(far.astype(jnp.bfloat16), before, preferred_element_type=jnp.float32)
    rank = jnp.where(
        near, rank_near.astype(jnp.int32), nears[:, None] + rank_far.astype(jnp.int32)
    )
    spot = jnp.arange(KEYS + CHUNK, dtype=jnp.int32)[None, :, None]
    at = here[:, None, :] & (rank[:, None, :] == spot)
    lists = jnp.sum(jnp.where(at, place[:, None, :], 0), axis=2)
    return lists, nears, jnp.sum(here.astype(jnp.int32), axis=1)


def exchange(array):
    return lax.all_to_all(array, GROUP, split_axis=0, concat_axis=0, tiled=True)


def on_device(queries, keys, values, kv_tiles, tile_count, assign):
    xi, yi = lax.axis_index("x"), lax.axis_index("y")
    lists = key_lists(kv_tiles, tile_count, xi, yi)
    spots = slot_spots(assign, xi, yi)
    by_head = jnp.transpose(queries.reshape(96, 16, HD), (1, 0, 2))
    sent = jnp.stack([a.reshape(96, 16, HD) for a in (keys, values)])
    got = exchange(jnp.transpose(sent, (2, 0, 1, 3)))
    got, by_head, spots, *lists = lax.optimization_barrier((got, by_head, spots, *lists))
    k0, v0 = prepare(got)
    k3, v1 = shift(k0, "x", 1), shift(v0, "x", -1)
    k1, v3 = shift(k0, "x", -1), shift(v0, "x", 1)
    q0 = exchange(by_head).reshape(OWN, BLK, HD)
    k2, v2 = shift(k3, "x", 1), shift(v1, "x", -1)
    q0, q1, q2, q3 = around(q0, "y")
    near = (k0, v0, k1, v1, k3, v3)
    state = attend((0,), "near", lists, (q0,), near)
    o0, e0 = attend((0,), "far", lists, (q0,), (k2, v2), state)
    q2, o0 = lax.optimization_barrier((q2, o0))
    kv = (*near, k2, v2)
    o2, e2 = attend((2,), "full", lists, (q2,), kv)
    q1, o2 = lax.optimization_barrier((q1, o2))
    o2 = shift(o2, "y", 2)
    o1, o3, e1, e3 = attend((1, 3), "full", lists, (q1, q3), kv)
    e1, o2 = lax.optimization_barrier((e1, o2))
    parts = lax.all_to_all(
        pick(spots, (e0, e1, e2, e3)), ("x", "y"), split_axis=0, concat_axis=0, tiled=True
    )
    o0, parts = lax.optimization_barrier((o0, parts))
    blended = combine(e0, (o0, shift(o1, "y", 1), o2, shift(o3, "y", -1)))
    back = exchange(blended.reshape(16, 96, HD))
    attended = jnp.transpose(back, (1, 0, 2)).reshape(96, 16 * HD)
    turned = [(b * RING + a, a * RING + b) for a in range(RING) for b in range(RING)]
    return attended, lax.ppermute(merge(parts).reshape(1, OWN * BLK), ("zh", "y"), turned)


def solution(mesh):
    split = jax.sharding.Mesh(
        mesh.devices.reshape(RING, RING, RING, 2, 2), ("x", "zh", "y", "zl", "core")
    )
    tokens = P(("x", "zh", "y", "zl", "core"), None)
    return jax.shard_map(
        on_device,
        mesh=split,
        in_specs=(tokens, tokens, tokens, P(), P(), P()),
        out_specs=(tokens, P(("y", "zl", "core"), ("x", "zh"))),
        check_vma=False,
    )
```

```python
import functools

import jax
import jax.numpy as jnp
from jax import lax
from jax.experimental import pallas as pl
from jax.experimental.pallas import tpu as pltpu
from jax.sharding import PartitionSpec as P

HD = 128
BLK = 128
LIST = 96
RING = 4
OWN = 12
KEYS = RING * OWN
NEAR = 3 * OWN
CHUNK = 4
WIDTH = 8
PAD = 16
NEG = -1e30
SCALE = HD**-0.5
LOG2E = 1.4426950408889634
VMEM = pl.BlockSpec(memory_space=pltpu.VMEM)
SMEM = pl.BlockSpec(memory_space=pltpu.SMEM)
SPACE = pltpu.CompilerParams(vmem_limit_bytes=16 * 1024 * 1024)
GROUP = ("zh", "zl", "core")


def shift(array, axis, by):
    return lax.ppermute(array, axis, [(i, (i + by) % RING) for i in range(RING)])


def around(array, axis):
    return [array] + [shift(array, axis, -by) for by in range(1, RING)]


def prepare_kernel(got_ref, kv_ref):
    for part in range(RING):
        k, v = (
            got_ref[4 * part : 4 * part + 4, which].reshape(3, BLK, HD) for which in range(2)
        )
        kv_ref[0, 3 * part : 3 * part + 3] = k
        for i in range(3):
            kv_ref[1, 3 * part + i] = v[i].T


def prepare(got):
    return pl.pallas_call(
        prepare_kernel,
        out_shape=jax.ShapeDtypeStruct((2, OWN, BLK, HD), jnp.bfloat16),
        in_specs=[VMEM],
        out_specs=VMEM,
        compiler_params=SPACE,
        name="prepare",
    )(got)


def split(log):
    high = log.astype(jnp.bfloat16)
    rest = log - high.astype(jnp.float32)
    middle = rest.astype(jnp.bfloat16)
    return [high, middle, (rest - middle.astype(jnp.float32)).astype(jnp.bfloat16)]


def joined(rows, block):
    parts = [rows[3 * block + i : 3 * block + i + 1] for i in range(3)]
    return parts[0] + parts[1] + parts[2]


def attend_kernel(blocks, mode, lists, nears, counts, *refs):
    count = len(blocks)
    tiles = count * OWN
    queries, refs = refs[:count], refs[count:]
    if mode != "far":
        for_near, refs = refs[:3], refs[3:]
    if mode != "near":
        (k2, v2), refs = refs[:2], refs[2:]
    if mode == "far":
        states, refs = refs[: 3 * count], refs[3 * count :]
    size = (3 if mode == "near" else 2) * count
    outs, refs = refs[:size], refs[size:]
    rows, begins, sizes, qs, ks, vs, m_ref, l_ref, acc_ref = refs[:9]
    s_refs, top_refs = refs[9 : 9 + WIDTH], refs[9 + WIDTH :]
    for b, q in enumerate(queries):
        qs[b * OWN : (b + 1) * OWN] = q[...]
    if mode != "far":
        for b, kv in enumerate(for_near):
            ks[b * OWN : (b + 1) * OWN] = kv[0]
            vs[b * OWN : (b + 1) * OWN] = kv[1]
    if mode != "near":
        at = 0 if mode == "far" else NEAR
        ks[at : at + OWN] = k2[...]
        vs[at : at + OWN] = v2[...]
    m_ref[...] = jnp.full(m_ref.shape, NEG, jnp.float32)
    l_ref[...] = jnp.zeros(l_ref.shape, jnp.float32)
    acc_ref[...] = jnp.zeros(acc_ref.shape, jnp.float32)
    if mode == "far":
        for b in range(count):
            for held, state in zip((m_ref, l_ref, acc_ref), states[3 * b : 3 * b + 3]):
                held[b * OWN : (b + 1) * OWN] = state[...]
    yi = lax.axis_index("y")
    items = jnp.int32(0)
    for b, block in enumerate(blocks):
        owner = lax.rem(yi + block, RING) * 3
        for t in range(OWN):
            row = owner + (t // 3 * OWN + t % 3)
            begin = nears[row] if mode == "far" else jnp.int32(0)
            total = (nears[row] if mode == "near" else counts[row]) - begin
            rows[b * OWN + t] = row
            begins[b * OWN + t] = begin
            sizes[b * OWN + t] = total
            items += jnp.maximum((total + CHUNK - 1) // CHUNK, 1)
    rows[tiles] = 0
    begins[tiles] = 0
    sizes[tiles] = 0

    def advance(t, j):
        more = (j + 1) * CHUNK < sizes[t]
        return jnp.where(more, t, jnp.minimum(t + 1, tiles)), jnp.where(more, j + 1, 0)

    def listed(t, j):
        row = rows[t]
        at = begins[t] + j * CHUNK
        found = [lists[row, at + u] for u in range(CHUNK)]
        if mode == "near":
            return [jnp.minimum(u, NEAR - 1) for u in found]
        return [jnp.maximum(u - NEAR, 0) for u in found] if mode == "far" else found

    def score(lane, t, j):
        left = sizes[t] - j * CHUNK
        tile = listed(t, j)
        s = lax.dot_general(
            jnp.concatenate([ks[u] for u in tile], axis=0),
            qs[jnp.minimum(t, tiles - 1)],
            (((1,), (1,)), ((), ())),
            preferred_element_type=jnp.float32,
        )
        s_refs[lane][...] = s
        top = jnp.full((8, BLK), NEG, jnp.float32)
        for u in range(CHUNK):
            part = jnp.max(s[u * BLK : (u + 1) * BLK].reshape(16, 8, BLK), axis=0)
            top = jnp.maximum(top, jnp.where(u < left, part, NEG))
        top_refs[lane][...] = jnp.max(top, axis=0, keepdims=True)

    def blend(lane, t, j):
        left = sizes[t] - j * CHUNK
        m_old = m_ref[t]
        m_new = jnp.maximum(m_old, top_refs[lane][...])
        m_ref[t] = m_new
        alpha = jnp.exp2((m_old - m_new) * (SCALE * LOG2E))
        base = m_new * (SCALE * LOG2E)
        total = jnp.zeros((8, BLK), jnp.float32)
        weights = []
        for u in range(CHUNK):
            s = s_refs[lane][u * BLK : (u + 1) * BLK] * (SCALE * LOG2E)
            w = jnp.exp2(s - jnp.where(u < left, base, -NEG))
            total = total + jnp.sum(w.reshape(16, 8, BLK), axis=0)
            weights.append(w.astype(jnp.bfloat16))
        vt = jnp.concatenate([vs[tile] for tile in listed(t, j)], axis=1)
        mixed = jnp.dot(vt, jnp.concatenate(weights, axis=0), preferred_element_type=jnp.float32)
        l_ref[t] = l_ref[t] * alpha + total
        acc_ref[t] = acc_ref[t] * alpha + mixed

    def following(t, j):
        group = []
        for _ in range(WIDTH):
            t, j = advance(t, j)
            group += [t, j]
        return tuple(group)

    start = [jnp.int32(0), jnp.int32(0)]
    for _ in range(WIDTH - 1):
        start += advance(*start[-2:])
    for lane in range(WIDTH):
        score(lane, start[2 * lane], start[2 * lane + 1])

    def step(_, now):
        later = following(*now[-2:])
        for lane in range(WIDTH):
            blend(lane, now[2 * lane], now[2 * lane + 1])
            score(lane, later[2 * lane], later[2 * lane + 1])
        return later

    lax.fori_loop(0, (items + WIDTH - 1) // WIDTH, step, tuple(start))

    if mode == "near":
        for b in range(count):
            for held, out in zip((m_ref, l_ref, acc_ref), outs[3 * b : 3 * b + 3]):
                out[...] = held[b * OWN : (b + 1) * OWN]
        return

    def finish(i, _):
        for u in range(4):
            t = i * 4 + u
            logs = {}
            for b, block in enumerate(blocks):
                total = jnp.sum(l_ref[b * OWN + t], axis=0, keepdims=True)
                some = total > 0.0
                safe = jnp.where(some, total, 1.0)
                share = jnp.where(some, 1.0 / safe, 0.0)
                outs[b][t, :HD] = (acc_ref[b * OWN + t] * share).astype(jnp.bfloat16)
                logs[block] = jnp.where(some, m_ref[b * OWN + t] * SCALE + jnp.log(safe), NEG)
                outs[count + b][pl.ds(t, 1)] = logs[block]
            none = [jnp.zeros((1, BLK), jnp.bfloat16)] * 3
            below = [row for b in range(RING) for row in (split(logs[b]) if b in logs else none)]
            below.append(jnp.zeros((PAD - 3 * RING, BLK), jnp.bfloat16))
            for b in range(count):
                outs[b][t, HD:] = jnp.concatenate(below, axis=0)
        return 0

    lax.fori_loop(0, OWN // 4, finish, 0)


def attend(blocks, mode, lists, queries, keys_values, states=()):
    count = len(blocks)
    slots = count * OWN + 1
    keys = {"near": NEAR, "far": OWN, "full": KEYS}[mode]
    pairs = count * keys * 4
    shapes = ((1, BLK), (8, BLK), (HD, BLK))
    if mode == "near":
        out_shape = [jax.ShapeDtypeStruct((OWN, *shape), jnp.float32) for shape in shapes] * count
    else:
        out_shape = [jax.ShapeDtypeStruct((OWN, HD + PAD, BLK), jnp.bfloat16)] * count
        out_shape += [jax.ShapeDtypeStruct((OWN, BLK), jnp.float32)] * count
    operands = (*queries, *keys_values, *states)
    return pl.pallas_call(
        functools.partial(attend_kernel, blocks, mode),
        out_shape=tuple(out_shape),
        in_specs=[SMEM] * 3 + [VMEM] * len(operands),
        out_specs=(VMEM,) * len(out_shape),
        scratch_shapes=[pltpu.SMEM((slots,), jnp.int32)] * 3
        + [
            pltpu.VMEM((count * OWN, BLK, HD), jnp.bfloat16),
            pltpu.VMEM((keys, BLK, HD), jnp.bfloat16),
            pltpu.VMEM((keys, HD, BLK), jnp.bfloat16),
        ]
        + [pltpu.VMEM((slots, *shape), jnp.float32) for shape in shapes]
        + [pltpu.VMEM((CHUNK * BLK, BLK), jnp.float32)] * WIDTH
        + [pltpu.VMEM((1, BLK), jnp.float32)] * WIDTH,
        compiler_params=SPACE,
        cost_estimate=pl.CostEstimate(
            flops=pairs * 4 * BLK * BLK * HD,
            bytes_accessed=5 << 20,
            transcendentals=pairs * BLK * BLK,
        ),
        name=mode,
    )(*lists, *operands)


def combine_kernel(e0, *refs):
    outs, o_ref = refs[:-1], refs[-1]
    for t in range(OWN):
        parts = [e0[t : t + 1]]
        for block in range(1, RING):
            parts.append(joined(outs[block][t, HD:].astype(jnp.float32), block))
        top = jnp.maximum(jnp.maximum(parts[0], parts[1]), jnp.maximum(parts[2], parts[3]))
        shares = [jnp.exp(part - top) for part in parts]
        total = (shares[0] + shares[1]) + (shares[2] + shares[3])
        mixed = sum(o[t, :HD].astype(jnp.float32) * (w / total) for o, w in zip(outs, shares))
        o_ref[t] = mixed.T.astype(jnp.bfloat16)


def combine(e0, outs):
    return pl.pallas_call(
        combine_kernel,
        out_shape=jax.ShapeDtypeStruct((OWN, BLK, HD), jnp.bfloat16),
        in_specs=[VMEM] * (RING + 1),
        out_specs=VMEM,
        compiler_params=SPACE,
        name="combine",
    )(e0, *outs)


def pick_kernel(spots, e0, e1, e2, e3, out, every):
    for block, log in enumerate((e0, e1, e2, e3)):
        every[block * OWN : (block + 1) * OWN] = log[...]
    every[KEYS : KEYS + 8] = jnp.full((8, BLK), NEG, jnp.float32)
    for ctx in range(RING * RING):
        for slot in range(OWN):
            out[ctx, slot : slot + 1] = every[pl.ds(spots[ctx * OWN + slot], 1)]


def pick(spots, logs):
    return pl.pallas_call(
        pick_kernel,
        out_shape=jax.ShapeDtypeStruct((RING * RING, OWN, BLK), jnp.float32),
        in_specs=[SMEM] + [VMEM] * RING,
        out_specs=VMEM,
        scratch_shapes=[pltpu.VMEM((KEYS + 8, BLK), jnp.float32)],
        compiler_params=SPACE,
        name="pick",
    )(spots, *logs)


def merge_kernel(parts, out):
    top = jnp.max(parts[...], axis=0)
    out[...] = top + jnp.log(jnp.sum(jnp.exp(parts[...] - top[None]), axis=0))


def merge(parts):
    return pl.pallas_call(
        merge_kernel,
        out_shape=jax.ShapeDtypeStruct((OWN, BLK), jnp.float32),
        in_specs=[VMEM],
        out_specs=VMEM,
        compiler_params=SPACE,
        name="merge",
    )(parts)


def slot_spots(assign, xi, yi):
    spots = (assign % OWN // 3 - yi) % RING * OWN + assign % KEYS // OWN * 3 + assign % 3
    return jnp.where(assign // KEYS == xi, spots, KEYS)


def key_lists(kv_tiles, tile_count, xi, yi):
    rows = lax.dynamic_slice_in_dim(kv_tiles, xi * KEYS, KEYS)
    used = lax.dynamic_slice_in_dim(tile_count, xi * KEYS, KEYS)
    here = (rows % OWN // 3 == yi) & (jnp.arange(LIST, dtype=jnp.int32)[None, :] < used[:, None])
    away = (rows // KEYS - xi) % RING
    block = jnp.where(away == 2, 3, jnp.minimum(away, 2))
    place = block * OWN + rows % KEYS // OWN * 3 + rows % 3
    near, far = here & (away != 2), here & (away == 2)
    nears = jnp.sum(near.astype(jnp.int32), axis=1)
    before = (jnp.arange(LIST)[:, None] < jnp.arange(LIST)[None, :]).astype(jnp.bfloat16)
    rank_near = jnp.dot(near.astype(jnp.bfloat16), before, preferred_element_type=jnp.float32)
    rank_far = jnp.dot(far.astype(jnp.bfloat16), before, preferred_element_type=jnp.float32)
    rank = jnp.where(
        near, rank_near.astype(jnp.int32), nears[:, None] + rank_far.astype(jnp.int32)
    )
    spot = jnp.arange(KEYS + CHUNK, dtype=jnp.int32)[None, :, None]
    at = here[:, None, :] & (rank[:, None, :] == spot)
    lists = jnp.sum(jnp.where(at, place[:, None, :], 0), axis=2)
    return lists, nears, jnp.sum(here.astype(jnp.int32), axis=1)


def exchange(array):
    return lax.all_to_all(array, GROUP, split_axis=0, concat_axis=0, tiled=True)


def on_device(queries, keys, values, kv_tiles, tile_count, assign):
    xi, yi = lax.axis_index("x"), lax.axis_index("y")
    lists = key_lists(kv_tiles, tile_count, xi, yi)
    spots = slot_spots(assign, xi, yi)
    by_head = jnp.transpose(queries.reshape(96, 16, HD), (1, 0, 2))
    sent = jnp.stack([a.reshape(96, 16, HD) for a in (keys, values)])
    got = exchange(jnp.transpose(sent, (2, 0, 1, 3)))
    got, by_head, spots, *lists = lax.optimization_barrier((got, by_head, spots, *lists))
    kv0 = prepare(got)
    kv1, kv3 = shift(kv0, "x", -1), shift(kv0, "x", 1)
    q0 = exchange(by_head).reshape(OWN, BLK, HD)
    k2, v2 = shift(kv3[0], "x", 1), shift(kv1[1], "x", -1)
    q0, q1, q2, q3 = around(q0, "y")
    state = attend((0,), "near", lists, (q0,), (kv0, kv1, kv3))
    o0, e0 = attend((0,), "far", lists, (q0,), (k2, v2), state)
    q2, o0 = lax.optimization_barrier((q2, o0))
    kv = (kv0, kv1, kv3, k2, v2)
    o2, e2 = attend((2,), "full", lists, (q2,), kv)
    q1, o2 = lax.optimization_barrier((q1, o2))
    o2 = shift(o2, "y", 2)
    o1, o3, e1, e3 = attend((1, 3), "full", lists, (q1, q3), kv)
    e1, o2 = lax.optimization_barrier((e1, o2))
    parts = lax.all_to_all(
        pick(spots, (e0, e1, e2, e3)), ("x", "y"), split_axis=0, concat_axis=0, tiled=True
    )
    o0, parts = lax.optimization_barrier((o0, parts))
    blended = combine(e0, (o0, shift(o1, "y", 1), o2, shift(o3, "y", -1)))
    back = exchange(blended.reshape(16, 96, HD))
    attended = jnp.transpose(back, (1, 0, 2)).reshape(96, 16 * HD)
    turned = [(b * RING + a, a * RING + b) for a in range(RING) for b in range(RING)]
    return attended, lax.ppermute(merge(parts).reshape(1, OWN * BLK), ("zh", "y"), turned)


def solution(mesh):
    split = jax.sharding.Mesh(
        mesh.devices.reshape(RING, RING, RING, 2, 2), ("x", "zh", "y", "zl", "core")
    )
    tokens = P(("x", "zh", "y", "zl", "core"), None)
    return jax.shard_map(
        on_device,
        mesh=split,
        in_specs=(tokens, tokens, tokens, P(), P(), P()),
        out_specs=(tokens, P(("y", "zl", "core"), ("x", "zh"))),
        check_vma=False,
    )
```

```python
import functools

import jax
import jax.numpy as jnp
from jax import lax
from jax.experimental import pallas as pl
from jax.experimental.pallas import tpu as pltpu
from jax.sharding import PartitionSpec as P

HD = 128
BLK = 128
LIST = 96
RING = 4
OWN = 12
KEYS = RING * OWN
NEAR = 3 * OWN
CHUNK = 4
WIDTHS = {1: 8, 2: 12}
PAD = 16
NEG = -1e30
SCALE = HD**-0.5
LOG2E = 1.4426950408889634
VMEM = pl.BlockSpec(memory_space=pltpu.VMEM)
SMEM = pl.BlockSpec(memory_space=pltpu.SMEM)
SPACE = pltpu.CompilerParams(vmem_limit_bytes=16 * 1024 * 1024)
GROUP = ("zh", "zl", "core")


def shift(array, axis, by):
    return lax.ppermute(array, axis, [(i, (i + by) % RING) for i in range(RING)])


def around(array, axis):
    return [array] + [shift(array, axis, -by) for by in range(1, RING)]


def prepare_kernel(got_ref, kv_ref):
    for part in range(RING):
        k, v = (
            got_ref[4 * part : 4 * part + 4, which].reshape(3, BLK, HD) for which in range(2)
        )
        kv_ref[0, 3 * part : 3 * part + 3] = k
        for i in range(3):
            kv_ref[1, 3 * part + i] = v[i].T


def prepare(got):
    return pl.pallas_call(
        prepare_kernel,
        out_shape=jax.ShapeDtypeStruct((2, OWN, BLK, HD), jnp.bfloat16),
        in_specs=[VMEM],
        out_specs=VMEM,
        compiler_params=SPACE,
        name="prepare",
    )(got)


def split(log):
    high = log.astype(jnp.bfloat16)
    rest = log - high.astype(jnp.float32)
    middle = rest.astype(jnp.bfloat16)
    return [high, middle, (rest - middle.astype(jnp.float32)).astype(jnp.bfloat16)]


def joined(rows, block):
    parts = [rows[3 * block + i : 3 * block + i + 1] for i in range(3)]
    return parts[0] + parts[1] + parts[2]


def attend_kernel(blocks, mode, lists, nears, counts, *refs):
    count = len(blocks)
    tiles = count * OWN
    width = WIDTHS[count]
    queries, refs = refs[:count], refs[count:]
    if mode != "far":
        for_near, refs = refs[:3], refs[3:]
    if mode != "near":
        (k2, v2), refs = refs[:2], refs[2:]
    if mode == "far":
        states, refs = refs[: 3 * count], refs[3 * count :]
    size = (3 if mode == "near" else 2) * count
    outs, refs = refs[:size], refs[size:]
    rows, begins, sizes, qs, ks, vs, m_ref, l_ref, acc_ref = refs[:9]
    s_refs, top_refs = refs[9 : 9 + width], refs[9 + width :]
    for b, q in enumerate(queries):
        qs[b * OWN : (b + 1) * OWN] = q[...]
    if mode != "far":
        for b, kv in enumerate(for_near):
            ks[b * OWN : (b + 1) * OWN] = kv[0]
            vs[b * OWN : (b + 1) * OWN] = kv[1]
    if mode != "near":
        at = 0 if mode == "far" else NEAR
        ks[at : at + OWN] = k2[...]
        vs[at : at + OWN] = v2[...]
    m_ref[...] = jnp.full(m_ref.shape, NEG, jnp.float32)
    l_ref[...] = jnp.zeros(l_ref.shape, jnp.float32)
    acc_ref[...] = jnp.zeros(acc_ref.shape, jnp.float32)
    if mode == "far":
        for b in range(count):
            for held, state in zip((m_ref, l_ref, acc_ref), states[3 * b : 3 * b + 3]):
                held[b * OWN : (b + 1) * OWN] = state[...]
    yi = lax.axis_index("y")
    items = jnp.int32(0)
    for b, block in enumerate(blocks):
        owner = lax.rem(yi + block, RING) * 3
        for t in range(OWN):
            row = owner + (t // 3 * OWN + t % 3)
            begin = nears[row] if mode == "far" else jnp.int32(0)
            total = (nears[row] if mode == "near" else counts[row]) - begin
            rows[b * OWN + t] = row
            begins[b * OWN + t] = begin
            sizes[b * OWN + t] = total
            items += jnp.maximum((total + CHUNK - 1) // CHUNK, 1)
    rows[tiles] = 0
    begins[tiles] = 0
    sizes[tiles] = 0

    def advance(t, j):
        more = (j + 1) * CHUNK < sizes[t]
        return jnp.where(more, t, jnp.minimum(t + 1, tiles)), jnp.where(more, j + 1, 0)

    def listed(t, j):
        row = rows[t]
        at = begins[t] + j * CHUNK
        found = [lists[row, at + u] for u in range(CHUNK)]
        if mode == "near":
            return [jnp.minimum(u, NEAR - 1) for u in found]
        return [jnp.maximum(u - NEAR, 0) for u in found] if mode == "far" else found

    def score(lane, t, j):
        left = sizes[t] - j * CHUNK
        tile = listed(t, j)
        s = lax.dot_general(
            jnp.concatenate([ks[u] for u in tile], axis=0),
            qs[jnp.minimum(t, tiles - 1)],
            (((1,), (1,)), ((), ())),
            preferred_element_type=jnp.float32,
        )
        s_refs[lane][...] = s
        top = jnp.full((8, BLK), NEG, jnp.float32)
        for u in range(CHUNK):
            part = jnp.max(s[u * BLK : (u + 1) * BLK].reshape(16, 8, BLK), axis=0)
            top = jnp.maximum(top, jnp.where(u < left, part, NEG))
        top_refs[lane][...] = jnp.max(top, axis=0, keepdims=True)

    def blend(lane, t, j):
        left = sizes[t] - j * CHUNK
        m_old = m_ref[t]
        m_new = jnp.maximum(m_old, top_refs[lane][...])
        m_ref[t] = m_new
        alpha = jnp.exp2((m_old - m_new) * (SCALE * LOG2E))
        base = m_new * (SCALE * LOG2E)
        total = jnp.zeros((8, BLK), jnp.float32)
        weights = []
        for u in range(CHUNK):
            s = s_refs[lane][u * BLK : (u + 1) * BLK] * (SCALE * LOG2E)
            w = jnp.exp2(s - jnp.where(u < left, base, -NEG))
            total = total + jnp.sum(w.reshape(16, 8, BLK), axis=0)
            weights.append(w.astype(jnp.bfloat16))
        vt = jnp.concatenate([vs[tile] for tile in listed(t, j)], axis=1)
        mixed = jnp.dot(vt, jnp.concatenate(weights, axis=0), preferred_element_type=jnp.float32)
        l_ref[t] = l_ref[t] * alpha + total
        acc_ref[t] = acc_ref[t] * alpha + mixed

    def following(t, j):
        group = []
        for _ in range(width):
            t, j = advance(t, j)
            group += [t, j]
        return tuple(group)

    start = [jnp.int32(0), jnp.int32(0)]
    for _ in range(width - 1):
        start += advance(*start[-2:])
    for lane in range(width):
        score(lane, start[2 * lane], start[2 * lane + 1])

    def step(_, now):
        later = following(*now[-2:])
        for lane in range(width):
            blend(lane, now[2 * lane], now[2 * lane + 1])
            score(lane, later[2 * lane], later[2 * lane + 1])
        return later

    end = lax.fori_loop(0, (items + width - 1) // width - 1, step, tuple(start))
    for lane in range(width):
        blend(lane, end[2 * lane], end[2 * lane + 1])

    if mode == "near":
        for b in range(count):
            for held, out in zip((m_ref, l_ref, acc_ref), outs[3 * b : 3 * b + 3]):
                out[...] = held[b * OWN : (b + 1) * OWN]
        return

    def finish(i, _):
        for u in range(4):
            t = i * 4 + u
            logs = {}
            for b, block in enumerate(blocks):
                total = jnp.sum(l_ref[b * OWN + t], axis=0, keepdims=True)
                some = total > 0.0
                safe = jnp.where(some, total, 1.0)
                share = jnp.where(some, 1.0 / safe, 0.0)
                outs[b][t, :HD] = (acc_ref[b * OWN + t] * share).astype(jnp.bfloat16)
                logs[block] = jnp.where(some, m_ref[b * OWN + t] * SCALE + jnp.log(safe), NEG)
                outs[count + b][pl.ds(t, 1)] = logs[block]
            none = [jnp.zeros((1, BLK), jnp.bfloat16)] * 3
            below = [row for b in range(RING) for row in (split(logs[b]) if b in logs else none)]
            below.append(jnp.zeros((PAD - 3 * RING, BLK), jnp.bfloat16))
            for b in range(count):
                outs[b][t, HD:] = jnp.concatenate(below, axis=0)
        return 0

    lax.fori_loop(0, OWN // 4, finish, 0)


def attend(blocks, mode, lists, queries, keys_values, states=()):
    count = len(blocks)
    slots = count * OWN + 1
    keys = {"near": NEAR, "far": OWN, "full": KEYS}[mode]
    pairs = count * keys * 4
    shapes = ((1, BLK), (8, BLK), (HD, BLK))
    if mode == "near":
        out_shape = [jax.ShapeDtypeStruct((OWN, *shape), jnp.float32) for shape in shapes] * count
    else:
        out_shape = [jax.ShapeDtypeStruct((OWN, HD + PAD, BLK), jnp.bfloat16)] * count
        out_shape += [jax.ShapeDtypeStruct((OWN, BLK), jnp.float32)] * count
    operands = (*queries, *keys_values, *states)
    return pl.pallas_call(
        functools.partial(attend_kernel, blocks, mode),
        out_shape=tuple(out_shape),
        in_specs=[SMEM] * 3 + [VMEM] * len(operands),
        out_specs=(VMEM,) * len(out_shape),
        scratch_shapes=[pltpu.SMEM((slots,), jnp.int32)] * 3
        + [
            pltpu.VMEM((count * OWN, BLK, HD), jnp.bfloat16),
            pltpu.VMEM((keys, BLK, HD), jnp.bfloat16),
            pltpu.VMEM((keys, HD, BLK), jnp.bfloat16),
        ]
        + [pltpu.VMEM((slots, *shape), jnp.float32) for shape in shapes]
        + [pltpu.VMEM((CHUNK * BLK, BLK), jnp.float32)] * WIDTHS[count]
        + [pltpu.VMEM((1, BLK), jnp.float32)] * WIDTHS[count],
        compiler_params=SPACE,
        cost_estimate=pl.CostEstimate(
            flops=pairs * 4 * BLK * BLK * HD,
            bytes_accessed=5 << 20,
            transcendentals=pairs * BLK * BLK,
        ),
        name=mode,
    )(*lists, *operands)


def combine_kernel(e0, *refs):
    outs, o_ref = refs[:-1], refs[-1]
    for t in range(OWN):
        parts = [e0[t : t + 1]]
        for block in range(1, RING):
            parts.append(joined(outs[block][t, HD:].astype(jnp.float32), block))
        top = jnp.maximum(jnp.maximum(parts[0], parts[1]), jnp.maximum(parts[2], parts[3]))
        shares = [jnp.exp(part - top) for part in parts]
        total = (shares[0] + shares[1]) + (shares[2] + shares[3])
        mixed = sum(o[t, :HD].astype(jnp.float32) * (w / total) for o, w in zip(outs, shares))
        o_ref[t] = mixed.T.astype(jnp.bfloat16)


def combine(e0, outs):
    return pl.pallas_call(
        combine_kernel,
        out_shape=jax.ShapeDtypeStruct((OWN, BLK, HD), jnp.bfloat16),
        in_specs=[VMEM] * (RING + 1),
        out_specs=VMEM,
        compiler_params=SPACE,
        name="combine",
    )(e0, *outs)


def pick_kernel(spots, e0, e1, e2, e3, out, every):
    for block, log in enumerate((e0, e1, e2, e3)):
        every[block * OWN : (block + 1) * OWN] = log[...]
    every[KEYS : KEYS + 8] = jnp.full((8, BLK), NEG, jnp.float32)
    for ctx in range(RING * RING):
        for slot in range(OWN):
            out[ctx, slot : slot + 1] = every[pl.ds(spots[ctx * OWN + slot], 1)]


def pick(spots, logs):
    return pl.pallas_call(
        pick_kernel,
        out_shape=jax.ShapeDtypeStruct((RING * RING, OWN, BLK), jnp.float32),
        in_specs=[SMEM] + [VMEM] * RING,
        out_specs=VMEM,
        scratch_shapes=[pltpu.VMEM((KEYS + 8, BLK), jnp.float32)],
        compiler_params=SPACE,
        name="pick",
    )(spots, *logs)


def merge_kernel(parts, out):
    top = jnp.max(parts[...], axis=0)
    out[...] = top + jnp.log(jnp.sum(jnp.exp(parts[...] - top[None]), axis=0))


def merge(parts):
    return pl.pallas_call(
        merge_kernel,
        out_shape=jax.ShapeDtypeStruct((OWN, BLK), jnp.float32),
        in_specs=[VMEM],
        out_specs=VMEM,
        compiler_params=SPACE,
        name="merge",
    )(parts)


def slot_spots(assign, xi, yi):
    spots = (assign % OWN // 3 - yi) % RING * OWN + assign % KEYS // OWN * 3 + assign % 3
    return jnp.where(assign // KEYS == xi, spots, KEYS)


def key_lists(kv_tiles, tile_count, xi, yi):
    rows = lax.dynamic_slice_in_dim(kv_tiles, xi * KEYS, KEYS)
    used = lax.dynamic_slice_in_dim(tile_count, xi * KEYS, KEYS)
    here = (rows % OWN // 3 == yi) & (jnp.arange(LIST, dtype=jnp.int32)[None, :] < used[:, None])
    away = (rows // KEYS - xi) % RING
    block = jnp.where(away == 2, 3, jnp.minimum(away, 2))
    place = block * OWN + rows % KEYS // OWN * 3 + rows % 3
    near, far = here & (away != 2), here & (away == 2)
    nears = jnp.sum(near.astype(jnp.int32), axis=1)
    before = (jnp.arange(LIST)[:, None] < jnp.arange(LIST)[None, :]).astype(jnp.bfloat16)
    rank_near = jnp.dot(near.astype(jnp.bfloat16), before, preferred_element_type=jnp.float32)
    rank_far = jnp.dot(far.astype(jnp.bfloat16), before, preferred_element_type=jnp.float32)
    rank = jnp.where(
        near, rank_near.astype(jnp.int32), nears[:, None] + rank_far.astype(jnp.int32)
    )
    spot = jnp.arange(KEYS + CHUNK, dtype=jnp.int32)[None, :, None]
    at = here[:, None, :] & (rank[:, None, :] == spot)
    lists = jnp.sum(jnp.where(at, place[:, None, :], 0), axis=2)
    return lists, nears, jnp.sum(here.astype(jnp.int32), axis=1)


def exchange(array):
    return lax.all_to_all(array, GROUP, split_axis=0, concat_axis=0, tiled=True)


def on_device(queries, keys, values, kv_tiles, tile_count, assign):
    xi, yi = lax.axis_index("x"), lax.axis_index("y")
    lists = key_lists(kv_tiles, tile_count, xi, yi)
    spots = slot_spots(assign, xi, yi)
    by_head = jnp.transpose(queries.reshape(96, 16, HD), (1, 0, 2))
    sent = jnp.stack([a.reshape(96, 16, HD) for a in (keys, values)])
    got = exchange(jnp.transpose(sent, (2, 0, 1, 3)))
    got, by_head, spots, *lists = lax.optimization_barrier((got, by_head, spots, *lists))
    kv0 = prepare(got)
    kv1, kv3 = shift(kv0, "x", -1), shift(kv0, "x", 1)
    q0 = exchange(by_head).reshape(OWN, BLK, HD)
    k2, v2 = shift(kv3[0], "x", 1), shift(kv1[1], "x", -1)
    q0, q1, q2, q3 = around(q0, "y")
    state = attend((0,), "near", lists, (q0,), (kv0, kv1, kv3))
    o0, e0 = attend((0,), "far", lists, (q0,), (k2, v2), state)
    q2, o0 = lax.optimization_barrier((q2, o0))
    kv = (kv0, kv1, kv3, k2, v2)
    o2, e2 = attend((2,), "full", lists, (q2,), kv)
    q1, o2 = lax.optimization_barrier((q1, o2))
    o2 = shift(o2, "y", 2)
    o1, o3, e1, e3 = attend((1, 3), "full", lists, (q1, q3), kv)
    e1, o2 = lax.optimization_barrier((e1, o2))
    parts = lax.all_to_all(
        pick(spots, (e0, e1, e2, e3)), ("x", "y"), split_axis=0, concat_axis=0, tiled=True
    )
    o0, parts = lax.optimization_barrier((o0, parts))
    blended = combine(e0, (o0, shift(o1, "y", 1), o2, shift(o3, "y", -1)))
    back = exchange(blended.reshape(16, 96, HD))
    attended = jnp.transpose(back, (1, 0, 2)).reshape(96, 16 * HD)
    turned = [(b * RING + a, a * RING + b) for a in range(RING) for b in range(RING)]
    return attended, lax.ppermute(merge(parts).reshape(1, OWN * BLK), ("zh", "y"), turned)


def solution(mesh):
    split = jax.sharding.Mesh(
        mesh.devices.reshape(RING, RING, RING, 2, 2), ("x", "zh", "y", "zl", "core")
    )
    tokens = P(("x", "zh", "y", "zl", "core"), None)
    return jax.shard_map(
        on_device,
        mesh=split,
        in_specs=(tokens, tokens, tokens, P(), P(), P()),
        out_specs=(tokens, P(("y", "zl", "core"), ("x", "zh"))),
        check_vma=False,
    )
```

```python
import functools

import jax
import jax.numpy as jnp
from jax import lax
from jax.experimental import pallas as pl
from jax.experimental.pallas import tpu as pltpu
from jax.sharding import PartitionSpec as P

HD = 128
BLK = 128
LIST = 96
RING = 4
OWN = 12
KEYS = RING * OWN
NEAR = 3 * OWN
CHUNK = 4
WIDTHS = {1: 8, 2: 12}
PAD = 16
NEG = -1e30
SCALE = HD**-0.5
LOG2E = 1.4426950408889634
VMEM = pl.BlockSpec(memory_space=pltpu.VMEM)
SMEM = pl.BlockSpec(memory_space=pltpu.SMEM)
SPACE = pltpu.CompilerParams(vmem_limit_bytes=16 * 1024 * 1024)
GROUP = ("zh", "zl", "core")


def shift(array, axis, by):
    return lax.ppermute(array, axis, [(i, (i + by) % RING) for i in range(RING)])


def around(array, axis):
    return [array] + [shift(array, axis, -by) for by in range(1, RING)]


def prepare_kernel(got_ref, kv_ref):
    for part in range(RING):
        k, v = (
            got_ref[4 * part : 4 * part + 4, which].reshape(3, BLK, HD) for which in range(2)
        )
        kv_ref[0, 3 * part : 3 * part + 3] = k
        for i in range(3):
            kv_ref[1, 3 * part + i] = v[i].T


def prepare(got):
    return pl.pallas_call(
        prepare_kernel,
        out_shape=jax.ShapeDtypeStruct((2, OWN, BLK, HD), jnp.bfloat16),
        in_specs=[VMEM],
        out_specs=VMEM,
        compiler_params=SPACE,
        name="prepare",
    )(got)


def split(log):
    high = log.astype(jnp.bfloat16)
    rest = log - high.astype(jnp.float32)
    middle = rest.astype(jnp.bfloat16)
    return [high, middle, (rest - middle.astype(jnp.float32)).astype(jnp.bfloat16)]


def joined(rows, block):
    parts = [rows[3 * block + i : 3 * block + i + 1] for i in range(3)]
    return parts[0] + parts[1] + parts[2]


def attend_kernel(blocks, mode, lists, nears, counts, *refs):
    count = len(blocks)
    tiles = count * OWN
    width = WIDTHS[count]
    queries, refs = refs[:count], refs[count:]
    for_near, refs = refs[:3], refs[3:]
    if mode != "near":
        (k2, v2), refs = refs[:2], refs[2:]
    if mode == "rest":
        state, refs = refs[:3], refs[3:]
    size = (3 if mode == "near" else 2) * count
    outs, refs = refs[:size], refs[size:]
    rows, begins, sizes, qs, ks, vs, m_ref, l_ref, acc_ref = refs[:9]
    s_refs, top_refs = refs[9 : 9 + width], refs[9 + width :]
    for b, q in enumerate(queries):
        qs[b * OWN : (b + 1) * OWN] = q[...]
    for b, kv in enumerate(for_near):
        ks[b * OWN : (b + 1) * OWN] = kv[0]
        vs[b * OWN : (b + 1) * OWN] = kv[1]
    if mode != "near":
        ks[NEAR:KEYS] = k2[...]
        vs[NEAR:KEYS] = v2[...]
    m_ref[...] = jnp.full(m_ref.shape, NEG, jnp.float32)
    l_ref[...] = jnp.zeros(l_ref.shape, jnp.float32)
    acc_ref[...] = jnp.zeros(acc_ref.shape, jnp.float32)
    if mode == "rest":
        for held, part in zip((m_ref, l_ref, acc_ref), state):
            held[:OWN] = part[...]
    yi = lax.axis_index("y")
    items = jnp.int32(0)
    for b, block in enumerate(blocks):
        owner = lax.rem(yi + block, RING) * 3
        for t in range(OWN):
            row = owner + (t // 3 * OWN + t % 3)
            begin = nears[row] if mode == "rest" and b == 0 else jnp.int32(0)
            total = (nears[row] if mode == "near" else counts[row]) - begin
            rows[b * OWN + t] = row
            begins[b * OWN + t] = begin
            sizes[b * OWN + t] = total
            items += jnp.maximum((total + CHUNK - 1) // CHUNK, 1)
    rows[tiles] = 0
    begins[tiles] = 0
    sizes[tiles] = 0

    def advance(t, j):
        more = (j + 1) * CHUNK < sizes[t]
        return jnp.where(more, t, jnp.minimum(t + 1, tiles)), jnp.where(more, j + 1, 0)

    def listed(t, j):
        row = rows[t]
        at = begins[t] + j * CHUNK
        found = [lists[row, at + u] for u in range(CHUNK)]
        return [jnp.minimum(u, NEAR - 1) for u in found] if mode == "near" else found

    def score(lane, t, j):
        left = sizes[t] - j * CHUNK
        tile = listed(t, j)
        s = lax.dot_general(
            jnp.concatenate([ks[u] for u in tile], axis=0),
            qs[jnp.minimum(t, tiles - 1)],
            (((1,), (1,)), ((), ())),
            preferred_element_type=jnp.float32,
        )
        s_refs[lane][...] = s
        top = jnp.full((8, BLK), NEG, jnp.float32)
        for u in range(CHUNK):
            part = jnp.max(s[u * BLK : (u + 1) * BLK].reshape(16, 8, BLK), axis=0)
            top = jnp.maximum(top, jnp.where(u < left, part, NEG))
        top_refs[lane][...] = jnp.max(top, axis=0, keepdims=True)

    def blend(lane, t, j):
        left = sizes[t] - j * CHUNK
        m_old = m_ref[t]
        m_new = jnp.maximum(m_old, top_refs[lane][...])
        m_ref[t] = m_new
        alpha = jnp.exp2((m_old - m_new) * (SCALE * LOG2E))
        base = m_new * (SCALE * LOG2E)
        total = jnp.zeros((8, BLK), jnp.float32)
        weights = []
        for u in range(CHUNK):
            s = s_refs[lane][u * BLK : (u + 1) * BLK] * (SCALE * LOG2E)
            w = jnp.exp2(s - jnp.where(u < left, base, -NEG))
            total = total + jnp.sum(w.reshape(16, 8, BLK), axis=0)
            weights.append(w.astype(jnp.bfloat16))
        vt = jnp.concatenate([vs[tile] for tile in listed(t, j)], axis=1)
        mixed = jnp.dot(vt, jnp.concatenate(weights, axis=0), preferred_element_type=jnp.float32)
        l_ref[t] = l_ref[t] * alpha + total
        acc_ref[t] = acc_ref[t] * alpha + mixed

    def following(t, j):
        group = []
        for _ in range(width):
            t, j = advance(t, j)
            group += [t, j]
        return tuple(group)

    start = [jnp.int32(0), jnp.int32(0)]
    for _ in range(width - 1):
        start += advance(*start[-2:])
    for lane in range(width):
        score(lane, start[2 * lane], start[2 * lane + 1])

    def step(_, now):
        later = following(*now[-2:])
        for lane in range(width):
            blend(lane, now[2 * lane], now[2 * lane + 1])
            score(lane, later[2 * lane], later[2 * lane + 1])
        return later

    end = lax.fori_loop(0, (items + width - 1) // width - 1, step, tuple(start))
    for lane in range(width):
        blend(lane, end[2 * lane], end[2 * lane + 1])

    if mode == "near":
        for b in range(count):
            for held, out in zip((m_ref, l_ref, acc_ref), outs[3 * b : 3 * b + 3]):
                out[...] = held[b * OWN : (b + 1) * OWN]
        return

    def finish(i, _):
        for u in range(4):
            t = i * 4 + u
            logs = {}
            for b, block in enumerate(blocks):
                total = jnp.sum(l_ref[b * OWN + t], axis=0, keepdims=True)
                some = total > 0.0
                safe = jnp.where(some, total, 1.0)
                share = jnp.where(some, 1.0 / safe, 0.0)
                outs[b][t, :HD] = (acc_ref[b * OWN + t] * share).astype(jnp.bfloat16)
                logs[block] = jnp.where(some, m_ref[b * OWN + t] * SCALE + jnp.log(safe), NEG)
                outs[count + b][pl.ds(t, 1)] = logs[block]
            none = [jnp.zeros((1, BLK), jnp.bfloat16)] * 3
            below = [row for b in range(RING) for row in (split(logs[b]) if b in logs else none)]
            below.append(jnp.zeros((PAD - 3 * RING, BLK), jnp.bfloat16))
            for b in range(count):
                outs[b][t, HD:] = jnp.concatenate(below, axis=0)
        return 0

    lax.fori_loop(0, OWN // 4, finish, 0)


def attend(blocks, mode, lists, queries, keys_values, states=()):
    count = len(blocks)
    slots = count * OWN + 1
    keys = NEAR if mode == "near" else KEYS
    pairs = count * keys * 4
    shapes = ((1, BLK), (8, BLK), (HD, BLK))
    if mode == "near":
        out_shape = [jax.ShapeDtypeStruct((OWN, *shape), jnp.float32) for shape in shapes] * count
    else:
        out_shape = [jax.ShapeDtypeStruct((OWN, HD + PAD, BLK), jnp.bfloat16)] * count
        out_shape += [jax.ShapeDtypeStruct((OWN, BLK), jnp.float32)] * count
    operands = (*queries, *keys_values, *states)
    return pl.pallas_call(
        functools.partial(attend_kernel, blocks, mode),
        out_shape=tuple(out_shape),
        in_specs=[SMEM] * 3 + [VMEM] * len(operands),
        out_specs=(VMEM,) * len(out_shape),
        scratch_shapes=[pltpu.SMEM((slots,), jnp.int32)] * 3
        + [
            pltpu.VMEM((count * OWN, BLK, HD), jnp.bfloat16),
            pltpu.VMEM((keys, BLK, HD), jnp.bfloat16),
            pltpu.VMEM((keys, HD, BLK), jnp.bfloat16),
        ]
        + [pltpu.VMEM((slots, *shape), jnp.float32) for shape in shapes]
        + [pltpu.VMEM((CHUNK * BLK, BLK), jnp.float32)] * WIDTHS[count]
        + [pltpu.VMEM((1, BLK), jnp.float32)] * WIDTHS[count],
        compiler_params=SPACE,
        cost_estimate=pl.CostEstimate(
            flops=pairs * 4 * BLK * BLK * HD,
            bytes_accessed=5 << 20,
            transcendentals=pairs * BLK * BLK,
        ),
        name=mode,
    )(*lists, *operands)


def combine_kernel(e0, *refs):
    outs, o_ref = refs[:-1], refs[-1]
    for t in range(OWN):
        parts = [e0[t : t + 1]]
        for block in range(1, RING):
            parts.append(joined(outs[block][t, HD:].astype(jnp.float32), block))
        top = jnp.maximum(jnp.maximum(parts[0], parts[1]), jnp.maximum(parts[2], parts[3]))
        shares = [jnp.exp(part - top) for part in parts]
        total = (shares[0] + shares[1]) + (shares[2] + shares[3])
        mixed = sum(o[t, :HD].astype(jnp.float32) * (w / total) for o, w in zip(outs, shares))
        o_ref[t] = mixed.T.astype(jnp.bfloat16)


def combine(e0, outs):
    return pl.pallas_call(
        combine_kernel,
        out_shape=jax.ShapeDtypeStruct((OWN, BLK, HD), jnp.bfloat16),
        in_specs=[VMEM] * (RING + 1),
        out_specs=VMEM,
        compiler_params=SPACE,
        name="combine",
    )(e0, *outs)


def pick_kernel(spots, e0, e1, e2, e3, out, every):
    for block, log in enumerate((e0, e1, e2, e3)):
        every[block * OWN : (block + 1) * OWN] = log[...]
    every[KEYS : KEYS + 8] = jnp.full((8, BLK), NEG, jnp.float32)
    for ctx in range(RING * RING):
        for slot in range(OWN):
            out[ctx, slot : slot + 1] = every[pl.ds(spots[ctx * OWN + slot], 1)]


def pick(spots, logs):
    return pl.pallas_call(
        pick_kernel,
        out_shape=jax.ShapeDtypeStruct((RING * RING, OWN, BLK), jnp.float32),
        in_specs=[SMEM] + [VMEM] * RING,
        out_specs=VMEM,
        scratch_shapes=[pltpu.VMEM((KEYS + 8, BLK), jnp.float32)],
        compiler_params=SPACE,
        name="pick",
    )(spots, *logs)


def merge_kernel(parts, out):
    top = jnp.max(parts[...], axis=0)
    out[...] = top + jnp.log(jnp.sum(jnp.exp(parts[...] - top[None]), axis=0))


def merge(parts):
    return pl.pallas_call(
        merge_kernel,
        out_shape=jax.ShapeDtypeStruct((OWN, BLK), jnp.float32),
        in_specs=[VMEM],
        out_specs=VMEM,
        compiler_params=SPACE,
        name="merge",
    )(parts)


def slot_spots(assign, xi, yi):
    spots = (assign % OWN // 3 - yi) % RING * OWN + assign % KEYS // OWN * 3 + assign % 3
    return jnp.where(assign // KEYS == xi, spots, KEYS)


def key_lists(kv_tiles, tile_count, xi, yi):
    rows = lax.dynamic_slice_in_dim(kv_tiles, xi * KEYS, KEYS)
    used = lax.dynamic_slice_in_dim(tile_count, xi * KEYS, KEYS)
    here = (rows % OWN // 3 == yi) & (jnp.arange(LIST, dtype=jnp.int32)[None, :] < used[:, None])
    away = (rows // KEYS - xi) % RING
    block = jnp.where(away == 2, 3, jnp.minimum(away, 2))
    place = block * OWN + rows % KEYS // OWN * 3 + rows % 3
    near, far = here & (away != 2), here & (away == 2)
    nears = jnp.sum(near.astype(jnp.int32), axis=1)
    before = (jnp.arange(LIST)[:, None] < jnp.arange(LIST)[None, :]).astype(jnp.bfloat16)
    rank_near = jnp.dot(near.astype(jnp.bfloat16), before, preferred_element_type=jnp.float32)
    rank_far = jnp.dot(far.astype(jnp.bfloat16), before, preferred_element_type=jnp.float32)
    rank = jnp.where(
        near, rank_near.astype(jnp.int32), nears[:, None] + rank_far.astype(jnp.int32)
    )
    spot = jnp.arange(KEYS + CHUNK, dtype=jnp.int32)[None, :, None]
    at = here[:, None, :] & (rank[:, None, :] == spot)
    lists = jnp.sum(jnp.where(at, place[:, None, :], 0), axis=2)
    return lists, nears, jnp.sum(here.astype(jnp.int32), axis=1)


def exchange(array):
    return lax.all_to_all(array, GROUP, split_axis=0, concat_axis=0, tiled=True)


def on_device(queries, keys, values, kv_tiles, tile_count, assign):
    xi, yi = lax.axis_index("x"), lax.axis_index("y")
    lists = key_lists(kv_tiles, tile_count, xi, yi)
    spots = slot_spots(assign, xi, yi)
    by_head = jnp.transpose(queries.reshape(96, 16, HD), (1, 0, 2))
    sent = jnp.stack([a.reshape(96, 16, HD) for a in (keys, values)])
    got = exchange(jnp.transpose(sent, (2, 0, 1, 3)))
    got, by_head, spots, *lists = lax.optimization_barrier((got, by_head, spots, *lists))
    kv0 = prepare(got)
    kv1, kv3 = shift(kv0, "x", -1), shift(kv0, "x", 1)
    q0 = exchange(by_head).reshape(OWN, BLK, HD)
    k2, v2 = shift(kv3[0], "x", 1), shift(kv1[1], "x", -1)
    q0, q1, q2, q3 = around(q0, "y")
    state = attend((0,), "near", lists, (q0,), (kv0, kv1, kv3))
    kv = (kv0, kv1, kv3, k2, v2)
    o0, o2, e0, e2 = attend((0, 2), "rest", lists, (q0, q2), kv, state)
    q1, o2 = lax.optimization_barrier((q1, o2))
    o2 = shift(o2, "y", 2)
    o1, o3, e1, e3 = attend((1, 3), "full", lists, (q1, q3), kv)
    e1, o2 = lax.optimization_barrier((e1, o2))
    parts = lax.all_to_all(
        pick(spots, (e0, e1, e2, e3)), ("x", "y"), split_axis=0, concat_axis=0, tiled=True
    )
    o0, parts = lax.optimization_barrier((o0, parts))
    blended = combine(e0, (o0, shift(o1, "y", 1), o2, shift(o3, "y", -1)))
    back = exchange(blended.reshape(16, 96, HD))
    attended = jnp.transpose(back, (1, 0, 2)).reshape(96, 16 * HD)
    turned = [(b * RING + a, a * RING + b) for a in range(RING) for b in range(RING)]
    return attended, lax.ppermute(merge(parts).reshape(1, OWN * BLK), ("zh", "y"), turned)


def solution(mesh):
    split = jax.sharding.Mesh(
        mesh.devices.reshape(RING, RING, RING, 2, 2), ("x", "zh", "y", "zl", "core")
    )
    tokens = P(("x", "zh", "y", "zl", "core"), None)
    return jax.shard_map(
        on_device,
        mesh=split,
        in_specs=(tokens, tokens, tokens, P(), P(), P()),
        out_specs=(tokens, P(("y", "zl", "core"), ("x", "zh"))),
        check_vma=False,
    )
```

```python
import functools

import jax
import jax.numpy as jnp
from jax import lax
from jax.experimental import pallas as pl
from jax.experimental.pallas import tpu as pltpu
from jax.sharding import PartitionSpec as P

HD = 128
BLK = 128
LIST = 96
RING = 4
OWN = 12
KEYS = RING * OWN
NEAR = 3 * OWN
CHUNK = 4
WIDTHS = {1: 8, 2: 16}
PAD = 16
NEG = -1e30
SCALE = HD**-0.5
LOG2E = 1.4426950408889634
VMEM = pl.BlockSpec(memory_space=pltpu.VMEM)
SMEM = pl.BlockSpec(memory_space=pltpu.SMEM)
SPACE = pltpu.CompilerParams(vmem_limit_bytes=16 * 1024 * 1024)
GROUP = ("zh", "zl", "core")


def shift(array, axis, by):
    return lax.ppermute(array, axis, [(i, (i + by) % RING) for i in range(RING)])


def around(array, axis):
    return [array] + [shift(array, axis, -by) for by in range(1, RING)]


def prepare_kernel(got_ref, kv_ref):
    for part in range(RING):
        k, v = (
            got_ref[4 * part : 4 * part + 4, which].reshape(3, BLK, HD) for which in range(2)
        )
        kv_ref[0, 3 * part : 3 * part + 3] = k
        for i in range(3):
            kv_ref[1, 3 * part + i] = v[i].T


def prepare(got):
    return pl.pallas_call(
        prepare_kernel,
        out_shape=jax.ShapeDtypeStruct((2, OWN, BLK, HD), jnp.bfloat16),
        in_specs=[VMEM],
        out_specs=VMEM,
        compiler_params=SPACE,
        name="prepare",
    )(got)


def split(log):
    high = log.astype(jnp.bfloat16)
    rest = log - high.astype(jnp.float32)
    middle = rest.astype(jnp.bfloat16)
    return [high, middle, (rest - middle.astype(jnp.float32)).astype(jnp.bfloat16)]


def joined(rows, block):
    parts = [rows[3 * block + i : 3 * block + i + 1] for i in range(3)]
    return parts[0] + parts[1] + parts[2]


def attend_kernel(blocks, mode, lists, nears, counts, *refs):
    count = len(blocks)
    tiles = count * OWN
    width = WIDTHS[count]
    queries, refs = refs[:count], refs[count:]
    if mode != "far":
        for_near, refs = refs[:3], refs[3:]
    if mode != "near":
        (k2, v2), refs = refs[:2], refs[2:]
    if mode == "far":
        states, refs = refs[: 3 * count], refs[3 * count :]
    size = (3 if mode == "near" else 2) * count
    outs, refs = refs[:size], refs[size:]
    rows, begins, sizes, qs, ks, vs, m_ref, l_ref, acc_ref = refs[:9]
    s_refs, top_refs = refs[9 : 9 + width], refs[9 + width :]
    for b, q in enumerate(queries):
        qs[b * OWN : (b + 1) * OWN] = q[...]
    if mode != "far":
        for b, kv in enumerate(for_near):
            ks[b * OWN : (b + 1) * OWN] = kv[0]
            vs[b * OWN : (b + 1) * OWN] = kv[1]
    if mode != "near":
        at = 0 if mode == "far" else NEAR
        ks[at : at + OWN] = k2[...]
        vs[at : at + OWN] = v2[...]
    m_ref[...] = jnp.full(m_ref.shape, NEG, jnp.float32)
    l_ref[...] = jnp.zeros(l_ref.shape, jnp.float32)
    acc_ref[...] = jnp.zeros(acc_ref.shape, jnp.float32)
    if mode == "far":
        for b in range(count):
            for held, state in zip((m_ref, l_ref, acc_ref), states[3 * b : 3 * b + 3]):
                held[b * OWN : (b + 1) * OWN] = state[...]
    yi = lax.axis_index("y")
    items = jnp.int32(0)
    for b, block in enumerate(blocks):
        owner = lax.rem(yi + block, RING) * 3
        for t in range(OWN):
            row = owner + (t // 3 * OWN + t % 3)
            begin = nears[row] if mode == "far" else jnp.int32(0)
            total = (nears[row] if mode == "near" else counts[row]) - begin
            rows[b * OWN + t] = row
            begins[b * OWN + t] = begin
            sizes[b * OWN + t] = total
            items += jnp.maximum((total + CHUNK - 1) // CHUNK, 1)
    rows[tiles] = 0
    begins[tiles] = 0
    sizes[tiles] = 0

    def advance(t, j):
        more = (j + 1) * CHUNK < sizes[t]
        return jnp.where(more, t, jnp.minimum(t + 1, tiles)), jnp.where(more, j + 1, 0)

    def listed(t, j):
        row = rows[t]
        at = begins[t] + j * CHUNK
        found = [lists[row, at + u] for u in range(CHUNK)]
        if mode == "near":
            return [jnp.minimum(u, NEAR - 1) for u in found]
        return [jnp.maximum(u - NEAR, 0) for u in found] if mode == "far" else found

    def score(lane, t, j):
        left = sizes[t] - j * CHUNK
        tile = listed(t, j)
        s = lax.dot_general(
            jnp.concatenate([ks[u] for u in tile], axis=0),
            qs[jnp.minimum(t, tiles - 1)],
            (((1,), (1,)), ((), ())),
            preferred_element_type=jnp.float32,
        )
        s_refs[lane][...] = s
        top = jnp.full((8, BLK), NEG, jnp.float32)
        for u in range(CHUNK):
            part = jnp.max(s[u * BLK : (u + 1) * BLK].reshape(16, 8, BLK), axis=0)
            top = jnp.maximum(top, jnp.where(u < left, part, NEG))
        top_refs[lane][...] = jnp.max(top, axis=0, keepdims=True)

    def blend(lane, t, j):
        left = sizes[t] - j * CHUNK
        m_old = m_ref[t]
        m_new = jnp.maximum(m_old, top_refs[lane][...])
        m_ref[t] = m_new
        alpha = jnp.exp2((m_old - m_new) * (SCALE * LOG2E))
        base = m_new * (SCALE * LOG2E)
        total = jnp.zeros((8, BLK), jnp.float32)
        weights = []
        for u in range(CHUNK):
            s = s_refs[lane][u * BLK : (u + 1) * BLK] * (SCALE * LOG2E)
            w = jnp.exp2(s - jnp.where(u < left, base, -NEG))
            total = total + jnp.sum(w.reshape(16, 8, BLK), axis=0)
            weights.append(w.astype(jnp.bfloat16))
        vt = jnp.concatenate([vs[tile] for tile in listed(t, j)], axis=1)
        mixed = jnp.dot(vt, jnp.concatenate(weights, axis=0), preferred_element_type=jnp.float32)
        l_ref[t] = l_ref[t] * alpha + total
        acc_ref[t] = acc_ref[t] * alpha + mixed

    def following(t, j):
        group = []
        for _ in range(width):
            t, j = advance(t, j)
            group += [t, j]
        return tuple(group)

    start = [jnp.int32(0), jnp.int32(0)]
    for _ in range(width - 1):
        start += advance(*start[-2:])
    for lane in range(width):
        score(lane, start[2 * lane], start[2 * lane + 1])

    def step(_, now):
        later = following(*now[-2:])
        for lane in range(width):
            blend(lane, now[2 * lane], now[2 * lane + 1])
            score(lane, later[2 * lane], later[2 * lane + 1])
        return later

    end = lax.fori_loop(0, (items + width - 1) // width - 1, step, tuple(start))
    for lane in range(width):
        blend(lane, end[2 * lane], end[2 * lane + 1])

    if mode == "near":
        for b in range(count):
            for held, out in zip((m_ref, l_ref, acc_ref), outs[3 * b : 3 * b + 3]):
                out[...] = held[b * OWN : (b + 1) * OWN]
        return

    def finish(i, _):
        for u in range(4):
            t = i * 4 + u
            logs = {}
            for b, block in enumerate(blocks):
                total = jnp.sum(l_ref[b * OWN + t], axis=0, keepdims=True)
                some = total > 0.0
                safe = jnp.where(some, total, 1.0)
                share = jnp.where(some, 1.0 / safe, 0.0)
                outs[b][t, :HD] = (acc_ref[b * OWN + t] * share).astype(jnp.bfloat16)
                logs[block] = jnp.where(some, m_ref[b * OWN + t] * SCALE + jnp.log(safe), NEG)
                outs[count + b][pl.ds(t, 1)] = logs[block]
            none = [jnp.zeros((1, BLK), jnp.bfloat16)] * 3
            below = [row for b in range(RING) for row in (split(logs[b]) if b in logs else none)]
            below.append(jnp.zeros((PAD - 3 * RING, BLK), jnp.bfloat16))
            for b in range(count):
                outs[b][t, HD:] = jnp.concatenate(below, axis=0)
        return 0

    lax.fori_loop(0, OWN // 4, finish, 0)


def attend(blocks, mode, lists, queries, keys_values, states=()):
    count = len(blocks)
    slots = count * OWN + 1
    keys = {"near": NEAR, "far": OWN, "full": KEYS}[mode]
    pairs = count * keys * 4
    shapes = ((1, BLK), (8, BLK), (HD, BLK))
    if mode == "near":
        out_shape = [jax.ShapeDtypeStruct((OWN, *shape), jnp.float32) for shape in shapes] * count
    else:
        out_shape = [jax.ShapeDtypeStruct((OWN, HD + PAD, BLK), jnp.bfloat16)] * count
        out_shape += [jax.ShapeDtypeStruct((OWN, BLK), jnp.float32)] * count
    operands = (*queries, *keys_values, *states)
    return pl.pallas_call(
        functools.partial(attend_kernel, blocks, mode),
        out_shape=tuple(out_shape),
        in_specs=[SMEM] * 3 + [VMEM] * len(operands),
        out_specs=(VMEM,) * len(out_shape),
        scratch_shapes=[pltpu.SMEM((slots,), jnp.int32)] * 3
        + [
            pltpu.VMEM((count * OWN, BLK, HD), jnp.bfloat16),
            pltpu.VMEM((keys, BLK, HD), jnp.bfloat16),
            pltpu.VMEM((keys, HD, BLK), jnp.bfloat16),
        ]
        + [pltpu.VMEM((slots, *shape), jnp.float32) for shape in shapes]
        + [pltpu.VMEM((CHUNK * BLK, BLK), jnp.float32)] * WIDTHS[count]
        + [pltpu.VMEM((1, BLK), jnp.float32)] * WIDTHS[count],
        compiler_params=SPACE,
        cost_estimate=pl.CostEstimate(
            flops=pairs * 4 * BLK * BLK * HD,
            bytes_accessed=5 << 20,
            transcendentals=pairs * BLK * BLK,
        ),
        name=mode,
    )(*lists, *operands)


def combine_kernel(e0, *refs):
    outs, o_ref = refs[:-1], refs[-1]
    for t in range(OWN):
        parts = [e0[t : t + 1]]
        for block in range(1, RING):
            parts.append(joined(outs[block][t, HD:].astype(jnp.float32), block))
        top = jnp.maximum(jnp.maximum(parts[0], parts[1]), jnp.maximum(parts[2], parts[3]))
        shares = [jnp.exp(part - top) for part in parts]
        total = (shares[0] + shares[1]) + (shares[2] + shares[3])
        mixed = sum(o[t, :HD].astype(jnp.float32) * (w / total) for o, w in zip(outs, shares))
        o_ref[t] = mixed.T.astype(jnp.bfloat16)


def combine(e0, outs):
    return pl.pallas_call(
        combine_kernel,
        out_shape=jax.ShapeDtypeStruct((OWN, BLK, HD), jnp.bfloat16),
        in_specs=[VMEM] * (RING + 1),
        out_specs=VMEM,
        compiler_params=SPACE,
        name="combine",
    )(e0, *outs)


def pick_kernel(spots, e0, e1, e2, e3, out, every):
    for block, log in enumerate((e0, e1, e2, e3)):
        every[block * OWN : (block + 1) * OWN] = log[...]
    every[KEYS : KEYS + 8] = jnp.full((8, BLK), NEG, jnp.float32)
    for ctx in range(RING * RING):
        for slot in range(OWN):
            out[ctx, slot : slot + 1] = every[pl.ds(spots[ctx * OWN + slot], 1)]


def pick(spots, logs):
    return pl.pallas_call(
        pick_kernel,
        out_shape=jax.ShapeDtypeStruct((RING * RING, OWN, BLK), jnp.float32),
        in_specs=[SMEM] + [VMEM] * RING,
        out_specs=VMEM,
        scratch_shapes=[pltpu.VMEM((KEYS + 8, BLK), jnp.float32)],
        compiler_params=SPACE,
        name="pick",
    )(spots, *logs)


def merge_kernel(parts, out):
    top = jnp.max(parts[...], axis=0)
    out[...] = top + jnp.log(jnp.sum(jnp.exp(parts[...] - top[None]), axis=0))


def merge(parts):
    return pl.pallas_call(
        merge_kernel,
        out_shape=jax.ShapeDtypeStruct((OWN, BLK), jnp.float32),
        in_specs=[VMEM],
        out_specs=VMEM,
        compiler_params=SPACE,
        name="merge",
    )(parts)


def slot_spots(assign, xi, yi):
    spots = (assign % OWN // 3 - yi) % RING * OWN + assign % KEYS // OWN * 3 + assign % 3
    return jnp.where(assign // KEYS == xi, spots, KEYS)


def key_lists(kv_tiles, tile_count, xi, yi):
    rows = lax.dynamic_slice_in_dim(kv_tiles, xi * KEYS, KEYS)
    used = lax.dynamic_slice_in_dim(tile_count, xi * KEYS, KEYS)
    here = (rows % OWN // 3 == yi) & (jnp.arange(LIST, dtype=jnp.int32)[None, :] < used[:, None])
    away = (rows // KEYS - xi) % RING
    block = jnp.where(away == 2, 3, jnp.minimum(away, 2))
    place = block * OWN + rows % KEYS // OWN * 3 + rows % 3
    near, far = here & (away != 2), here & (away == 2)
    nears = jnp.sum(near.astype(jnp.int32), axis=1)
    before = (jnp.arange(LIST)[:, None] < jnp.arange(LIST)[None, :]).astype(jnp.bfloat16)
    rank_near = jnp.dot(near.astype(jnp.bfloat16), before, preferred_element_type=jnp.float32)
    rank_far = jnp.dot(far.astype(jnp.bfloat16), before, preferred_element_type=jnp.float32)
    rank = jnp.where(
        near, rank_near.astype(jnp.int32), nears[:, None] + rank_far.astype(jnp.int32)
    )
    spot = jnp.arange(KEYS + CHUNK, dtype=jnp.int32)[None, :, None]
    at = here[:, None, :] & (rank[:, None, :] == spot)
    lists = jnp.sum(jnp.where(at, place[:, None, :], 0), axis=2)
    return lists, nears, jnp.sum(here.astype(jnp.int32), axis=1)


def exchange(array):
    return lax.all_to_all(array, GROUP, split_axis=0, concat_axis=0, tiled=True)


def on_device(queries, keys, values, kv_tiles, tile_count, assign):
    xi, yi = lax.axis_index("x"), lax.axis_index("y")
    lists = key_lists(kv_tiles, tile_count, xi, yi)
    spots = slot_spots(assign, xi, yi)
    by_head = jnp.transpose(queries.reshape(96, 16, HD), (1, 0, 2))
    sent = jnp.stack([a.reshape(96, 16, HD) for a in (keys, values)])
    got = exchange(jnp.transpose(sent, (2, 0, 1, 3)))
    got, by_head, spots, *lists = lax.optimization_barrier((got, by_head, spots, *lists))
    kv0 = prepare(got)
    kv1, kv3 = shift(kv0, "x", -1), shift(kv0, "x", 1)
    q0 = exchange(by_head).reshape(OWN, BLK, HD)
    k2, v2 = shift(kv3[0], "x", 1), shift(kv1[1], "x", -1)
    q0, q1, q2, q3 = around(q0, "y")
    state = attend((0,), "near", lists, (q0,), (kv0, kv1, kv3))
    o0, e0 = attend((0,), "far", lists, (q0,), (k2, v2), state)
    q2, o0 = lax.optimization_barrier((q2, o0))
    kv = (kv0, kv1, kv3, k2, v2)
    o2, e2 = attend((2,), "full", lists, (q2,), kv)
    q1, o2 = lax.optimization_barrier((q1, o2))
    o2 = shift(o2, "y", 2)
    o1, o3, e1, e3 = attend((1, 3), "full", lists, (q1, q3), kv)
    e1, o2 = lax.optimization_barrier((e1, o2))
    parts = lax.all_to_all(
        pick(spots, (e0, e1, e2, e3)), ("x", "y"), split_axis=0, concat_axis=0, tiled=True
    )
    o0, parts = lax.optimization_barrier((o0, parts))
    blended = combine(e0, (o0, shift(o1, "y", 1), o2, shift(o3, "y", -1)))
    back = exchange(blended.reshape(16, 96, HD))
    attended = jnp.transpose(back, (1, 0, 2)).reshape(96, 16 * HD)
    turned = [(b * RING + a, a * RING + b) for a in range(RING) for b in range(RING)]
    return attended, lax.ppermute(merge(parts).reshape(1, OWN * BLK), ("zh", "y"), turned)


def solution(mesh):
    split = jax.sharding.Mesh(
        mesh.devices.reshape(RING, RING, RING, 2, 2), ("x", "zh", "y", "zl", "core")
    )
    tokens = P(("x", "zh", "y", "zl", "core"), None)
    return jax.shard_map(
        on_device,
        mesh=split,
        in_specs=(tokens, tokens, tokens, P(), P(), P()),
        out_specs=(tokens, P(("y", "zl", "core"), ("x", "zh"))),
        check_vma=False,
    )
```
